128 devices in a mesh: replica: 16 (over z_lo, y, core), shard: 8 (over z_hi, x).
Axes of the slice: x: 4, y: 4, z: 4 (z_hi: 2, z_lo: 2; z = z_hi * 2 + z_lo), core: 2. Of those that a mesh axis runs over, the one named last changes fastest.
Arguments:
- tokens: bfloat16 [32, 576, 1024], P('replica', 'shard'), may hold values from -6 to 6
- cotangent: bfloat16 [32, 576, 1024], P('replica', 'shard'), may hold values from -6 to 6
- attn_gain: bfloat16 [1024], P('shard'), may hold values from 0.099609375 to 1.8984375
- attn_shift: bfloat16 [1024], P('shard'), may hold values from -1.5 to 1.5
- qkv_weight: bfloat16 [1024, 3072], P('shard'), may hold values from -0.1875 to 0.1875
- query_bias: bfloat16 [1024], P('shard'), may hold values from -2.5 to 2.5
- value_bias: bfloat16 [1024], P('shard'), may hold values from -2.5 to 2.5
- out_weight: bfloat16 [1024, 1024], P('shard'), may hold values from -1.5 to 1.5
- out_bias: bfloat16 [1024], P('shard'), may hold values from -1.5 to 1.5
- mlp_gain: bfloat16 [1024], P('shard'), may hold values from 0.099609375 to 1.8984375
- mlp_shift: bfloat16 [1024], P('shard'), may hold values from -1.5 to 1.5
- up_weight: bfloat16 [1024, 4096], P('shard'), may hold values from -0.1875 to 0.1875
- up_bias: bfloat16 [4096], P('shard'), may hold values from -2.5 to 2.5
- down_weight: bfloat16 [4096, 1024], P('shard'), may hold values from -0.09375 to 0.09375
- down_bias: bfloat16 [1024], P('shard'), may hold values from -1.5 to 1.5
Outputs:
- block_out: bfloat16 [32, 576, 1024], P('replica', 'shard')
- input_grad: bfloat16 [32, 576, 1024], P('replica', 'shard')
- attn_gain_grad: float32 [1024], P('shard')
- attn_shift_grad: float32 [1024], P('shard')
- qkv_weight_grad: float32 [1024, 3072], P('shard')
- query_bias_grad: float32 [1024], P('shard')
- value_bias_grad: float32 [1024], P('shard')
- out_weight_grad: float32 [1024, 1024], P('shard')
- out_bias_grad: float32 [1024], P('shard')
- mlp_gain_grad: float32 [1024], P('shard')
- mlp_shift_grad: float32 [1024], P('shard')
- up_weight_grad: float32 [1024, 4096], P('shard')
- up_bias_grad: float32 [4096], P('shard')
- down_weight_grad: float32 [4096, 1024], P('shard')
- down_bias_grad: float32 [1024], P('shard')
The draws below stay inside these ranges and needn't reach their ends.
All inputs are finite; a program needn't handle non-finite values.
Results may differ from the reference program's by a relative error of at most 0.024.
Values may be sent and summed in bfloat16 or wider, within the bound.
A program may use at most 192 MiB of HBM per device.

```python
import jax
import jax.numpy as jnp
from jax import lax

D = 1024
FF = 4096
HEAD_DIM = 64
SEQ = 576
IMAGES = 32


def steps_of(key, shape, pieces, least, top_value):
    loudness, own = 1.0, jax.random.fold_in(key, 6)
    for axis_at, parts in pieces:
        steps = jnp.exp(jax.random.uniform(jax.random.fold_in(own, axis_at), (parts,), jnp.float32, least / len(pieces), top_value / len(pieces)))
        loudness = loudness * jnp.repeat(steps, shape[axis_at] // parts).reshape([-1 if axis == axis_at else 1 for axis in range(len(shape))])
    return loudness


def noise(rng, shape, scale, bound, split=(), kind=jnp.bfloat16):
    gain = steps_of(rng, shape, split, -0.22, 0.18) if split else 1.0
    result = jax.random.normal(rng, shape, jnp.float32) * scale * gain
    return jnp.minimum(jnp.maximum(result, -bound), bound).astype(kind)


def setup_inputs(seed: int = 0) -> dict:
    seeds = jax.random.split(jax.random.key(seed), 16)
    return {
        "tokens": noise(seeds[0], (IMAGES, SEQ, D), 1.0, 6.0, ((0, 16), (1, 8))),
        "cotangent": noise(seeds[1], (IMAGES, SEQ, D), 1.0, 6.0, ((0, 16), (1, 8))),
        "attn_gain": jnp.clip(1.0 + 0.18 * jax.random.normal(seeds[2], (D,), jnp.float32), 0.099609375, 1.8984375).astype(jnp.bfloat16),
        "attn_shift": noise(seeds[3], (D,), 0.3, 1.5, ((0, 8),)),
        "qkv_weight": noise(seeds[4], (D, 3 * D), D ** -0.5, 0.1875, ((0, 8),)),
        "query_bias": noise(seeds[5], (D,), 0.5, 2.5, ((0, 8),)),
        "value_bias": noise(seeds[6], (D,), 0.5, 2.5, ((0, 8),)),
        "out_weight": noise(seeds[7], (D, D), (D // 64) ** -0.5, 1.5, ((0, 8),)),
        "out_bias": noise(seeds[8], (D,), 0.3, 1.5, ((0, 8),)),
        "mlp_gain": jnp.clip(1.0 + 0.18 * jax.random.normal(seeds[9], (D,), jnp.float32), 0.099609375, 1.8984375).astype(jnp.bfloat16),
        "mlp_shift": noise(seeds[10], (D,), 0.3, 1.5, ((0, 8),)),
        "up_weight": noise(seeds[11], (D, FF), D ** -0.5, 0.1875, ((0, 8),)),
        "up_bias": noise(seeds[12], (FF,), 0.5, 2.5, ((0, 8),)),
        "down_weight": noise(seeds[13], (FF, D), FF ** -0.5, 0.09375, ((0, 8),)),
        "down_bias": noise(seeds[14], (D,), 0.3, 1.5, ((0, 8),)),
    }


@jax.custom_vjp
def low(v):
    return lax.optimization_barrier(v.astype(jnp.bfloat16)).astype(jnp.float32)

@jax.custom_vjp
def low_back(v):
    return v

def low_keep(v):
    return (low(v), None)

def low_pass(kept, grad):
    return (grad,)

def back_keep(v):
    return (v, None)

def back_low(kept, grad):
    return (low(grad),)
low.defvjp(low_keep, low_pass)
low_back.defvjp(back_keep, back_low)
highest = lax.Precision.HIGHEST
epsilon = 1e-06

def rounded_both(value_in):
    return low_back(low(value_in))

def layer_norm(inputs, norm_gain, norm_shift):
    row_mean = lax.optimization_barrier(jnp.mean(inputs, -1, keepdims=True))
    centred = inputs - row_mean
    variance = lax.optimization_barrier(jnp.mean(centred * centred, -1, keepdims=True))
    return centred * lax.rsqrt(variance + epsilon) * norm_gain + norm_shift

def gelu_tanh(values):
    return jax.nn.gelu(values, approximate=True)

def attend_image(triple):
    query_rows, key_rows, value_rows = triple
    head_count = D // HEAD_DIM
    query_heads = query_rows.reshape(SEQ, head_count, HEAD_DIM)
    key_heads = key_rows.reshape(SEQ, head_count, HEAD_DIM)
    value_heads = value_rows.reshape(SEQ, head_count, HEAD_DIM)
    scores = jnp.einsum('qhe,khe->hqk', query_heads, key_heads, precision=highest) * HEAD_DIM ** (-0.5)
    scores = low_back(scores)
    row_max = lax.optimization_barrier(jnp.max(scores, -1, keepdims=True))
    exponentials = jnp.exp(scores - row_max)
    weights = exponentials / lax.optimization_barrier(jnp.sum(exponentials, -1, keepdims=True))
    mixed = jnp.einsum('hqk,khe->qhe', low(weights), value_heads, precision=highest)
    return mixed.reshape(SEQ, D)

def layer(inputs, attn_gain, attn_shift, qkv_weight, query_bias, value_bias, out_weight, out_bias, mlp_gain, mlp_shift, up_weight, up_bias, down_weight, down_bias):
    first = low(layer_norm(inputs, attn_gain, attn_shift))
    projected = jnp.einsum('bsd,de->bse', first, qkv_weight, precision=highest)
    query_rows = rounded_both(projected[..., :D] + query_bias)
    key_rows = rounded_both(projected[..., D:2 * D])
    value_rows = rounded_both(projected[..., 2 * D:] + value_bias)
    attended = lax.map(jax.checkpoint(attend_image), (query_rows, key_rows, value_rows))
    attended = rounded_both(attended)
    branch = low_back(jnp.einsum('bsd,de->bse', attended, out_weight, precision=highest) + out_bias)
    resid = inputs + branch
    second = low(layer_norm(resid, mlp_gain, mlp_shift))
    upper = low_back(jnp.einsum('bsd,df->bsf', second, up_weight, precision=highest) + up_bias)
    active = low(gelu_tanh(upper))
    outcome = low_back(jnp.einsum('bsf,fd->bsd', active, down_weight, precision=highest) + down_bias)
    return resid + outcome

def reference(tokens, cotangent, attn_gain, attn_shift, qkv_weight, query_bias, value_bias, out_weight, out_bias, mlp_gain, mlp_shift, up_weight, up_bias, down_weight, down_bias):
    params = (attn_gain, attn_shift, qkv_weight, query_bias, value_bias, out_weight, out_bias, mlp_gain, mlp_shift, up_weight, up_bias, down_weight, down_bias)
    params = tuple((item.astype(jnp.float32) for item in params))
    block_out, pull_back = jax.vjp(layer, tokens.astype(jnp.float32), *params)
    grads = pull_back(cotangent.astype(jnp.float32))
    return (block_out.astype(jnp.bfloat16), grads[0].astype(jnp.bfloat16), grads[1], grads[2], grads[3], grads[4], grads[5], grads[6], grads[7], grads[8], grads[9], grads[10], grads[11], grads[12], grads[13])
```

```python
import jax
import jax.numpy as jnp
from jax import lax
from jax.experimental import pallas as pl
from jax.experimental.pallas import tpu as pltpu
from jax.sharding import PartitionSpec as P

HEAD_DIM = 64
EPS = 1e-06
F32 = jnp.float32
BF16 = jnp.bfloat16
SCALE = HEAD_DIM ** (-0.5)


def dot(a, b):
    return lax.dot_general(a, b, (((1,), (0,)), ((), ())), preferred_element_type=F32)


def dot_last(a, b):
    return lax.dot_general(a, b, (((1,), (1,)), ((), ())), preferred_element_type=F32)


def dot_first(a, b):
    return lax.dot_general(a, b, (((0,), (0,)), ((), ())), preferred_element_type=F32)


def norm_unit(v):
    mean = jnp.mean(v, -1, keepdims=True)
    centred = v - mean
    inverse = lax.rsqrt(jnp.mean(centred * centred, -1, keepdims=True) + EPS)
    return centred * inverse, inverse


def norm_back(grad, unit, inverse, gain):
    gn = grad * gain
    inner = jnp.mean(gn * unit, -1, keepdims=True)
    return inverse * (gn - jnp.mean(gn, -1, keepdims=True) - unit * inner)


def head_masks(shape):
    low = lax.broadcasted_iota(jnp.int32, shape, 1) < HEAD_DIM
    return (low, jnp.logical_not(low))


def attend_kernel(qkv_ref, out_ref, lse_ref):
    q, k, v = (qkv_ref[0, :, i * 128 : (i + 1) * 128] for i in range(3))
    zero = jnp.zeros_like(q)
    total = jnp.zeros(q.shape, F32)
    for h, mask in enumerate(head_masks(q.shape)):
        s = dot_last(jnp.where(mask, q, zero), k) * SCALE
        top = jnp.max(s, -1, keepdims=True)
        e = jnp.exp(s - top)
        row = jnp.sum(e, -1, keepdims=True)
        p = (e * (1.0 / row)).astype(BF16)
        total += dot(p, jnp.where(mask, v, zero))
        lse_ref[0, :, h : h + 1] = top + jnp.log(row)
    out_ref[0] = total.astype(BF16)


def attend(qkv):
    images, seq, width = qkv.shape
    return pl.pallas_call(
        attend_kernel,
        grid=(images,),
        in_specs=[pl.BlockSpec((1, seq, width), lambda i: (i, 0, 0))],
        out_specs=[
            pl.BlockSpec((1, seq, 128), lambda i: (i, 0, 0)),
            pl.BlockSpec((1, seq, 2), lambda i: (i, 0, 0)),
        ],
        out_shape=[
            jax.ShapeDtypeStruct((images, seq, 128), BF16),
            jax.ShapeDtypeStruct((images, seq, 2), F32),
        ],
        name="attend",
        compiler_params=pltpu.CompilerParams(vmem_limit_bytes=40 << 20),
    )(qkv)


def attend_back_kernel(qkv_ref, lse_ref, grad_ref, out_ref):
    q, k, v = (qkv_ref[0, :, i * 128 : (i + 1) * 128] for i in range(3))
    grad = grad_ref[0]
    zero = jnp.zeros_like(q)
    dq = jnp.zeros(q.shape, F32)
    dk, dv = dq, dq
    for h, mask in enumerate(head_masks(q.shape)):
        qh, kh, gh = (jnp.where(mask, a, zero) for a in (q, k, grad))
        p = jnp.exp(dot_last(qh, k) * SCALE - lse_ref[0, :, h : h + 1])
        dp = dot_last(gh, v)
        inner = jnp.sum(p * dp, -1, keepdims=True)
        ds = (p * (dp - inner)).astype(BF16)
        dq += dot(ds, kh)
        dk += dot_first(ds, qh)
        dv += dot_first(p.astype(BF16), gh)
    out_ref[0, :, 0:128] = (dq * SCALE).astype(BF16)
    out_ref[0, :, 128:256] = (dk * SCALE).astype(BF16)
    out_ref[0, :, 256:384] = dv.astype(BF16)


def attend_back(qkv, lse, grad):
    images, seq, width = qkv.shape
    return pl.pallas_call(
        attend_back_kernel,
        grid=(images,),
        in_specs=[
            pl.BlockSpec((1, seq, width), lambda i: (i, 0, 0)),
            pl.BlockSpec((1, seq, 2), lambda i: (i, 0, 0)),
            pl.BlockSpec((1, seq, 128), lambda i: (i, 0, 0)),
        ],
        out_specs=pl.BlockSpec((1, seq, width), lambda i: (i, 0, 0)),
        out_shape=jax.ShapeDtypeStruct((images, seq, width), BF16),
        name="attend_back",
        compiler_params=pltpu.CompilerParams(vmem_limit_bytes=40 << 20),
    )(qkv, lse, grad)


def gather(a):
    return lax.all_gather(a, "shard", axis=0, tiled=True)


def scatter(a):
    return lax.psum_scatter(a.astype(BF16), "shard", scatter_dimension=0, tiled=True).astype(F32)


def turn(a):
    return lax.all_to_all(a, "shard", 0, 0, tiled=True)


def by_image(a):
    return a.reshape(8, 2, 72, a.shape[-1]).swapaxes(0, 1).reshape(2, 576, a.shape[-1])


def by_device(a):
    return a.reshape(2, 8, 72, a.shape[-1]).swapaxes(0, 1).reshape(1152, a.shape[-1])


def body(
    tokens,
    cotangent,
    attn_gain,
    attn_shift,
    qkv_weight,
    query_bias,
    value_bias,
    out_weight,
    out_bias,
    mlp_gain,
    mlp_shift,
    up_weight,
    up_bias,
    down_weight,
    down_bias,
):
    D = 1024
    shard = lax.axis_index("shard")
    columns = jnp.concatenate(
        [qkv_weight.reshape(128, 3, 8, 128), up_weight.reshape(128, 8, 4, 128).swapaxes(1, 2)], 1
    )
    columns = columns.transpose(2, 0, 1, 3).reshape(8, 128, 896)
    vectors = jnp.stack([attn_gain, attn_shift, mlp_gain, mlp_shift, out_bias, down_bias])
    vectors = jnp.broadcast_to(jnp.pad(vectors, ((0, 10), (0, 768))), (8, 16, 896))
    turned = turn(jnp.concatenate([columns, vectors], 1))
    weights = turned[:, :128].reshape(D, 896)
    qkv_columns, up_columns = weights[:, :384], weights[:, 384:]
    vectors = turned[:, 128:134, :128].swapaxes(0, 1).reshape(6, D).astype(F32)
    gain1, shift1, gain2, shift2, bias_out, bias_down = vectors

    x = tokens.reshape(144, D).astype(F32)
    unit1, inverse1 = norm_unit(x)
    first = gather((unit1 * gain1 + shift1).astype(BF16))
    grad_all = gather(cotangent.reshape(144, D))
    zeros = jnp.zeros((128,), F32)
    qkv_bias = jnp.concatenate([query_bias.astype(F32), zeros, value_bias.astype(F32)])
    qkv = by_image((dot(first, qkv_columns) + qkv_bias).astype(BF16))
    attended, lse = attend(qkv)
    attended = by_device(attended)
    resid = x + (scatter(dot(attended, out_weight)) + bias_out)
    unit2, inverse2 = norm_unit(resid)
    second = gather((unit2 * gain2 + shift2).astype(BF16))
    upper = dot(second, up_columns) + up_bias.astype(F32)
    active, gelu_pull = jax.vjp(lambda u: jax.nn.gelu(u, approximate=True), upper)
    active = active.astype(BF16)
    outcome = scatter(dot(active, down_weight)) + bias_down
    block_out = (resid + outcome).astype(BF16).reshape(2, 72, D)

    down_grad = dot_first(active, grad_all)
    grad_upper32 = gelu_pull(dot_last(grad_all, down_weight))[0]
    grad_upper = grad_upper32.astype(BF16)
    up_grad = dot_first(second, grad_upper)
    up_bias_grad = jnp.sum(grad_upper.astype(F32), 0)
    grad_second = scatter(dot_last(grad_upper, up_columns))
    grad_resid = cotangent.reshape(144, D).astype(F32) + norm_back(
        grad_second, unit2, inverse2, gain2
    )
    gain2_grad = jnp.sum(grad_second * unit2, 0)
    shift2_grad = jnp.sum(grad_second, 0)
    branch_all = gather(grad_resid.astype(BF16))
    out_grad = dot_first(attended, branch_all)
    grad_attended = dot_last(branch_all, out_weight).astype(BF16)
    grad_qkv = by_device(attend_back(qkv, lse, by_image(grad_attended)))
    qkv_grad = dot_first(first, grad_qkv)
    qkv_bias_grad = jnp.sum(grad_qkv.astype(F32), 0)
    grad_first = scatter(dot_last(grad_qkv, qkv_columns))
    input_grad = (grad_resid + norm_back(grad_first, unit1, inverse1, gain1)).astype(BF16)
    input_grad = input_grad.reshape(2, 72, D)
    gain1_grad = jnp.sum(grad_first * unit1, 0)
    shift1_grad = jnp.sum(grad_first, 0)

    own = lambda a: lax.dynamic_slice_in_dim(a, shard * 128, 128, axis=1)
    out_bias_grad = jnp.sum(own(branch_all).astype(F32), 0)
    down_bias_grad = jnp.sum(own(grad_all).astype(F32), 0)

    up_turned = turn(up_grad.astype(BF16).reshape(8, 128, 512))
    early = jnp.concatenate([down_grad.astype(BF16), up_turned.reshape(512, D)], 0)
    early = lax.psum(early, "replica").astype(F32)
    four = jnp.stack([gain1_grad, shift1_grad, gain2_grad, shift2_grad]).reshape(4, 8, 128)
    four = jnp.pad(four.swapaxes(0, 1), ((0, 0), (0, 12), (0, 256)))
    late = turn(jnp.concatenate([qkv_grad.reshape(8, 128, 384), four], 1).astype(BF16))
    four = jnp.sum(late[:, 128:132, :128].astype(F32), 0).reshape(512)
    small = jnp.concatenate(
        [four, qkv_bias_grad[:128], qkv_bias_grad[256:], out_bias_grad, down_bias_grad]
    )
    small = jnp.pad(jnp.stack([small, jnp.pad(up_bias_grad, (0, 512))]), ((0, 14), (0, 0)))
    late = jnp.concatenate(
        [out_grad.astype(BF16), late[:, :128].reshape(384, D), small.astype(BF16)], 0
    )
    late = lax.psum(late, "replica").astype(F32)
    out_weight_grad = late[:128]
    qkv_weight_grad = late[128:512].reshape(8, 128, 3, 128)
    qkv_weight_grad = qkv_weight_grad.transpose(1, 2, 0, 3).reshape(128, 3 * D)
    small = late[512].reshape(8, 128)
    down_weight_grad = early[:512]
    up_weight_grad = early[512:].reshape(8, 128, 512).swapaxes(0, 1).reshape(128, 4096)
    return (
        block_out,
        input_grad,
        small[0],
        small[1],
        qkv_weight_grad,
        small[4],
        small[5],
        out_weight_grad,
        small[6],
        small[2],
        small[3],
        up_weight_grad,
        late[513, :512],
        down_weight_grad,
        small[7],
    )


def solution(mesh):
    row, cube, flat = P("shard"), P("replica", "shard", None), P("shard", None)
    return jax.shard_map(
        body,
        mesh=mesh,
        in_specs=(cube, cube, row, row, flat, row, row, flat, row, row, row, flat, row, flat, row),
        out_specs=(cube, cube, row, row, flat, row, row, flat, row, row, row, flat, row, flat, row),
        check_vma=False,
    )
```

```python
import jax
import jax.numpy as jnp
from jax import lax
from jax.experimental import pallas as pl
from jax.experimental.pallas import tpu as pltpu
from jax.sharding import PartitionSpec as P

HEAD_DIM = 64
EPS = 1e-06
F32 = jnp.float32
BF16 = jnp.bfloat16
SCALE = HEAD_DIM ** (-0.5)
MESH = pl.DeviceIdType.MESH
D = 1024
ROWS = 144
HALF = 512
GELU = 0.7978845608028654


def dot(a, b):
    return lax.dot_general(a, b, (((1,), (0,)), ((), ())), preferred_element_type=F32)


def dot_last(a, b):
    return lax.dot_general(a, b, (((1,), (1,)), ((), ())), preferred_element_type=F32)


def dot_first(a, b):
    return lax.dot_general(a, b, (((0,), (0,)), ((), ())), preferred_element_type=F32)


def norm_unit(v):
    mean = jnp.mean(v, -1, keepdims=True)
    centred = v - mean
    inverse = lax.rsqrt(jnp.mean(centred * centred, -1, keepdims=True) + EPS)
    return centred * inverse, inverse


def norm_back(grad, unit, inverse, gain):
    gn = grad * gain
    inner = jnp.mean(gn * unit, -1, keepdims=True)
    return inverse * (gn - jnp.mean(gn, -1, keepdims=True) - unit * inner)


def head_masks(shape):
    low = lax.broadcasted_iota(jnp.int32, shape, 1) < HEAD_DIM
    return (low, jnp.logical_not(low))


def add(*terms):
    total = terms[0].astype(F32)
    for term in terms[1:]:
        total = total + term.astype(F32)
    return total


class Net:
    def __init__(self, send, recv):
        self.send, self.recv, self.count, self.open = send, recv, 0, []
        self.s = lax.axis_index("shard")
        self.h, self.x = self.s // 4, lax.rem(self.s, 4)
        r = lax.axis_index("replica")
        self.core, self.y = lax.rem(r, 2), lax.rem(r // 2, 4)
        zlow = r // 8
        base = r - self.y * 2
        self.right = {"shard": self.at(self.h, self.x + 1)}
        self.left = {"shard": self.at(self.h, self.x + 3)}
        self.across = {"shard": self.at(1 - self.h, self.x)}
        self.twin = {"replica": r + 1 - 2 * self.core}
        self.up = {"replica": base + lax.rem(self.y + 1, 4) * 2}
        self.down = {"replica": base + lax.rem(self.y + 3, 4) * 2}
        self.beside = {"replica": r + 8 - 16 * zlow}
        self.peers = [{"shard": lax.rem(self.s + k, 8)} for k in range(1, 8)]

    def at(self, h, x):
        return h * 4 + lax.rem(x, 4)

    def copy(self, src, dst, to):
        i = self.count
        self.count += 1
        made = pltpu.make_async_remote_copy(
            src_ref=src,
            dst_ref=dst,
            send_sem=self.send.at[i],
            recv_sem=self.recv.at[i],
            device_id=to,
            device_id_type=MESH,
        )
        made.start()
        self.open.append(made)
        return made

    def drain(self):
        for made in self.open:
            made.wait_send()
        self.open = []

    def barrier(self, others):
        semaphore = pltpu.get_barrier_semaphore()
        for other in others:
            pl.semaphore_signal(semaphore, inc=1, device_id=other, device_id_type=MESH)
        pl.semaphore_wait(semaphore, len(others))


class Gather:
    def __init__(self, net, whole):
        self.net, self.whole = net, whole
        own = whole.at[net.s]
        self.z = net.copy(own, own, net.across)
        self.a = net.copy(own, own, net.right)
        self.b = net.copy(own, own, net.left)

    def piece(self, block, first, to):
        part = self.whole.at[block, :, pl.ds(0 if first else HALF, HALF)]
        return self.net.copy(part, part, to)

    def relay_one(self):
        net = self.net
        self.z.wait_recv()
        part = self.whole.at[net.at(1 - net.h, net.x)]
        self.za = net.copy(part, part, net.right)
        self.zb = net.copy(part, part, net.left)
        self.a.wait_recv()
        self.c = self.piece(net.at(net.h, net.x + 3), True, net.right)
        self.b.wait_recv()
        self.d = self.piece(net.at(net.h, net.x + 1), False, net.left)

    def relay_two(self):
        net = self.net
        self.za.wait_recv()
        self.e = self.piece(net.at(1 - net.h, net.x + 3), True, net.right)
        self.zb.wait_recv()
        self.f = self.piece(net.at(1 - net.h, net.x + 1), False, net.left)

    def finish(self):
        for made in (self.c, self.d, self.e, self.f):
            made.wait_recv()


class Scatter:
    def __init__(self, net, part, far, near, passed, kept, came):
        self.net, self.part = net, part
        self.far, self.near, self.passed, self.kept, self.came = far, near, passed, kept, came
        self.rows = (1 - net.h, net.h)
        halves = (pl.ds(0, HALF), pl.ds(HALF, HALF))
        self.first, self.second = halves
        self.fars, self.nears, self.passes = [], [], [None, None]
        for j, h in enumerate(self.rows):
            block = net.at(h, net.x + 2)
            self.fars.append(
                (
                    net.copy(part.at[block, :, self.first], far.at[0, j], net.right),
                    net.copy(part.at[block, :, self.second], far.at[1, j], net.left),
                )
            )
        for j, h in enumerate(self.rows):
            r, l = net.at(h, net.x + 1), net.at(h, net.x + 3)
            self.nears.append(
                (
                    net.copy(part.at[r, :, self.second], near.at[0, j], net.right),
                    net.copy(part.at[l, :, self.first], near.at[1, j], net.left),
                )
            )

    def relay(self, j):
        net, part, far, passed = self.net, self.part, self.far, self.passed
        h = self.rows[j]
        made = []
        steps = ((0, net.at(h, net.x + 1), self.first, net.right),)
        steps += ((1, net.at(h, net.x + 3), self.second, net.left),)
        for k, block, half, to in steps:
            self.fars[j][k].wait_recv()
            far[k, j] = add(far[k, j], part[block, :, half]).astype(BF16)
            made.append(net.copy(far.at[k, j], passed.at[k, j], to))
        self.passes[j] = made

    def halves(self, j):
        for made in (*self.nears[j], *self.passes[j]):
            made.wait_recv()
        own = self.net.at(self.rows[j], self.net.x)
        part, near, passed = self.part, self.near, self.passed
        return (
            add(part[own, :, self.first], passed[0, j], near[1, j]),
            add(part[own, :, self.second], passed[1, j], near[0, j]),
        )

    def over(self):
        one, two = self.halves(0)
        self.kept[:, 0:HALF] = one.astype(BF16)
        self.kept[:, HALF:D] = two.astype(BF16)
        self.z = self.net.copy(self.kept, self.came, self.net.across)

    def finish(self):
        one, two = self.halves(1)
        self.z.wait_recv()
        return jnp.concatenate(
            [add(one, self.came[:, 0:HALF]), add(two, self.came[:, HALF:D])], axis=1
        )


def layer_kernel(
    tokens,
    cotangent,
    vectors,
    qkv_weight,
    up_weight,
    out_weight,
    down_weight,
    qkv_bias,
    up_bias,
    block_out,
    input_grad,
    rows_grad,
    columns_grad,
    small_grad,
    all_vectors,
    columns,
    first,
    cot,
    second,
    branch,
    mixed,
    qkv_low,
    heads,
    lse,
    attended,
    active,
    grad_upper,
    grad_qkv,
    resid_ref,
    grad_resid_ref,
    small,
    fours,
    fours_in,
    parts,
    far,
    near,
    passed,
    kept,
    came,
    send,
    recv,
):
    net = Net(send, recv)
    s, core = net.s, net.core
    net.barrier([*net.peers, net.twin])
    source = [lax.rem(s + 8 - k, 8) for k in range(1, 8)]
    mine = pl.ds(pl.multiple_of(core * 64, 64), 64)

    def scatter(i):
        return Scatter(
            net, parts.at[i], far.at[i], near.at[i], passed.at[i], kept.at[i], came.at[i]
        )

    vec = [net.copy(vectors, all_vectors.at[s], to) for to in net.peers]
    all_vectors[s] = vectors[...]
    qkv_in, up_in = [], []
    for k, to in enumerate(net.peers):
        t = to["shard"]
        qkv_in.append(
            [
                net.copy(
                    qkv_weight.at[mine, pl.ds(pl.multiple_of(i * D + t * 128, 128), 128)],
                    columns.at[s, mine, pl.ds(i * 128, 128)],
                    to,
                )
                for i in range(3)
            ]
        )
    for i in range(3):
        columns[s, :, i * 128 : (i + 1) * 128] = qkv_weight[
            :, pl.ds(pl.multiple_of(i * D + s * 128, 128), 128)
        ]
    columns[s, :, 384:896] = up_weight[:, pl.ds(pl.multiple_of(s * 512, 512), 512)]
    cot[s] = cotangent[...]
    x = tokens[...].astype(F32)
    unit1, inverse1 = norm_unit(x)
    for made in vec:
        made.wait_recv()
    table = [all_vectors[j].astype(F32) for j in range(8)]
    gain1, shift1, gain2, shift2, bias_out, bias_down = (
        jnp.concatenate([t[i : i + 1] for t in table], axis=1) for i in range(6)
    )
    first[s] = (unit1 * gain1 + shift1).astype(BF16)
    ag = Gather(net, first)
    qkv_pass = []
    for k in range(7):
        for made in qkv_in[k]:
            made.wait_recv()
        block = columns.at[source[k], mine, pl.ds(0, 384)]
        qkv_pass.append(net.copy(block, block, net.twin))
    ag.relay_one()
    ag.relay_two()
    for k, to in enumerate(net.peers):
        up_in.append(
            net.copy(
                up_weight.at[mine, pl.ds(pl.multiple_of(to["shard"] * 512, 512), 512)],
                columns.at[s, mine, pl.ds(384, 512)],
                to,
            )
        )
    ag.finish()
    for made in qkv_pass:
        made.wait_recv()
    ag_cot = Gather(net, cot)

    def project(b, carry):
        value = dot(first[b], columns[:, :, 0:384].reshape(D, 384)) + qkv_bias[...]
        at = pl.multiple_of(b * 72, 8)
        mixed[0, pl.ds(at, 72), :] = value[0:72]
        mixed[1, pl.ds(at, 72), :] = value[72:144]
        return carry

    lax.fori_loop(0, 8, project, 0)
    qkv_low[...] = mixed[...].astype(BF16)
    ag_cot.relay_one()

    def attend(image, carry):
        q, k, v = (qkv_low[image, :, i * 128 : (i + 1) * 128] for i in range(3))
        zero = jnp.zeros_like(q)
        total = jnp.zeros(q.shape, F32)
        for h, mask in enumerate(head_masks(q.shape)):
            score = dot_last(jnp.where(mask, q, zero), k) * SCALE
            top = jnp.max(score, -1, keepdims=True)
            e = jnp.exp(score - top)
            row = jnp.sum(e, -1, keepdims=True)
            p = (e * (1.0 / row)).astype(BF16)
            total += dot(p, jnp.where(mask, v, zero))
            lse[image, :, h : h + 1] = top + jnp.log(row)
        heads[image] = total
        return carry

    lax.fori_loop(0, 2, attend, 0)
    ag_cot.relay_two()
    up_pass = []
    for k in range(7):
        up_in[k].wait_recv()
        block = columns.at[source[k], mine, pl.ds(384, 512)]
        up_pass.append(net.copy(block, block, net.twin))

    def by_device(ref, b):
        at = pl.multiple_of(b * 72, 8)
        both = [ref[i, pl.ds(at, 72), :] for i in range(2)]
        return jnp.concatenate(both, axis=0).astype(BF16)

    def outward(b, carry):
        value = by_device(heads, b)
        attended[b] = value
        parts[0, b] = dot(value, out_weight[...]).astype(BF16)
        return carry

    lax.fori_loop(0, 8, outward, 0)
    rs = scatter(0)
    rs.relay(0)
    rs.relay(1)
    rs.over()
    resid = tokens[...].astype(F32) + (rs.finish() + bias_out)
    resid_ref[...] = resid
    unit2, inverse2 = norm_unit(resid)
    second[s] = (unit2 * gain2 + shift2).astype(BF16)
    ag = Gather(net, second)
    ag.relay_one()
    ag.relay_two()
    ag_cot.finish()
    for made in up_pass:
        made.wait_recv()
    ag.finish()

    def feed(b, total):
        up = columns[:, :, 384:896].reshape(D, 512)
        u = dot(second[b], up) + up_bias[...]
        square = u * u
        t = jnp.tanh(GELU * (u + 0.044715 * u * square))
        act = (0.5 * u * (1.0 + t)).astype(BF16)
        slope = 0.5 * (1.0 + t) + (0.5 * GELU) * u * (1.0 - t * t) * (
            1.0 + 0.134145 * square
        )
        active[b] = act
        gu = (dot_last(cot[b], down_weight[...]) * slope).astype(BF16)
        grad_upper[b] = gu
        parts[1, b] = dot_last(gu, up).astype(BF16)
        parts[2, b] = dot(act, down_weight[...]).astype(BF16)
        return total + jnp.sum(gu.astype(F32), 0, keepdims=True)

    up_bias_grad = lax.fori_loop(0, 8, feed, jnp.zeros((1, 512), F32))
    rs = scatter(1)
    own = pl.ds(pl.multiple_of(s * 128, 128), 128)
    small[...] = jnp.zeros_like(small)
    for i in range(4):
        small[8 + i : 9 + i, 0:128] = up_bias_grad[:, i * 128 : (i + 1) * 128]
    small[7:8, 0:128] = jnp.sum(cot[:, :, own].astype(F32).reshape(1152, 128), 0, keepdims=True)

    def down_tile(i):
        at = pl.ds(i * 256, 256)
        value = dot_first(
            active[...].reshape(1152, 512), cot[:, :, at].reshape(1152, 256)
        ).astype(BF16)
        for q in range(8):
            rows_grad[q, 0:64, at] = value[q * 64 : (q + 1) * 64]

    down_tile(0)
    rs.relay(0)
    down_tile(1)
    rs.relay(1)
    down_tile(2)
    rs.over()
    down_tile(3)
    grad_second = rs.finish()
    unit2, inverse2 = norm_unit(resid_ref[...])
    grad_resid = cotangent[...].astype(F32) + norm_back(grad_second, unit2, inverse2, gain2)
    grad_resid_ref[...] = grad_resid
    branch[s] = grad_resid.astype(BF16)
    ag = Gather(net, branch)
    gain2_grad = jnp.sum(grad_second * unit2, 0, keepdims=True)
    shift2_grad = jnp.sum(grad_second, 0, keepdims=True)

    def up_tile(i):
        value = dot_first(
            second[:, :, i * 256 : (i + 1) * 256].reshape(1152, 256),
            grad_upper[...].reshape(1152, 512),
        ).astype(BF16)
        for j in range(2):
            for q in range(8):
                columns_grad[q, (2 * i + j) * 16 : (2 * i + j + 1) * 16, 384:896] = value[
                    j * 128 + q * 16 : j * 128 + (q + 1) * 16
                ]

    up_tile(0)
    ag.relay_one()
    up_tile(1)
    ag.relay_two()
    rs_out = scatter(2)
    up_tile(2)
    up_tile(3)
    ag.finish()

    def back_heads(b, carry):
        value = dot_last(branch[b], out_weight[...])
        at = pl.multiple_of(b * 72, 8)
        heads[0, pl.ds(at, 72), :] = value[0:72]
        heads[1, pl.ds(at, 72), :] = value[72:144]
        return carry

    lax.fori_loop(0, 8, back_heads, 0)
    rs_out.relay(0)

    def attend_back(image, carry):
        q, k, v = (qkv_low[image, :, i * 128 : (i + 1) * 128] for i in range(3))
        grad = heads[image].astype(BF16)
        zero = jnp.zeros_like(q)
        dq = jnp.zeros(q.shape, F32)
        dk, dv = dq, dq
        for h, mask in enumerate(head_masks(q.shape)):
            qh, kh, gh = (jnp.where(mask, a, zero) for a in (q, k, grad))
            p = jnp.exp(dot_last(qh, k) * SCALE - lse[image, :, h : h + 1])
            dp = dot_last(gh, v)
            inner = jnp.sum(p * dp, -1, keepdims=True)
            ds = (p * (dp - inner)).astype(BF16)
            dq += dot(ds, kh)
            dk += dot_first(ds, qh)
            dv += dot_first(p.astype(BF16), gh)
        mixed[image, :, 0:128] = dq * SCALE
        mixed[image, :, 128:256] = dk * SCALE
        mixed[image, :, 256:384] = dv
        return carry

    lax.fori_loop(0, 2, attend_back, 0)
    rs_out.relay(1)

    def back_first(b, total):
        value = by_device(mixed, b)
        grad_qkv[b] = value
        parts[3, b] = dot_last(value, columns[:, :, 0:384].reshape(D, 384)).astype(BF16)
        return total + jnp.sum(value.astype(F32), 0, keepdims=True)

    qkv_bias_grad = lax.fori_loop(0, 8, back_first, jnp.zeros((1, 384), F32))
    rs = scatter(3)
    rs_out.over()
    small[4:5, 0:128] = qkv_bias_grad[:, 0:128]
    small[5:6, 0:128] = qkv_bias_grad[:, 256:384]
    small[6:7, 0:128] = jnp.sum(branch[:, :, own].astype(F32).reshape(1152, 128), 0, keepdims=True)

    def qkv_tile(i):
        value = dot_first(
            first[:, :, i * 256 : (i + 1) * 256].reshape(1152, 256),
            grad_qkv[...].reshape(1152, 384),
        ).astype(BF16)
        for j in range(2):
            for q in range(8):
                columns_grad[q, (2 * i + j) * 16 : (2 * i + j + 1) * 16, 0:384] = value[
                    j * 128 + q * 16 : j * 128 + (q + 1) * 16
                ]

    qkv_tile(0)
    rs.relay(0)
    qkv_tile(1)
    rs.relay(1)
    qkv_tile(2)
    qkv_tile(3)
    rs.over()
    value = dot_first(attended[...].reshape(1152, 128), branch[...].reshape(1152, D)).astype(BF16)
    for q in range(8):
        rows_grad[q, 64:80, :] = value[q * 16 : (q + 1) * 16]
    block_out[...] = (resid_ref[...] + (rs_out.finish() + bias_down)).astype(BF16)
    grad_first = rs.finish()
    unit1, inverse1 = norm_unit(tokens[...].astype(F32))
    input_grad[...] = (
        grad_resid_ref[...] + norm_back(grad_first, unit1, inverse1, gain1)
    ).astype(BF16)
    gain1_grad = jnp.sum(grad_first * unit1, 0, keepdims=True)
    shift1_grad = jnp.sum(grad_first, 0, keepdims=True)
    four = jnp.concatenate(
        [gain1_grad, shift1_grad, gain2_grad, shift2_grad, jnp.zeros((12, D), F32)], axis=0
    ).astype(BF16)
    for t in range(8):
        fours[t] = four[:, t * 128 : (t + 1) * 128]
    moved = [net.copy(fours.at[to["shard"]], fours_in.at[s], to) for to in net.peers]
    fours_in[s] = fours[s]
    for made in moved:
        made.wait_recv()
    total = jnp.sum(fours_in[...].astype(F32), 0)
    small[0:4, 0:128] = total[0:4]
    small_grad[...] = jnp.zeros_like(small_grad)
    small_grad[0] = small[...].astype(BF16)
    net.drain()


def layer(*arguments):
    vmem = lambda *shape: pltpu.VMEM(shape, BF16)
    wide = lambda *shape: pltpu.VMEM(shape, F32)
    space = pl.BlockSpec(memory_space=pltpu.VMEM)
    shape = lambda *sizes: jax.ShapeDtypeStruct(sizes, BF16)
    return pl.pallas_call(
        layer_kernel,
        out_shape=[
            shape(ROWS, D),
            shape(ROWS, D),
            shape(8, 80, D),
            shape(8, 128, 896),
            shape(8, 16, 256),
        ],
        in_specs=[space] * 9,
        out_specs=[space] * 5,
        scratch_shapes=[
            vmem(8, 16, 128),
            vmem(8, 128, 896),
            vmem(8, ROWS, D),
            vmem(8, ROWS, D),
            vmem(8, ROWS, D),
            vmem(8, ROWS, D),
            wide(2, 576, 384),
            vmem(2, 576, 384),
            wide(2, 576, 128),
            wide(2, 576, 128),
            vmem(8, ROWS, 128),
            vmem(8, ROWS, 512),
            vmem(8, ROWS, 512),
            vmem(8, ROWS, 384),
            wide(ROWS, D),
            wide(ROWS, D),
            wide(16, 256),
            vmem(8, 16, 128),
            vmem(8, 16, 128),
            vmem(4, 8, ROWS, D),
            vmem(4, 2, 2, ROWS, HALF),
            vmem(4, 2, 2, ROWS, HALF),
            vmem(4, 2, 2, ROWS, HALF),
            vmem(4, ROWS, D),
            vmem(4, ROWS, D),
            pltpu.SemaphoreType.DMA((160,)),
            pltpu.SemaphoreType.DMA((160,)),
        ],
        name="layer",
        cost_estimate=pl.CostEstimate(
            flops=11 * 10**9, bytes_accessed=12 * 10**6, transcendentals=0
        ),
        compiler_params=pltpu.CompilerParams(
            collective_id=1, has_side_effects=True, vmem_limit_bytes=60 << 20
        ),
    )(*arguments)


def sum_kernel(*refs):
    inputs, refs = refs[:3], refs[3:]
    outs, refs = refs[:5], refs[5:]
    sent, refs = refs[:3], refs[3:]
    work, refs = refs[:3], refs[3:]
    far, near, passed = refs[:3], refs[3:6], refs[6:9]
    kept, came, final = refs[9:12], refs[12:15], refs[15:18]
    turned, send, recv = refs[18:]
    net = Net(send, recv)
    net.barrier([net.twin, net.up, net.down, net.beside, *net.peers])
    core, y, s = net.core, net.y, net.s
    half = [512, 512, 128]
    width = [D, 896, 256]
    mine = pl.ds(core * 4, 4)
    up, down, facing = (lax.rem(y + k, 4) for k in (1, 3, 2))
    q = core * 4 + y

    moved = [net.copy(a.at[pl.ds((1 - core) * 4, 4)], b, net.twin) for a, b in zip(inputs, sent)]
    for i in range(3):
        moved[i].wait_recv()
        work[i][...] = add(inputs[i][mine], sent[i][...]).astype(BF16)

    halves = [(pl.ds(0, n), pl.ds(n, w - n)) for n, w in zip(half, width)]
    fars, nears, passes = [], [], []
    for i in range(3):
        one, two = halves[i]
        fars.append(
            (
                net.copy(work[i].at[facing, :, one], far[i].at[:, one], net.up),
                net.copy(work[i].at[facing, :, two], far[i].at[:, two], net.down),
            )
        )
    for i in range(3):
        one, two = halves[i]
        nears.append(
            (
                net.copy(work[i].at[up, :, two], near[i].at[:, two], net.up),
                net.copy(work[i].at[down, :, one], near[i].at[:, one], net.down),
            )
        )
    for i in range(3):
        made = []
        for k, (block, to) in enumerate(((up, net.up), (down, net.down))):
            fars[i][k].wait_recv()
            part = halves[i][k]
            far[i][:, part] = add(far[i][:, part], work[i][block, :, part]).astype(BF16)
            made.append(net.copy(far[i].at[:, part], passed[i].at[:, part], to))
        passes.append(made)
    over = []
    for i in range(3):
        for made in (*nears[i], *passes[i]):
            made.wait_recv()
        kept[i][...] = add(work[i][y], near[i][...], passed[i][...]).astype(BF16)
        over.append(net.copy(kept[i], came[i], net.beside))
    over[1].wait_recv()
    turned[...] = add(kept[1][...], came[1][...]).astype(BF16).reshape(8, 16, 896)
    place = lambda t: pl.ds(pl.multiple_of(t * 16, 16), 16)
    crossed = [
        net.copy(turned.at[to["shard"]], final[1].at[q, place(s)], to) for to in net.peers
    ]
    final[1][q, place(s)] = turned[s]
    for i in (0, 2):
        over[i].wait_recv()
        final[i][q] = add(kept[i][...], came[i][...]).astype(BF16)
    for made in crossed:
        made.wait_recv()

    steps = []
    for i in range(3):
        own = final[i].at[q]
        steps.append((net.copy(own, own, net.up), net.copy(own, own, net.down)))
    lasts = []
    for i in range(3):
        one, two = halves[i]
        steps[i][0].wait_recv()
        part = final[i].at[core * 4 + down, :, one]
        lasts.append(net.copy(part, part, net.up))
        steps[i][1].wait_recv()
        part = final[i].at[core * 4 + up, :, two]
        lasts.append(net.copy(part, part, net.down))
    ends = []
    for i in range(3):
        lasts[2 * i].wait_recv()
        lasts[2 * i + 1].wait_recv()
        part = final[i].at[mine]
        ends.append(net.copy(part, part, net.twin))
    for made in ends:
        made.wait_recv()
    qkv_grad, out_grad, up_grad, down_grad, small = outs
    for k in range(8):
        down_grad[k * 64 : (k + 1) * 64, :] = final[0][k, 0:64, :]
        out_grad[k * 16 : (k + 1) * 16, :] = final[0][k, 64:80, :]
        rows = slice(k * 16, (k + 1) * 16)
        for t in range(8):
            block = final[1][k, t * 16 : (t + 1) * 16, :]
            up_grad[rows, t * 512 : (t + 1) * 512] = block[:, 384:896]
            for i in range(3):
                at = i * D + t * 128
                qkv_grad[rows, at : at + 128] = block[:, i * 128 : (i + 1) * 128]
    small[...] = final[2][0]
    net.drain()


def sum_replicas(*arguments):
    space = pl.BlockSpec(memory_space=pltpu.VMEM)
    shape = lambda *sizes: jax.ShapeDtypeStruct(sizes, BF16)
    sizes = ((80, D), (128, 896), (16, 256))
    vmem = lambda *lead: [pltpu.VMEM((*lead, *size), BF16) for size in sizes]
    return pl.pallas_call(
        sum_kernel,
        out_shape=[
            shape(128, 3 * D),
            shape(128, D),
            shape(128, 4096),
            shape(512, D),
            shape(16, 256),
        ],
        in_specs=[space] * 3,
        out_specs=[space] * 5,
        scratch_shapes=[
            *vmem(4),
            *vmem(4),
            *vmem(),
            *vmem(),
            *vmem(),
            *vmem(),
            *vmem(),
            *vmem(8),
            pltpu.VMEM((8, 16, 896), BF16),
            pltpu.SemaphoreType.DMA((64,)),
            pltpu.SemaphoreType.DMA((64,)),
        ],
        name="sum_replicas",
        compiler_params=pltpu.CompilerParams(
            collective_id=2, has_side_effects=True, vmem_limit_bytes=48 << 20
        ),
    )(*arguments)


def body(
    tokens,
    cotangent,
    attn_gain,
    attn_shift,
    qkv_weight,
    query_bias,
    value_bias,
    out_weight,
    out_bias,
    mlp_gain,
    mlp_shift,
    up_weight,
    up_bias,
    down_weight,
    down_bias,
):
    vectors = jnp.stack([attn_gain, attn_shift, mlp_gain, mlp_shift, out_bias, down_bias])
    vectors = jnp.pad(vectors, ((0, 10), (0, 0)))
    zeros = jnp.zeros((128,), F32)
    qkv_bias = jnp.concatenate([query_bias.astype(F32), zeros, value_bias.astype(F32)])
    block_out, input_grad, *grads = layer(
        tokens.reshape(ROWS, D),
        cotangent.reshape(ROWS, D),
        vectors,
        qkv_weight,
        up_weight,
        out_weight,
        down_weight,
        qkv_bias.reshape(1, 384),
        up_bias.astype(F32).reshape(1, 512),
    )
    sums = [a.astype(F32) for a in sum_replicas(*grads)]
    qkv_grad, out_grad, up_grad, down_grad, small = sums
    small = small[:, :128]
    return (
        block_out.reshape(2, 72, D),
        input_grad.reshape(2, 72, D),
        small[0],
        small[1],
        qkv_grad,
        small[4],
        small[5],
        out_grad,
        small[6],
        small[2],
        small[3],
        up_grad,
        small[8:12].reshape(512),
        down_grad,
        small[7],
    )


def solution(mesh):
    row, cube, flat = P("shard"), P("replica", "shard", None), P("shard", None)
    return jax.shard_map(
        body,
        mesh=mesh,
        in_specs=(cube, cube, row, row, flat, row, row, flat, row, row, row, flat, row, flat, row),
        out_specs=(cube, cube, row, row, flat, row, row, flat, row, row, row, flat, row, flat, row),
        check_vma=False,
    )
```

```python
import jax
import jax.numpy as jnp
from jax import lax
from jax.experimental import pallas as pl
from jax.experimental.pallas import tpu as pltpu
from jax.sharding import PartitionSpec as P

HEAD_DIM = 64
EPS = 1e-06
F32 = jnp.float32
BF16 = jnp.bfloat16
SCALE = HEAD_DIM ** (-0.5)
MESH = pl.DeviceIdType.MESH
D = 1024
ROWS = 144
HALF = 512
GELU = 0.7978845608028654


def dot(a, b):
    return lax.dot_general(a, b, (((1,), (0,)), ((), ())), preferred_element_type=F32)


def dot_last(a, b):
    return lax.dot_general(a, b, (((1,), (1,)), ((), ())), preferred_element_type=F32)


def dot_first(a, b):
    return lax.dot_general(a, b, (((0,), (0,)), ((), ())), preferred_element_type=F32)


def norm_unit(v):
    mean = jnp.mean(v, -1, keepdims=True)
    centred = v - mean
    inverse = lax.rsqrt(jnp.mean(centred * centred, -1, keepdims=True) + EPS)
    return centred * inverse, inverse


def norm_back(grad, unit, inverse, gain):
    gn = grad * gain
    inner = jnp.mean(gn * unit, -1, keepdims=True)
    return inverse * (gn - jnp.mean(gn, -1, keepdims=True) - unit * inner)


def head_masks(shape):
    low = lax.broadcasted_iota(jnp.int32, shape, 1) < HEAD_DIM
    return (low, jnp.logical_not(low))


def add(*terms):
    total = terms[0].astype(F32)
    for term in terms[1:]:
        total = total + term.astype(F32)
    return total


class Net:
    def __init__(self, send, recv):
        self.send, self.recv, self.count, self.open = send, recv, 0, []
        self.s = lax.axis_index("shard")
        self.h, self.x = self.s // 4, lax.rem(self.s, 4)
        r = lax.axis_index("replica")
        self.core, self.y = lax.rem(r, 2), lax.rem(r // 2, 4)
        zlow = r // 8
        base = r - self.y * 2
        self.right = {"shard": self.at(self.h, self.x + 1)}
        self.left = {"shard": self.at(self.h, self.x + 3)}
        self.across = {"shard": self.at(1 - self.h, self.x)}
        self.twin = {"replica": r + 1 - 2 * self.core}
        self.up = {"replica": base + lax.rem(self.y + 1, 4) * 2}
        self.down = {"replica": base + lax.rem(self.y + 3, 4) * 2}
        self.beside = {"replica": r + 8 - 16 * zlow}
        self.peers = [{"shard": lax.rem(self.s + k, 8)} for k in range(1, 8)]

    def at(self, h, x):
        return h * 4 + lax.rem(x, 4)

    def copy(self, src, dst, to):
        i = self.count
        self.count += 1
        made = pltpu.make_async_remote_copy(
            src_ref=src,
            dst_ref=dst,
            send_sem=self.send.at[i],
            recv_sem=self.recv.at[i],
            device_id=to,
            device_id_type=MESH,
        )
        made.start()
        self.open.append(made)
        return made

    def drain(self):
        for made in self.open:
            made.wait_send()
        self.open = []

    def barrier(self, others):
        semaphore = pltpu.get_barrier_semaphore()
        for other in others:
            pl.semaphore_signal(semaphore, inc=1, device_id=other, device_id_type=MESH)
        pl.semaphore_wait(semaphore, len(others))


class Gather:
    def __init__(self, net, whole):
        self.net, self.whole = net, whole
        self.a = self.piece(net.s, 0, net.right)
        self.b = self.piece(net.s, 1, net.left)
        own = whole.at[net.s]
        self.z = net.copy(own, own, net.across)
        self.more = [self.piece(net.s, 1, net.right), self.piece(net.s, 0, net.left)]

    def piece(self, block, second, to):
        part = self.whole.at[block, :, pl.ds(second * HALF, HALF)]
        return self.net.copy(part, part, to)

    def relay_one(self):
        net = self.net
        self.a.wait_recv()
        self.c = self.piece(net.at(net.h, net.x + 3), 0, net.right)
        self.b.wait_recv()
        self.d = self.piece(net.at(net.h, net.x + 1), 1, net.left)

    def relay_two(self):
        net = self.net
        self.z.wait_recv()
        part = self.whole.at[net.at(1 - net.h, net.x)]
        self.rest = [net.copy(part, part, net.right), net.copy(part, part, net.left)]
        block = net.at(net.h, net.x + 2)
        self.c.wait_recv()
        self.rest.append(self.piece(block, 0, net.across))
        self.d.wait_recv()
        self.rest.append(self.piece(block, 1, net.across))

    def row(self):
        for made in self.more:
            made.wait_recv()

    def finish(self):
        for made in self.rest:
            made.wait_recv()


class Scatter:
    def __init__(self, net, part, hop, side, near, far, passed, kept, came):
        self.net, self.part, self.hop_in, self.side_in = net, part, hop, side
        self.near_in, self.far_in, self.passed, self.kept, self.came = near, far, passed, kept, came
        self.one, self.two = pl.ds(0, HALF), pl.ds(HALF, HALF)
        h, x = net.h, net.x
        self.own, self.facing = net.s, net.at(h, x + 2)
        self.right, self.left = net.at(h, x + 1), net.at(h, x + 3)
        self.other = [net.at(1 - h, x + k) for k in range(4)]

    def hop(self):
        self.hopped = self.net.copy(self.part.at[self.other[2]], self.hop_in, self.net.across)

    def side(self):
        net, part = self.net, self.part
        self.sides = [
            net.copy(part.at[self.other[1]], self.side_in.at[0], net.right),
            net.copy(part.at[self.other[3]], self.side_in.at[1], net.left),
        ]

    def near(self):
        net, part = self.net, self.part
        self.nears = [
            net.copy(part.at[self.right, :, self.two], self.near_in.at[0], net.right),
            net.copy(part.at[self.left, :, self.one], self.near_in.at[1], net.left),
        ]

    def far(self):
        net, hop = self.net, self.hop_in
        self.hopped.wait_recv()
        hop[...] = add(hop[...], self.part[self.facing]).astype(BF16)
        self.fars = [
            net.copy(hop.at[:, self.one], self.far_in.at[0], net.right),
            net.copy(hop.at[:, self.two], self.far_in.at[1], net.left),
        ]

    def over(self):
        for made in self.sides:
            made.wait_recv()
        self.kept[...] = add(
            self.part[self.other[0]], self.side_in[0], self.side_in[1]
        ).astype(BF16)
        self.crossed = self.net.copy(self.kept, self.came, self.net.across)

    def relay(self):
        net, part, far = self.net, self.part, self.far_in
        self.fars[0].wait_recv()
        far[0] = add(far[0], part[self.right, :, self.one]).astype(BF16)
        passes = [net.copy(far.at[0], self.passed.at[0], net.right)]
        self.fars[1].wait_recv()
        far[1] = add(far[1], part[self.left, :, self.two]).astype(BF16)
        passes.append(net.copy(far.at[1], self.passed.at[1], net.left))
        self.last = [*self.nears, *passes, self.crossed]

    def finish(self):
        for made in self.last:
            made.wait_recv()
        part, near, passed, came = self.part, self.near_in, self.passed, self.came
        one, two = self.one, self.two
        return jnp.concatenate(
            [
                add(part[self.own, :, one], passed[0], near[1], came[:, one]),
                add(part[self.own, :, two], passed[1], near[0], came[:, two]),
            ],
            axis=1,
        )


def layer_kernel(
    tokens,
    cotangent,
    vectors,
    qkv_weight,
    up_weight,
    out_weight,
    down_weight,
    qkv_bias,
    up_bias,
    block_out,
    input_grad,
    rows_grad,
    columns_grad,
    small_grad,
    all_vectors,
    columns,
    first,
    cot,
    second,
    branch,
    mixed,
    qkv_low,
    heads,
    lse,
    attended,
    active,
    grad_upper,
    grad_qkv,
    resid_ref,
    grad_resid_ref,
    small,
    fours,
    fours_in,
    parts,
    hop,
    side,
    near,
    far,
    passed,
    kept,
    came,
    send,
    recv,
):
    net = Net(send, recv)
    s, core = net.s, net.core
    net.barrier([*net.peers, net.twin])
    source = [lax.rem(s + 8 - k, 8) for k in range(1, 8)]
    mine = pl.ds(pl.multiple_of(core * 64, 64), 64)

    def scatter(i):
        buffers = (parts, hop, side, near, far, passed, kept, came)
        return Scatter(net, *(buffer.at[i] for buffer in buffers))

    def each(work, least, end, carry=0):
        def step(i, carry):
            row, j = i // 4, lax.rem(i, 4)
            same = j + j // 2 - 2 * (j // 3)
            cross = lax.rem(2 * j, 3) + 3 * (j // 3)
            h = net.h + row - 2 * net.h * row
            return work(net.at(h, net.x + (1 - row) * same + row * cross), carry)

        return lax.fori_loop(least, end, step, carry)

    def each_sent(rs, work, carry):
        carry = each(work, 5, 6, carry)
        rs.hop()
        carry = each(work, 6, 8, carry)
        rs.side()
        carry = each(work, 1, 3, carry)
        rs.near()
        carry = each(work, 3, 5, carry)
        rs.far()
        return each(work, 0, 1, carry)

    vec = [net.copy(vectors, all_vectors.at[s], to) for to in net.peers]
    all_vectors[s] = vectors[...]
    qkv_in, up_in = [], []
    for k, to in enumerate(net.peers):
        t = to["shard"]
        qkv_in.append(
            [
                net.copy(
                    qkv_weight.at[mine, pl.ds(pl.multiple_of(i * D + t * 128, 128), 128)],
                    columns.at[s, mine, pl.ds(i * 128, 128)],
                    to,
                )
                for i in range(3)
            ]
        )
    for i in range(3):
        columns[s, :, i * 128 : (i + 1) * 128] = qkv_weight[
            :, pl.ds(pl.multiple_of(i * D + s * 128, 128), 128)
        ]
    columns[s, :, 384:896] = up_weight[:, pl.ds(pl.multiple_of(s * 512, 512), 512)]
    cot[s] = cotangent[...]
    x = tokens[...].astype(F32)
    unit1, inverse1 = norm_unit(x)
    for made in vec:
        made.wait_recv()
    table = [all_vectors[j].astype(F32) for j in range(8)]
    gain1, shift1, gain2, shift2, bias_out, bias_down = (
        jnp.concatenate([t[i : i + 1] for t in table], axis=1) for i in range(6)
    )
    first[s] = (unit1 * gain1 + shift1).astype(BF16)
    ag = Gather(net, first)
    qkv_pass = []
    for k in range(7):
        for made in qkv_in[k]:
            made.wait_recv()
        block = columns.at[source[k], mine, pl.ds(0, 384)]
        qkv_pass.append(net.copy(block, block, net.twin))
    ag.relay_one()
    ag.relay_two()
    for k, to in enumerate(net.peers):
        up_in.append(
            net.copy(
                up_weight.at[mine, pl.ds(pl.multiple_of(to["shard"] * 512, 512), 512)],
                columns.at[s, mine, pl.ds(384, 512)],
                to,
            )
        )
    for made in qkv_pass:
        made.wait_recv()
    ag.row()

    def project(b, carry):
        value = dot(first[b], columns[:, :, 0:384].reshape(D, 384)) + qkv_bias[...]
        at = pl.multiple_of(b * 72, 8)
        mixed[0, pl.ds(at, 72), :] = value[0:72]
        mixed[1, pl.ds(at, 72), :] = value[72:144]
        return carry

    each(project, 0, 5)
    ag.finish()
    ag_cot = Gather(net, cot)
    each(project, 5, 8)
    qkv_low[...] = mixed[...].astype(BF16)
    ag_cot.relay_one()

    def attend(image, carry):
        q, k, v = (qkv_low[image, :, i * 128 : (i + 1) * 128] for i in range(3))
        zero = jnp.zeros_like(q)
        total = jnp.zeros(q.shape, F32)
        for h, mask in enumerate(head_masks(q.shape)):
            score = dot_last(jnp.where(mask, q, zero), k) * SCALE
            top = jnp.max(score, -1, keepdims=True)
            e = jnp.exp(score - top)
            row = jnp.sum(e, -1, keepdims=True)
            p = (e * (1.0 / row)).astype(BF16)
            total += dot(p, jnp.where(mask, v, zero))
            lse[image, :, h : h + 1] = top + jnp.log(row)
        heads[image] = total
        return carry

    lax.fori_loop(0, 2, attend, 0)
    ag_cot.relay_two()
    up_pass = []
    for k in range(7):
        up_in[k].wait_recv()
        block = columns.at[source[k], mine, pl.ds(384, 512)]
        up_pass.append(net.copy(block, block, net.twin))

    def by_device(ref, b):
        at = pl.multiple_of(b * 72, 8)
        both = [ref[i, pl.ds(at, 72), :] for i in range(2)]
        return jnp.concatenate(both, axis=0).astype(BF16)

    def outward(b, carry):
        value = by_device(heads, b)
        attended[b] = value
        parts[0, b] = dot(value, out_weight[...]).astype(BF16)
        return carry

    rs = scatter(0)
    each_sent(rs, outward, 0)
    rs.over()
    rs.relay()
    resid = tokens[...].astype(F32) + (rs.finish() + bias_out)
    resid_ref[...] = resid
    unit2, inverse2 = norm_unit(resid)
    second[s] = (unit2 * gain2 + shift2).astype(BF16)
    ag = Gather(net, second)
    ag_cot.row()
    ag_cot.finish()
    for made in up_pass:
        made.wait_recv()

    def feed(b, total):
        up = columns[:, :, 384:896].reshape(D, 512)
        u = dot(second[b], up) + up_bias[...]
        square = u * u
        t = jnp.tanh(GELU * (u + 0.044715 * u * square))
        act = (0.5 * u * (1.0 + t)).astype(BF16)
        slope = 0.5 * (1.0 + t) + (0.5 * GELU) * u * (1.0 - t * t) * (
            1.0 + 0.134145 * square
        )
        active[b] = act
        gu = (dot_last(cot[b], down_weight[...]) * slope).astype(BF16)
        grad_upper[b] = gu
        parts[1, b] = dot_last(gu, up).astype(BF16)
        parts[2, b] = dot(act, down_weight[...]).astype(BF16)
        return total + jnp.sum(gu.astype(F32), 0, keepdims=True)

    ag.relay_one()
    up_bias_grad = each(feed, 0, 1, jnp.zeros((1, 512), F32))
    ag.relay_two()
    ag.row()
    up_bias_grad = each(feed, 1, 5, up_bias_grad)
    ag.finish()
    rs = scatter(1)
    up_bias_grad = each(feed, 5, 6, up_bias_grad)
    rs.hop()
    up_bias_grad = each(feed, 6, 8, up_bias_grad)
    rs.side()
    rs.near()
    own = pl.ds(pl.multiple_of(s * 128, 128), 128)
    small[...] = jnp.zeros_like(small)
    for i in range(4):
        small[8 + i : 9 + i, 0:128] = up_bias_grad[:, i * 128 : (i + 1) * 128]
    small[7:8, 0:128] = jnp.sum(cot[:, :, own].astype(F32).reshape(1152, 128), 0, keepdims=True)

    def down_tile(i):
        at = pl.ds(i * 256, 256)
        value = dot_first(
            active[...].reshape(1152, 512), cot[:, :, at].reshape(1152, 256)
        ).astype(BF16)
        for q in range(8):
            rows_grad[q, 0:64, at] = value[q * 64 : (q + 1) * 64]

    down_tile(0)
    rs.far()
    down_tile(1)
    rs.over()
    rs.relay()
    down_tile(2)
    down_tile(3)
    grad_second = rs.finish()
    unit2, inverse2 = norm_unit(resid_ref[...])
    grad_resid = cotangent[...].astype(F32) + norm_back(grad_second, unit2, inverse2, gain2)
    grad_resid_ref[...] = grad_resid
    branch[s] = grad_resid.astype(BF16)
    ag = Gather(net, branch)
    gain2_grad = jnp.sum(grad_second * unit2, 0, keepdims=True)
    shift2_grad = jnp.sum(grad_second, 0, keepdims=True)

    def up_tile(i):
        value = dot_first(
            second[:, :, i * 256 : (i + 1) * 256].reshape(1152, 256),
            grad_upper[...].reshape(1152, 512),
        ).astype(BF16)
        for j in range(2):
            for q in range(8):
                columns_grad[q, (2 * i + j) * 16 : (2 * i + j + 1) * 16, 384:896] = value[
                    j * 128 + q * 16 : j * 128 + (q + 1) * 16
                ]

    ag.relay_one()
    up_tile(0)
    ag.relay_two()
    ag.row()
    up_tile(1)
    up_tile(2)
    ag.finish()
    rs_out = scatter(2)
    rs_out.hop()
    rs_out.side()
    rs_out.near()

    def back_heads(b, carry):
        value = dot_last(branch[b], out_weight[...])
        at = pl.multiple_of(b * 72, 8)
        heads[0, pl.ds(at, 72), :] = value[0:72]
        heads[1, pl.ds(at, 72), :] = value[72:144]
        return carry

    each(back_heads, 0, 8)
    up_tile(3)
    rs_out.far()

    def attend_back(image, carry):
        q, k, v = (qkv_low[image, :, i * 128 : (i + 1) * 128] for i in range(3))
        grad = heads[image].astype(BF16)
        zero = jnp.zeros_like(q)
        dq = jnp.zeros(q.shape, F32)
        dk, dv = dq, dq
        for h, mask in enumerate(head_masks(q.shape)):
            qh, kh, gh = (jnp.where(mask, a, zero) for a in (q, k, grad))
            p = jnp.exp(dot_last(qh, k) * SCALE - lse[image, :, h : h + 1])
            dp = dot_last(gh, v)
            inner = jnp.sum(p * dp, -1, keepdims=True)
            ds = (p * (dp - inner)).astype(BF16)
            dq += dot(ds, kh)
            dk += dot_first(ds, qh)
            dv += dot_first(p.astype(BF16), gh)
        mixed[image, :, 0:128] = dq * SCALE
        mixed[image, :, 128:256] = dk * SCALE
        mixed[image, :, 256:384] = dv
        return carry

    lax.fori_loop(0, 2, attend_back, 0)
    rs_out.over()
    rs_out.relay()

    def back_first(b, total):
        value = by_device(mixed, b)
        grad_qkv[b] = value
        parts[3, b] = dot_last(value, columns[:, :, 0:384].reshape(D, 384)).astype(BF16)
        return total + jnp.sum(value.astype(F32), 0, keepdims=True)

    rs = scatter(3)
    qkv_bias_grad = each_sent(rs, back_first, jnp.zeros((1, 384), F32))
    small[4:5, 0:128] = qkv_bias_grad[:, 0:128]
    small[5:6, 0:128] = qkv_bias_grad[:, 256:384]
    small[6:7, 0:128] = jnp.sum(branch[:, :, own].astype(F32).reshape(1152, 128), 0, keepdims=True)

    def qkv_tile(i):
        value = dot_first(
            first[:, :, i * 256 : (i + 1) * 256].reshape(1152, 256),
            grad_qkv[...].reshape(1152, 384),
        ).astype(BF16)
        for j in range(2):
            for q in range(8):
                columns_grad[q, (2 * i + j) * 16 : (2 * i + j + 1) * 16, 0:384] = value[
                    j * 128 + q * 16 : j * 128 + (q + 1) * 16
                ]

    qkv_tile(0)
    rs.over()
    qkv_tile(1)
    rs.relay()
    qkv_tile(2)
    qkv_tile(3)
    value = dot_first(attended[...].reshape(1152, 128), branch[...].reshape(1152, D)).astype(BF16)
    for q in range(8):
        rows_grad[q, 64:80, :] = value[q * 16 : (q + 1) * 16]
    block_out[...] = (resid_ref[...] + (rs_out.finish() + bias_down)).astype(BF16)
    grad_first = rs.finish()
    unit1, inverse1 = norm_unit(tokens[...].astype(F32))
    input_grad[...] = (
        grad_resid_ref[...] + norm_back(grad_first, unit1, inverse1, gain1)
    ).astype(BF16)
    gain1_grad = jnp.sum(grad_first * unit1, 0, keepdims=True)
    shift1_grad = jnp.sum(grad_first, 0, keepdims=True)
    four = jnp.concatenate(
        [gain1_grad, shift1_grad, gain2_grad, shift2_grad, jnp.zeros((12, D), F32)], axis=0
    ).astype(BF16)
    for t in range(8):
        fours[t] = four[:, t * 128 : (t + 1) * 128]
    moved = [net.copy(fours.at[to["shard"]], fours_in.at[s], to) for to in net.peers]
    fours_in[s] = fours[s]
    for made in moved:
        made.wait_recv()
    total = jnp.sum(fours_in[...].astype(F32), 0)
    small[0:4, 0:128] = total[0:4]
    small_grad[...] = jnp.zeros_like(small_grad)
    small_grad[0] = small[...].astype(BF16)
    net.drain()


def layer(*arguments):
    vmem = lambda *shape: pltpu.VMEM(shape, BF16)
    wide = lambda *shape: pltpu.VMEM(shape, F32)
    space = pl.BlockSpec(memory_space=pltpu.VMEM)
    shape = lambda *sizes: jax.ShapeDtypeStruct(sizes, BF16)
    return pl.pallas_call(
        layer_kernel,
        out_shape=[
            shape(ROWS, D),
            shape(ROWS, D),
            shape(8, 80, D),
            shape(8, 128, 896),
            shape(8, 16, 256),
        ],
        in_specs=[space] * 9,
        out_specs=[space] * 5,
        scratch_shapes=[
            vmem(8, 16, 128),
            vmem(8, 128, 896),
            vmem(8, ROWS, D),
            vmem(8, ROWS, D),
            vmem(8, ROWS, D),
            vmem(8, ROWS, D),
            wide(2, 576, 384),
            vmem(2, 576, 384),
            wide(2, 576, 128),
            wide(2, 576, 128),
            vmem(8, ROWS, 128),
            vmem(8, ROWS, 512),
            vmem(8, ROWS, 512),
            vmem(8, ROWS, 384),
            wide(ROWS, D),
            wide(ROWS, D),
            wide(16, 256),
            vmem(8, 16, 128),
            vmem(8, 16, 128),
            vmem(4, 8, ROWS, D),
            vmem(4, ROWS, D),
            vmem(4, 2, ROWS, D),
            vmem(4, 2, ROWS, HALF),
            vmem(4, 2, ROWS, HALF),
            vmem(4, 2, ROWS, HALF),
            vmem(4, ROWS, D),
            vmem(4, ROWS, D),
            pltpu.SemaphoreType.DMA((160,)),
            pltpu.SemaphoreType.DMA((160,)),
        ],
        name="layer",
        cost_estimate=pl.CostEstimate(
            flops=11 * 10**9, bytes_accessed=12 * 10**6, transcendentals=0
        ),
        compiler_params=pltpu.CompilerParams(
            collective_id=1, has_side_effects=True, vmem_limit_bytes=60 << 20
        ),
    )(*arguments)


def sum_kernel(*refs):
    inputs, refs = refs[:3], refs[3:]
    outs, refs = refs[:5], refs[5:]
    sent, refs = refs[:3], refs[3:]
    work, refs = refs[:3], refs[3:]
    far, near, passed = refs[:3], refs[3:6], refs[6:9]
    kept, came, final = refs[9:12], refs[12:15], refs[15:18]
    turned, send, recv = refs[18:]
    net = Net(send, recv)
    net.barrier([net.twin, net.up, net.down, net.beside, *net.peers])
    core, y, s = net.core, net.y, net.s
    half = [512, 512, 128]
    width = [D, 896, 256]
    mine = pl.ds(core * 4, 4)
    up, down, facing = (lax.rem(y + k, 4) for k in (1, 3, 2))
    q = core * 4 + y

    moved = [net.copy(a.at[pl.ds((1 - core) * 4, 4)], b, net.twin) for a, b in zip(inputs, sent)]
    for i in range(3):
        moved[i].wait_recv()
        work[i][...] = add(inputs[i][mine], sent[i][...]).astype(BF16)

    halves = [(pl.ds(0, n), pl.ds(n, w - n)) for n, w in zip(half, width)]
    fars, nears, passes = [], [], []
    for i in range(3):
        one, two = halves[i]
        fars.append(
            (
                net.copy(work[i].at[facing, :, one], far[i].at[:, one], net.up),
                net.copy(work[i].at[facing, :, two], far[i].at[:, two], net.down),
            )
        )
    for i in range(3):
        one, two = halves[i]
        nears.append(
            (
                net.copy(work[i].at[up, :, two], near[i].at[:, two], net.up),
                net.copy(work[i].at[down, :, one], near[i].at[:, one], net.down),
            )
        )
    for i in range(3):
        made = []
        for k, (block, to) in enumerate(((up, net.up), (down, net.down))):
            fars[i][k].wait_recv()
            part = halves[i][k]
            far[i][:, part] = add(far[i][:, part], work[i][block, :, part]).astype(BF16)
            made.append(net.copy(far[i].at[:, part], passed[i].at[:, part], to))
        passes.append(made)
    over = []
    for i in range(3):
        for made in (*nears[i], *passes[i]):
            made.wait_recv()
        kept[i][...] = add(work[i][y], near[i][...], passed[i][...]).astype(BF16)
        over.append(net.copy(kept[i], came[i], net.beside))
    over[1].wait_recv()
    turned[...] = add(kept[1][...], came[1][...]).astype(BF16).reshape(8, 16, 896)
    place = lambda t: pl.ds(pl.multiple_of(t * 16, 16), 16)
    crossed = [
        net.copy(turned.at[to["shard"]], final[1].at[q, place(s)], to) for to in net.peers
    ]
    final[1][q, place(s)] = turned[s]
    for i in (0, 2):
        over[i].wait_recv()
        final[i][q] = add(kept[i][...], came[i][...]).astype(BF16)
    for made in crossed:
        made.wait_recv()

    steps = []
    for i in range(3):
        own = final[i].at[q]
        steps.append((net.copy(own, own, net.up), net.copy(own, own, net.down)))
    lasts = []
    for i in range(3):
        one, two = halves[i]
        steps[i][0].wait_recv()
        part = final[i].at[core * 4 + down, :, one]
        lasts.append(net.copy(part, part, net.up))
        steps[i][1].wait_recv()
        part = final[i].at[core * 4 + up, :, two]
        lasts.append(net.copy(part, part, net.down))
    ends = []
    for i in range(3):
        lasts[2 * i].wait_recv()
        lasts[2 * i + 1].wait_recv()
        part = final[i].at[mine]
        ends.append(net.copy(part, part, net.twin))
    for made in ends:
        made.wait_recv()
    qkv_grad, out_grad, up_grad, down_grad, small = outs
    for k in range(8):
        down_grad[k * 64 : (k + 1) * 64, :] = final[0][k, 0:64, :]
        out_grad[k * 16 : (k + 1) * 16, :] = final[0][k, 64:80, :]
        rows = slice(k * 16, (k + 1) * 16)
        for t in range(8):
            block = final[1][k, t * 16 : (t + 1) * 16, :]
            up_grad[rows, t * 512 : (t + 1) * 512] = block[:, 384:896]
            for i in range(3):
                at = i * D + t * 128
                qkv_grad[rows, at : at + 128] = block[:, i * 128 : (i + 1) * 128]
    small[...] = final[2][0]
    net.drain()


def sum_replicas(*arguments):
    space = pl.BlockSpec(memory_space=pltpu.VMEM)
    shape = lambda *sizes: jax.ShapeDtypeStruct(sizes, BF16)
    sizes = ((80, D), (128, 896), (16, 256))
    vmem = lambda *lead: [pltpu.VMEM((*lead, *size), BF16) for size in sizes]
    return pl.pallas_call(
        sum_kernel,
        out_shape=[
            shape(128, 3 * D),
            shape(128, D),
            shape(128, 4096),
            shape(512, D),
            shape(16, 256),
        ],
        in_specs=[space] * 3,
        out_specs=[space] * 5,
        scratch_shapes=[
            *vmem(4),
            *vmem(4),
            *vmem(),
            *vmem(),
            *vmem(),
            *vmem(),
            *vmem(),
            *vmem(8),
            pltpu.VMEM((8, 16, 896), BF16),
            pltpu.SemaphoreType.DMA((64,)),
            pltpu.SemaphoreType.DMA((64,)),
        ],
        name="sum_replicas",
        compiler_params=pltpu.CompilerParams(
            collective_id=2, has_side_effects=True, vmem_limit_bytes=48 << 20
        ),
    )(*arguments)


def body(
    tokens,
    cotangent,
    attn_gain,
    attn_shift,
    qkv_weight,
    query_bias,
    value_bias,
    out_weight,
    out_bias,
    mlp_gain,
    mlp_shift,
    up_weight,
    up_bias,
    down_weight,
    down_bias,
):
    vectors = jnp.stack([attn_gain, attn_shift, mlp_gain, mlp_shift, out_bias, down_bias])
    vectors = jnp.pad(vectors, ((0, 10), (0, 0)))
    zeros = jnp.zeros((128,), F32)
    qkv_bias = jnp.concatenate([query_bias.astype(F32), zeros, value_bias.astype(F32)])
    block_out, input_grad, *grads = layer(
        tokens.reshape(ROWS, D),
        cotangent.reshape(ROWS, D),
        vectors,
        qkv_weight,
        up_weight,
        out_weight,
        down_weight,
        qkv_bias.reshape(1, 384),
        up_bias.astype(F32).reshape(1, 512),
    )
    sums = [a.astype(F32) for a in sum_replicas(*grads)]
    qkv_grad, out_grad, up_grad, down_grad, small = sums
    small = small[:, :128]
    return (
        block_out.reshape(2, 72, D),
        input_grad.reshape(2, 72, D),
        small[0],
        small[1],
        qkv_grad,
        small[4],
        small[5],
        out_grad,
        small[6],
        small[2],
        small[3],
        up_grad,
        small[8:12].reshape(512),
        down_grad,
        small[7],
    )


def solution(mesh):
    row, cube, flat = P("shard"), P("replica", "shard", None), P("shard", None)
    return jax.shard_map(
        body,
        mesh=mesh,
        in_specs=(cube, cube, row, row, flat, row, row, flat, row, row, row, flat, row, flat, row),
        out_specs=(cube, cube, row, row, flat, row, row, flat, row, row, row, flat, row, flat, row),
        check_vma=False,
    )
```

```python
import jax
import jax.numpy as jnp
from jax import lax
from jax.experimental import pallas as pl
from jax.experimental.pallas import tpu as pltpu
from jax.sharding import PartitionSpec as P

HEAD_DIM = 64
EPS = 1e-06
F32 = jnp.float32
BF16 = jnp.bfloat16
SCALE = HEAD_DIM ** (-0.5)
MESH = pl.DeviceIdType.MESH
D = 1024
ROWS = 144
HALF = 512
GELU = 0.7978845608028654


def dot(a, b):
    return lax.dot_general(a, b, (((1,), (0,)), ((), ())), preferred_element_type=F32)


def dot_last(a, b):
    return lax.dot_general(a, b, (((1,), (1,)), ((), ())), preferred_element_type=F32)


def dot_first(a, b):
    return lax.dot_general(a, b, (((0,), (0,)), ((), ())), preferred_element_type=F32)


def norm_unit(v):
    mean = jnp.mean(v, -1, keepdims=True)
    centred = v - mean
    inverse = lax.rsqrt(jnp.mean(centred * centred, -1, keepdims=True) + EPS)
    return centred * inverse, inverse


def norm_back(grad, unit, inverse, gain):
    gn = grad * gain
    inner = jnp.mean(gn * unit, -1, keepdims=True)
    return inverse * (gn - jnp.mean(gn, -1, keepdims=True) - unit * inner)


def head_masks(shape):
    low = lax.broadcasted_iota(jnp.int32, shape, 1) < HEAD_DIM
    return (low, jnp.logical_not(low))


def add(*terms):
    total = terms[0].astype(F32)
    for term in terms[1:]:
        total = total + term.astype(F32)
    return total


class Net:
    def __init__(self, send, recv):
        self.send, self.recv, self.count, self.open = send, recv, 0, []
        self.s = lax.axis_index("shard")
        self.h, self.x = self.s // 4, lax.rem(self.s, 4)
        r = lax.axis_index("replica")
        self.core, self.y = lax.rem(r, 2), lax.rem(r // 2, 4)
        zlow = r // 8
        base = r - self.y * 2
        self.right = {"shard": self.at(self.h, self.x + 1)}
        self.left = {"shard": self.at(self.h, self.x + 3)}
        self.across = {"shard": self.at(1 - self.h, self.x)}
        self.twin = {"replica": r + 1 - 2 * self.core}
        self.up = {"replica": base + lax.rem(self.y + 1, 4) * 2}
        self.down = {"replica": base + lax.rem(self.y + 3, 4) * 2}
        self.facing = {"replica": base + lax.rem(self.y + 2, 4) * 2}
        self.beside = {"replica": r + 8 - 16 * zlow}
        self.peers = [{"shard": lax.rem(self.s + k, 8)} for k in range(1, 8)]

    def at(self, h, x):
        return h * 4 + lax.rem(x, 4)

    def copy(self, src, dst, to):
        i = self.count
        self.count += 1
        made = pltpu.make_async_remote_copy(
            src_ref=src,
            dst_ref=dst,
            send_sem=self.send.at[i],
            recv_sem=self.recv.at[i],
            device_id=to,
            device_id_type=MESH,
        )
        made.start()
        self.open.append(made)
        return made

    def drain(self):
        for made in self.open:
            made.wait_send()
        self.open = []

    def settle(self, copies):
        for made in copies:
            made.wait_send()
            self.open = [other for other in self.open if other is not made]

    def barrier(self, others):
        semaphore = pltpu.get_barrier_semaphore()
        for other in others:
            pl.semaphore_signal(semaphore, inc=1, device_id=other, device_id_type=MESH)
        pl.semaphore_wait(semaphore, len(others))


class Gather:
    def __init__(self, net, whole):
        self.net, self.whole = net, whole
        self.a = self.piece(net.s, 0, net.right)
        self.b = self.piece(net.s, 1, net.left)
        own = whole.at[net.s]
        self.z = net.copy(own, own, net.across)
        self.more = [self.piece(net.s, 1, net.right), self.piece(net.s, 0, net.left)]

    def piece(self, block, second, to):
        part = self.whole.at[block, :, pl.ds(second * HALF, HALF)]
        return self.net.copy(part, part, to)

    def relay_one(self):
        net = self.net
        self.a.wait_recv()
        self.c = self.piece(net.at(net.h, net.x + 3), 0, net.right)
        self.b.wait_recv()
        self.d = self.piece(net.at(net.h, net.x + 1), 1, net.left)

    def relay_two(self):
        net = self.net
        self.z.wait_recv()
        part = self.whole.at[net.at(1 - net.h, net.x)]
        self.rest = [net.copy(part, part, net.right), net.copy(part, part, net.left)]
        block = net.at(net.h, net.x + 2)
        self.c.wait_recv()
        self.rest.append(self.piece(block, 0, net.across))
        self.d.wait_recv()
        self.rest.append(self.piece(block, 1, net.across))

    def row(self):
        for made in self.more:
            made.wait_recv()

    def finish(self):
        for made in self.rest:
            made.wait_recv()


class Scatter:
    def __init__(self, net, part, hop, side, near, far, passed, kept, came):
        self.net, self.part, self.hop_in, self.side_in = net, part, hop, side
        self.near_in, self.far_in, self.passed, self.kept, self.came = near, far, passed, kept, came
        self.one, self.two = pl.ds(0, HALF), pl.ds(HALF, HALF)
        h, x = net.h, net.x
        self.own, self.facing = net.s, net.at(h, x + 2)
        self.right, self.left = net.at(h, x + 1), net.at(h, x + 3)
        self.other = [net.at(1 - h, x + k) for k in range(4)]

    def hop(self):
        self.hopped = self.net.copy(self.part.at[self.other[2]], self.hop_in, self.net.across)

    def side(self):
        net, part = self.net, self.part
        self.sides = [
            net.copy(part.at[self.other[1]], self.side_in.at[0], net.right),
            net.copy(part.at[self.other[3]], self.side_in.at[1], net.left),
        ]

    def near(self):
        net, part = self.net, self.part
        self.nears = [
            net.copy(part.at[self.right, :, self.two], self.near_in.at[0], net.right),
            net.copy(part.at[self.left, :, self.one], self.near_in.at[1], net.left),
        ]

    def far(self):
        net, hop = self.net, self.hop_in
        self.hopped.wait_recv()
        hop[...] = add(hop[...], self.part[self.facing]).astype(BF16)
        self.fars = [
            net.copy(hop.at[:, self.one], self.far_in.at[0], net.right),
            net.copy(hop.at[:, self.two], self.far_in.at[1], net.left),
        ]

    def over(self):
        for made in self.sides:
            made.wait_recv()
        self.kept[...] = add(
            self.part[self.other[0]], self.side_in[0], self.side_in[1]
        ).astype(BF16)
        self.crossed = self.net.copy(self.kept, self.came, self.net.across)

    def relay(self):
        net, part, far = self.net, self.part, self.far_in
        self.fars[0].wait_recv()
        far[0] = add(far[0], part[self.right, :, self.one]).astype(BF16)
        passes = [net.copy(far.at[0], self.passed.at[0], net.right)]
        self.fars[1].wait_recv()
        far[1] = add(far[1], part[self.left, :, self.two]).astype(BF16)
        passes.append(net.copy(far.at[1], self.passed.at[1], net.left))
        self.last = [*self.nears, *passes, self.crossed]

    def finish(self):
        for made in self.last:
            made.wait_recv()
        part, near, passed, came = self.part, self.near_in, self.passed, self.came
        one, two = self.one, self.two
        return jnp.concatenate(
            [
                add(part[self.own, :, one], passed[0], near[1], came[:, one]),
                add(part[self.own, :, two], passed[1], near[0], came[:, two]),
            ],
            axis=1,
        )


class Reduce:
    def __init__(self, net, grad, pair, ring, out, turned=None):
        self.net, self.grad, self.out, self.turned = net, grad, out, turned
        self.sent, self.work = pair
        self.near_in, self.far_in, self.passed, self.kept, self.came = ring
        width = grad.shape[-1]
        cut = max(width // 256, 1) * 128 if width != 384 else 256
        self.one, self.two = pl.ds(0, cut), pl.ds(cut, width - cut)
        self.mine = pl.ds(net.core * 4, 4)
        self.q = net.core * 4 + net.y
        self.at_up, self.at_facing, self.at_down = (lax.rem(net.y + k, 4) for k in (1, 2, 3))

    def core(self):
        net = self.net
        self.moved = net.copy(self.grad.at[pl.ds((1 - net.core) * 4, 4)], self.sent, net.twin)

    def ring(self):
        net, work, near, far = self.net, self.work, self.near_in, self.far_in
        one, two = self.one, self.two
        self.moved.wait_recv()
        work[...] = add(self.grad[self.mine], self.sent[...]).astype(BF16)
        self.fars = [
            net.copy(work.at[self.at_facing, :, one], far.at[:, one], net.up),
            net.copy(work.at[self.at_facing, :, two], far.at[:, two], net.down),
        ]
        self.nears = [
            net.copy(work.at[self.at_up, :, two], near.at[:, two], net.up),
            net.copy(work.at[self.at_down, :, one], near.at[:, one], net.down),
        ]

    def relay(self):
        net, far = self.net, self.far_in
        steps = ((self.one, self.at_up, net.up), (self.two, self.at_down, net.down))
        for k, (part, block, to) in enumerate(steps):
            self.fars[k].wait_recv()
            far[:, part] = add(far[:, part], self.work[block, :, part]).astype(BF16)
            self.nears.append(net.copy(far.at[:, part], self.passed.at[:, part], to))

    def beside(self):
        net = self.net
        for made in self.nears:
            made.wait_recv()
        self.kept[...] = add(self.work[net.y], self.near_in[...], self.passed[...]).astype(BF16)
        self.over = net.copy(self.kept, self.came, net.beside)

    def place(self, q, eighths=1):
        rows = self.out.shape[0] // 8
        return pl.ds(pl.multiple_of(q * rows, 16), rows * eighths)

    def cross(self):
        net = self.net
        self.over.wait_recv()
        total = add(self.kept[...], self.came[...]).astype(BF16)
        if self.turned is None:
            self.out[self.place(self.q)] = total
            return
        away, back = self.turned
        away[...] = total.reshape(away.shape)
        self.crossed = [
            net.copy(away.at[to["shard"]], back.at[net.s], to) for to in net.peers
        ]
        back[net.s] = away[net.s]

    def back(self):
        net, out = self.net, self.out
        own = self.place(self.q)
        if self.turned is not None:
            for made in self.crossed:
                made.wait_recv()
            incoming = self.turned[1]
            blocks = [incoming[t] for t in range(8)]
            width = blocks[0].shape[-1]
            for i in range(width // 128 if width == 384 else 1):
                size = 128 if width == 384 else width
                for t in range(8):
                    at = i * D + t * size
                    out[own, at : at + size] = blocks[t][:, i * 128 : i * 128 + size]
        part = out.at[own]
        self.shared = [net.copy(part, part, net.up), net.copy(part, part, net.down)]

    def back_relay(self):
        net, out = self.net, self.out
        half = out.shape[1] // 2
        self.lasts = []
        steps = ((0, self.at_down, net.up), (half, self.at_up, net.down))
        for k, (at, block, to) in enumerate(steps):
            self.shared[k].wait_recv()
            part = out.at[self.place(net.core * 4 + block), pl.ds(at, half)]
            self.lasts.append(net.copy(part, part, to))

    def swap(self):
        for made in self.lasts:
            made.wait_recv()
        part = self.out.at[self.place(self.net.core * 4, 4)]
        self.ended = self.net.copy(part, part, self.net.twin)

    def end(self):
        self.ended.wait_recv()


def layer_kernel(
    tokens,
    cotangent,
    vectors,
    qkv_weight,
    up_weight,
    out_weight,
    down_weight,
    qkv_bias,
    up_bias,
    block_out,
    input_grad,
    down_sum,
    out_sum,
    up_sum,
    qkv_sum,
    small_sum,
    down_grad,
    out_grad,
    up_grad,
    qkv_grad,
    all_vectors,
    columns,
    first,
    cot,
    second,
    branch,
    mixed,
    qkv_low,
    heads,
    lse,
    attended,
    active,
    grad_upper,
    grad_qkv,
    resid_ref,
    grad_resid_ref,
    small,
    fours,
    fours_in,
    parts,
    hop,
    side,
    near,
    far,
    passed,
    kept,
    came,
    small_low,
    small_twin,
    small_ring,
    small_away,
    small_came,
    down_pair,
    down_ring,
    out_pair,
    out_ring,
    up_pair,
    up_ring,
    up_turned,
    qkv_pair,
    qkv_ring,
    qkv_turned,
    send,
    recv,
):
    net = Net(send, recv)
    s, core = net.s, net.core
    net.barrier([*net.peers, net.twin, net.up, net.down, net.facing, net.beside])

    def reduce(grad, pair, ring, out, turned=None):
        split = lambda ref, n: [ref.at[i] for i in range(n)]
        turned = None if turned is None else split(turned, 2)
        return Reduce(net, grad, split(pair, 2), split(ring, 5), out, turned)

    down_all = reduce(down_grad, down_pair, down_ring, down_sum)
    out_all = reduce(out_grad, out_pair, out_ring, out_sum)
    up_all = reduce(up_grad, up_pair, up_ring, up_sum, up_turned)
    qkv_all = reduce(qkv_grad, qkv_pair, qkv_ring, qkv_sum, qkv_turned)
    source = [lax.rem(s + 8 - k, 8) for k in range(1, 8)]
    mine = pl.ds(pl.multiple_of(core * 64, 64), 64)

    def scatter(i):
        buffers = (hop, side, near, far, passed, kept, came)
        return Scatter(net, parts.at[i % 3], *(buffer.at[i] for buffer in buffers))

    def each(work, least, end, carry=0):
        def step(i, carry):
            row, j = i // 4, lax.rem(i, 4)
            same = j + j // 2 - 2 * (j // 3)
            cross = lax.rem(2 * j, 3) + 3 * (j // 3)
            h = net.h + row - 2 * net.h * row
            return work(net.at(h, net.x + (1 - row) * same + row * cross), carry)

        return lax.fori_loop(least, end, step, carry)

    def each_sent(rs, work, carry):
        carry = each(work, 5, 6, carry)
        rs.hop()
        carry = each(work, 6, 8, carry)
        rs.side()
        carry = each(work, 1, 3, carry)
        rs.near()
        carry = each(work, 3, 5, carry)
        rs.far()
        return each(work, 0, 1, carry)

    vec = [net.copy(vectors, all_vectors.at[s], to) for to in net.peers]
    all_vectors[s] = vectors[...]
    qkv_in, up_in = [], []
    for k, to in enumerate(net.peers):
        t = to["shard"]
        qkv_in.append(
            [
                net.copy(
                    qkv_weight.at[mine, pl.ds(pl.multiple_of(i * D + t * 128, 128), 128)],
                    columns.at[s, mine, pl.ds(i * 128, 128)],
                    to,
                )
                for i in range(3)
            ]
        )
    for i in range(3):
        columns[s, :, i * 128 : (i + 1) * 128] = qkv_weight[
            :, pl.ds(pl.multiple_of(i * D + s * 128, 128), 128)
        ]
    columns[s, :, 384:896] = up_weight[:, pl.ds(pl.multiple_of(s * 512, 512), 512)]
    cot[s] = cotangent[...]
    x = tokens[...].astype(F32)
    unit1, inverse1 = norm_unit(x)
    for made in vec:
        made.wait_recv()
    table = [all_vectors[j].astype(F32) for j in range(8)]
    gain1, shift1, gain2, shift2, bias_out, bias_down = (
        jnp.concatenate([t[i : i + 1] for t in table], axis=1) for i in range(6)
    )
    first[s] = (unit1 * gain1 + shift1).astype(BF16)
    ag = Gather(net, first)
    qkv_pass = []
    for k in range(7):
        for made in qkv_in[k]:
            made.wait_recv()
        block = columns.at[source[k], mine, pl.ds(0, 384)]
        qkv_pass.append(net.copy(block, block, net.twin))
    ag.relay_one()
    ag.relay_two()
    for k, to in enumerate(net.peers):
        up_in.append(
            net.copy(
                up_weight.at[mine, pl.ds(pl.multiple_of(to["shard"] * 512, 512), 512)],
                columns.at[s, mine, pl.ds(384, 512)],
                to,
            )
        )
    for made in qkv_pass:
        made.wait_recv()
    ag.row()

    def project(b, carry):
        value = dot(first[b], columns[:, :, 0:384].reshape(D, 384)) + qkv_bias[...]
        at = pl.multiple_of(b * 72, 8)
        mixed[0, pl.ds(at, 72), :] = value[0:72]
        mixed[1, pl.ds(at, 72), :] = value[72:144]
        return carry

    each(project, 0, 5)
    ag.finish()
    ag_cot = Gather(net, cot)
    each(project, 5, 8)
    qkv_low[...] = mixed[...].astype(BF16)
    ag_cot.relay_one()

    def attend(image, carry):
        q, k, v = (qkv_low[image, :, i * 128 : (i + 1) * 128] for i in range(3))
        zero = jnp.zeros_like(q)
        total = jnp.zeros(q.shape, F32)
        for h, mask in enumerate(head_masks(q.shape)):
            score = dot_last(jnp.where(mask, q, zero), k) * SCALE
            top = jnp.max(score, -1, keepdims=True)
            e = jnp.exp(score - top)
            row = jnp.sum(e, -1, keepdims=True)
            p = (e * (1.0 / row)).astype(BF16)
            total += dot(p, jnp.where(mask, v, zero))
            lse[image, :, h : h + 1] = top + jnp.log(row)
        heads[image] = total
        return carry

    lax.fori_loop(0, 2, attend, 0)
    ag_cot.relay_two()
    up_pass = []
    for k in range(7):
        up_in[k].wait_recv()
        block = columns.at[source[k], mine, pl.ds(384, 512)]
        up_pass.append(net.copy(block, block, net.twin))

    def by_device(ref, b):
        at = pl.multiple_of(b * 72, 8)
        both = [ref[i, pl.ds(at, 72), :] for i in range(2)]
        return jnp.concatenate(both, axis=0).astype(BF16)

    def outward(b, carry):
        value = by_device(heads, b)
        attended[b] = value
        parts[0, b] = dot(value, out_weight[...]).astype(BF16)
        return carry

    rs = rs_branch = scatter(0)
    each_sent(rs, outward, 0)
    rs.over()
    rs.relay()
    resid = tokens[...].astype(F32) + (rs.finish() + bias_out)
    resid_ref[...] = resid
    unit2, inverse2 = norm_unit(resid)
    second[s] = (unit2 * gain2 + shift2).astype(BF16)
    ag = Gather(net, second)
    ag_cot.row()
    ag_cot.finish()
    for made in up_pass:
        made.wait_recv()

    def feed(b, total):
        up = columns[:, :, 384:896].reshape(D, 512)
        u = dot(second[b], up) + up_bias[...]
        square = u * u
        t = jnp.tanh(GELU * (u + 0.044715 * u * square))
        act = (0.5 * u * (1.0 + t)).astype(BF16)
        slope = 0.5 * (1.0 + t) + (0.5 * GELU) * u * (1.0 - t * t) * (
            1.0 + 0.134145 * square
        )
        active[b] = act
        gu = (dot_last(cot[b], down_weight[...]) * slope).astype(BF16)
        grad_upper[b] = gu
        parts[1, b] = dot_last(gu, up).astype(BF16)
        parts[2, b] = dot(act, down_weight[...]).astype(BF16)
        return total + jnp.sum(gu.astype(F32), 0, keepdims=True)

    ag.relay_one()
    up_bias_grad = each(feed, 0, 1, jnp.zeros((1, 512), F32))
    ag.relay_two()
    ag.row()
    up_bias_grad = each(feed, 1, 5, up_bias_grad)
    ag.finish()
    rs = scatter(1)
    up_bias_grad = each(feed, 5, 6, up_bias_grad)
    rs.hop()
    up_bias_grad = each(feed, 6, 8, up_bias_grad)
    rs.side()
    rs.near()
    own = pl.ds(pl.multiple_of(s * 128, 128), 128)
    small[...] = jnp.zeros_like(small)
    for i in range(4):
        small[8 + i : 9 + i, :] = up_bias_grad[:, i * 128 : (i + 1) * 128]
    small[7:8, :] = jnp.sum(cot[:, :, own].astype(F32).reshape(1152, 128), 0, keepdims=True)

    def down_tile(i):
        at = pl.ds(i * 256, 256)
        value = dot_first(
            active[...].reshape(1152, 512), cot[:, :, at].reshape(1152, 256)
        ).astype(BF16)
        for q in range(8):
            down_grad[q, :, at] = value[q * 64 : (q + 1) * 64]

    down_tile(0)
    rs.far()
    down_tile(1)
    rs.over()
    rs.relay()
    down_tile(2)
    down_tile(3)
    down_all.core()
    grad_second = rs.finish()
    unit2, inverse2 = norm_unit(resid_ref[...])
    grad_resid = cotangent[...].astype(F32) + norm_back(grad_second, unit2, inverse2, gain2)
    grad_resid_ref[...] = grad_resid
    branch[s] = grad_resid.astype(BF16)
    ag = Gather(net, branch)
    gain2_grad = jnp.sum(grad_second * unit2, 0, keepdims=True)
    shift2_grad = jnp.sum(grad_second, 0, keepdims=True)

    def up_tile(i):
        value = dot_first(
            second[:, :, i * 256 : (i + 1) * 256].reshape(1152, 256),
            grad_upper[...].reshape(1152, 512),
        ).astype(BF16)
        for j in range(2):
            for q in range(8):
                up_grad[q, (2 * i + j) * 16 : (2 * i + j + 1) * 16, :] = value[
                    j * 128 + q * 16 : j * 128 + (q + 1) * 16
                ]

    ag.relay_one()
    down_all.ring()
    up_tile(0)
    ag.relay_two()
    ag.row()
    up_tile(1)
    down_all.relay()
    up_tile(2)
    ag.finish()
    rs_out = scatter(2)
    rs_out.hop()
    rs_out.side()
    rs_out.near()
    down_all.beside()

    def back_heads(b, carry):
        value = dot_last(branch[b], out_weight[...])
        at = pl.multiple_of(b * 72, 8)
        heads[0, pl.ds(at, 72), :] = value[0:72]
        heads[1, pl.ds(at, 72), :] = value[72:144]
        return carry

    each(back_heads, 0, 8)
    up_tile(3)
    value = dot_first(attended[...].reshape(1152, 128), branch[...].reshape(1152, D)).astype(BF16)
    for q in range(8):
        out_grad[q] = value[q * 16 : (q + 1) * 16]
    rs_out.far()
    up_all.core()
    out_all.core()
    down_all.cross()
    down_all.back()

    def attend_back(image, carry):
        q, k, v = (qkv_low[image, :, i * 128 : (i + 1) * 128] for i in range(3))
        grad = heads[image].astype(BF16)
        zero = jnp.zeros_like(q)
        dq = jnp.zeros(q.shape, F32)
        dk, dv = dq, dq
        for h, mask in enumerate(head_masks(q.shape)):
            qh, kh, gh = (jnp.where(mask, a, zero) for a in (q, k, grad))
            p = jnp.exp(dot_last(qh, k) * SCALE - lse[image, :, h : h + 1])
            dp = dot_last(gh, v)
            inner = jnp.sum(p * dp, -1, keepdims=True)
            ds = (p * (dp - inner)).astype(BF16)
            dq += dot(ds, kh)
            dk += dot_first(ds, qh)
            dv += dot_first(p.astype(BF16), gh)
        mixed[image, :, 0:128] = dq * SCALE
        mixed[image, :, 128:256] = dk * SCALE
        mixed[image, :, 256:384] = dv
        return carry

    lax.fori_loop(0, 1, attend_back, 0)
    up_all.ring()
    out_all.ring()
    rs_out.over()
    lax.fori_loop(1, 2, attend_back, 0)
    rs_out.relay()
    down_all.back_relay()
    up_all.relay()
    out_all.relay()

    def back_first(b, total):
        value = by_device(mixed, b)
        grad_qkv[b] = value
        parts[0, b] = dot_last(value, columns[:, :, 0:384].reshape(D, 384)).astype(BF16)
        return total + jnp.sum(value.astype(F32), 0, keepdims=True)

    net.settle([rs_branch.hopped, *rs_branch.sides, *rs_branch.nears])
    rs = scatter(3)
    qkv_bias_grad = each_sent(rs, back_first, jnp.zeros((1, 384), F32))
    small[4:5, :] = qkv_bias_grad[:, 0:128]
    small[5:6, :] = qkv_bias_grad[:, 256:384]
    small[6:7, :] = jnp.sum(branch[:, :, own].astype(F32).reshape(1152, 128), 0, keepdims=True)

    def qkv_tile(i):
        value = dot_first(
            first[:, :, i * 256 : (i + 1) * 256].reshape(1152, 256),
            grad_qkv[...].reshape(1152, 384),
        ).astype(BF16)
        for j in range(2):
            for q in range(8):
                qkv_grad[q, (2 * i + j) * 16 : (2 * i + j + 1) * 16, :] = value[
                    j * 128 + q * 16 : j * 128 + (q + 1) * 16
                ]

    qkv_tile(0)
    up_all.beside()
    out_all.beside()
    qkv_tile(1)
    rs.over()
    qkv_tile(2)
    down_all.swap()
    qkv_tile(3)
    qkv_all.core()
    rs.relay()
    block_out[...] = (resid_ref[...] + (rs_out.finish() + bias_down)).astype(BF16)
    qkv_all.ring()
    up_all.cross()
    out_all.cross()
    out_all.back()
    qkv_all.relay()
    up_all.back()
    out_all.back_relay()
    qkv_all.beside()
    grad_first = rs.finish()
    unit1, inverse1 = norm_unit(tokens[...].astype(F32))
    input_grad[...] = (
        grad_resid_ref[...] + norm_back(grad_first, unit1, inverse1, gain1)
    ).astype(BF16)
    gain1_grad = jnp.sum(grad_first * unit1, 0, keepdims=True)
    shift1_grad = jnp.sum(grad_first, 0, keepdims=True)
    four = jnp.concatenate(
        [gain1_grad, shift1_grad, gain2_grad, shift2_grad, jnp.zeros((12, D), F32)], axis=0
    ).astype(BF16)
    for t in range(8):
        fours[t] = four[:, t * 128 : (t + 1) * 128]
    moved = [net.copy(fours.at[to["shard"]], fours_in.at[s], to) for to in net.peers]
    fours_in[s] = fours[s]
    qkv_all.cross()
    up_all.back_relay()
    out_all.swap()
    for made in moved:
        made.wait_recv()
    total = jnp.sum(fours_in[...].astype(F32), 0)
    small[0:4, :] = total[0:4]
    small_low[...] = small[...].astype(BF16)
    moved = net.copy(small_low, small_twin, net.twin)
    qkv_all.back()
    moved.wait_recv()
    small_ring[net.y] = add(small_low[...], small_twin[...]).astype(BF16)
    own = small_ring.at[net.y]
    moved = [net.copy(own, own, to) for to in (net.up, net.down, net.facing)]
    up_all.swap()
    qkv_all.back_relay()
    for made in moved:
        made.wait_recv()
    small_away[...] = add(*(small_ring[k] for k in range(4))).astype(BF16)
    moved = net.copy(small_away, small_came, net.beside)
    qkv_all.swap()
    moved.wait_recv()
    small_sum[...] = add(small_away[...], small_came[...]).astype(BF16)
    for every in (down_all, out_all, up_all, qkv_all):
        every.end()
    net.drain()


def layer(*arguments):
    vmem = lambda *shape: pltpu.VMEM(shape, BF16)
    wide = lambda *shape: pltpu.VMEM(shape, F32)
    space = pl.BlockSpec(memory_space=pltpu.VMEM)
    shape = lambda *sizes: jax.ShapeDtypeStruct(sizes, BF16)
    return pl.pallas_call(
        layer_kernel,
        out_shape=[
            shape(ROWS, D),
            shape(ROWS, D),
            shape(512, D),
            shape(128, D),
            shape(128, 4096),
            shape(128, 3 * D),
            shape(16, 128),
        ],
        in_specs=[space] * 9,
        out_specs=[space] * 7,
        scratch_shapes=[
            vmem(8, 64, D),
            vmem(8, 16, D),
            vmem(8, 128, 512),
            vmem(8, 128, 384),
            vmem(8, 16, 128),
            vmem(8, 128, 896),
            vmem(8, ROWS, D),
            vmem(8, ROWS, D),
            vmem(8, ROWS, D),
            vmem(8, ROWS, D),
            wide(2, 576, 384),
            vmem(2, 576, 384),
            wide(2, 576, 128),
            wide(2, 576, 128),
            vmem(8, ROWS, 128),
            vmem(8, ROWS, 512),
            vmem(8, ROWS, 512),
            vmem(8, ROWS, 384),
            wide(ROWS, D),
            wide(ROWS, D),
            wide(16, 128),
            vmem(8, 16, 128),
            vmem(8, 16, 128),
            vmem(3, 8, ROWS, D),
            vmem(4, ROWS, D),
            vmem(4, 2, ROWS, D),
            vmem(4, 2, ROWS, HALF),
            vmem(4, 2, ROWS, HALF),
            vmem(4, 2, ROWS, HALF),
            vmem(4, ROWS, D),
            vmem(4, ROWS, D),
            vmem(16, 128),
            vmem(16, 128),
            vmem(4, 16, 128),
            vmem(16, 128),
            vmem(16, 128),
            vmem(2, 4, 64, D),
            vmem(5, 64, D),
            vmem(2, 4, 16, D),
            vmem(5, 16, D),
            vmem(2, 4, 128, 512),
            vmem(5, 128, 512),
            vmem(2, 8, 16, 512),
            vmem(2, 4, 128, 384),
            vmem(5, 128, 384),
            vmem(2, 8, 16, 384),
            pltpu.SemaphoreType.DMA((240,)),
            pltpu.SemaphoreType.DMA((240,)),
        ],
        name="layer",
        cost_estimate=pl.CostEstimate(
            flops=11 * 10**9, bytes_accessed=12 * 10**6, transcendentals=0
        ),
        compiler_params=pltpu.CompilerParams(
            collective_id=1, has_side_effects=True, vmem_limit_bytes=62 << 20
        ),
    )(*arguments)


def body(
    tokens,
    cotangent,
    attn_gain,
    attn_shift,
    qkv_weight,
    query_bias,
    value_bias,
    out_weight,
    out_bias,
    mlp_gain,
    mlp_shift,
    up_weight,
    up_bias,
    down_weight,
    down_bias,
):
    vectors = jnp.stack([attn_gain, attn_shift, mlp_gain, mlp_shift, out_bias, down_bias])
    vectors = jnp.pad(vectors, ((0, 10), (0, 0)))
    zeros = jnp.zeros((128,), F32)
    qkv_bias = jnp.concatenate([query_bias.astype(F32), zeros, value_bias.astype(F32)])
    block_out, input_grad, *sums = layer(
        tokens.reshape(ROWS, D),
        cotangent.reshape(ROWS, D),
        vectors,
        qkv_weight,
        up_weight,
        out_weight,
        down_weight,
        qkv_bias.reshape(1, 384),
        up_bias.astype(F32).reshape(1, 512),
    )
    down_grad, out_grad, up_grad, qkv_grad, small = (a.astype(F32) for a in sums)
    return (
        block_out.reshape(2, 72, D),
        input_grad.reshape(2, 72, D),
        small[0],
        small[1],
        qkv_grad,
        small[4],
        small[5],
        out_grad,
        small[6],
        small[2],
        small[3],
        up_grad,
        small[8:12].reshape(512),
        down_grad,
        small[7],
    )


def solution(mesh):
    row, cube, flat = P("shard"), P("replica", "shard", None), P("shard", None)
    return jax.shard_map(
        body,
        mesh=mesh,
        in_specs=(cube, cube, row, row, flat, row, row, flat, row, row, row, flat, row, flat, row),
        out_specs=(cube, cube, row, row, flat, row, row, flat, row, row, row, flat, row, flat, row),
        check_vma=False,
    )
```

```python
import jax
import jax.numpy as jnp
from jax import lax
from jax.experimental import pallas as pl
from jax.experimental.pallas import tpu as pltpu
from jax.sharding import PartitionSpec as P

HEAD_DIM = 64
EPS = 1e-06
F32 = jnp.float32
BF16 = jnp.bfloat16
SCALE = HEAD_DIM ** (-0.5)
MESH = pl.DeviceIdType.MESH
D = 1024
ROWS = 144
HALF = 512
GELU = 0.7978845608028654


def dot(a, b):
    return lax.dot_general(a, b, (((1,), (0,)), ((), ())), preferred_element_type=F32)


def dot_last(a, b):
    return lax.dot_general(a, b, (((1,), (1,)), ((), ())), preferred_element_type=F32)


def dot_first(a, b):
    return lax.dot_general(a, b, (((0,), (0,)), ((), ())), preferred_element_type=F32)


def norm_unit(v):
    mean = jnp.mean(v, -1, keepdims=True)
    centred = v - mean
    inverse = lax.rsqrt(jnp.mean(centred * centred, -1, keepdims=True) + EPS)
    return centred * inverse, inverse


def norm_back(grad, unit, inverse, gain):
    gn = grad * gain
    inner = jnp.mean(gn * unit, -1, keepdims=True)
    return inverse * (gn - jnp.mean(gn, -1, keepdims=True) - unit * inner)


def head_masks(shape):
    low = lax.broadcasted_iota(jnp.int32, shape, 1) < HEAD_DIM
    return (low, jnp.logical_not(low))


def add(*terms):
    total = terms[0].astype(F32)
    for term in terms[1:]:
        total = total + term.astype(F32)
    return total


class Net:
    def __init__(self, send, recv):
        self.send, self.recv, self.count, self.open = send, recv, 0, []
        self.s = lax.axis_index("shard")
        self.h, self.x = self.s // 4, lax.rem(self.s, 4)
        r = lax.axis_index("replica")
        self.core, self.y = lax.rem(r, 2), lax.rem(r // 2, 4)
        zlow = r // 8
        base = r - self.y * 2
        self.right = {"shard": self.at(self.h, self.x + 1)}
        self.left = {"shard": self.at(self.h, self.x + 3)}
        self.across = {"shard": self.at(1 - self.h, self.x)}
        self.twin = {"replica": r + 1 - 2 * self.core}
        self.up = {"replica": base + lax.rem(self.y + 1, 4) * 2}
        self.down = {"replica": base + lax.rem(self.y + 3, 4) * 2}
        self.facing = {"replica": base + lax.rem(self.y + 2, 4) * 2}
        self.beside = {"replica": r + 8 - 16 * zlow}
        self.replicas = [{"replica": lax.rem(r + k, 16)} for k in range(1, 16)]
        self.r = r
        self.peers = [{"shard": lax.rem(self.s + k, 8)} for k in range(1, 8)]

    def at(self, h, x):
        return h * 4 + lax.rem(x, 4)

    def copy(self, src, dst, to):
        i = self.count
        self.count += 1
        made = pltpu.make_async_remote_copy(
            src_ref=src,
            dst_ref=dst,
            send_sem=self.send.at[i],
            recv_sem=self.recv.at[i],
            device_id=to,
            device_id_type=MESH,
        )
        made.start()
        self.open.append(made)
        return made

    def drain(self):
        for made in self.open:
            made.wait_send()
        self.open = []

    def settle(self, copies):
        for made in copies:
            made.wait_send()
            self.open = [other for other in self.open if other is not made]

    def barrier(self, others):
        semaphore = pltpu.get_barrier_semaphore()
        for other in others:
            pl.semaphore_signal(semaphore, inc=1, device_id=other, device_id_type=MESH)
        pl.semaphore_wait(semaphore, len(others))


class Gather:
    def __init__(self, net, whole):
        self.net, self.whole = net, whole
        self.a = self.piece(net.s, 0, net.right)
        self.b = self.piece(net.s, 1, net.left)
        own = whole.at[net.s]
        self.z = net.copy(own, own, net.across)
        self.more = [self.piece(net.s, 1, net.right), self.piece(net.s, 0, net.left)]

    def piece(self, block, second, to):
        part = self.whole.at[block, :, pl.ds(second * HALF, HALF)]
        return self.net.copy(part, part, to)

    def relay_one(self):
        net = self.net
        self.a.wait_recv()
        self.c = self.piece(net.at(net.h, net.x + 3), 0, net.right)
        self.b.wait_recv()
        self.d = self.piece(net.at(net.h, net.x + 1), 1, net.left)

    def relay_two(self):
        net = self.net
        self.z.wait_recv()
        part = self.whole.at[net.at(1 - net.h, net.x)]
        self.rest = [net.copy(part, part, net.right), net.copy(part, part, net.left)]
        block = net.at(net.h, net.x + 2)
        self.c.wait_recv()
        self.rest.append(self.piece(block, 0, net.across))
        self.d.wait_recv()
        self.rest.append(self.piece(block, 1, net.across))

    def row(self):
        for made in self.more:
            made.wait_recv()

    def finish(self):
        for made in self.rest:
            made.wait_recv()


class Scatter:
    def __init__(self, net, part, hop, side, near, far, passed, kept, came):
        self.net, self.part, self.hop_in, self.side_in = net, part, hop, side
        self.near_in, self.far_in, self.passed, self.kept, self.came = near, far, passed, kept, came
        self.one, self.two = pl.ds(0, HALF), pl.ds(HALF, HALF)
        h, x = net.h, net.x
        self.own, self.facing = net.s, net.at(h, x + 2)
        self.right, self.left = net.at(h, x + 1), net.at(h, x + 3)
        self.other = [net.at(1 - h, x + k) for k in range(4)]

    def hop(self):
        self.hopped = self.net.copy(self.part.at[self.other[2]], self.hop_in, self.net.across)

    def side(self):
        net, part = self.net, self.part
        self.sides = [
            net.copy(part.at[self.other[1]], self.side_in.at[0], net.right),
            net.copy(part.at[self.other[3]], self.side_in.at[1], net.left),
        ]

    def near(self):
        net, part = self.net, self.part
        self.nears = [
            net.copy(part.at[self.right, :, self.two], self.near_in.at[0], net.right),
            net.copy(part.at[self.left, :, self.one], self.near_in.at[1], net.left),
        ]

    def far(self):
        net, hop = self.net, self.hop_in
        self.hopped.wait_recv()
        hop[...] = add(hop[...], self.part[self.facing]).astype(BF16)
        self.fars = [
            net.copy(hop.at[:, self.one], self.far_in.at[0], net.right),
            net.copy(hop.at[:, self.two], self.far_in.at[1], net.left),
        ]

    def over(self):
        for made in self.sides:
            made.wait_recv()
        self.kept[...] = add(
            self.part[self.other[0]], self.side_in[0], self.side_in[1]
        ).astype(BF16)
        self.crossed = self.net.copy(self.kept, self.came, self.net.across)

    def relay(self):
        net, part, far = self.net, self.part, self.far_in
        self.fars[0].wait_recv()
        far[0] = add(far[0], part[self.right, :, self.one]).astype(BF16)
        passes = [net.copy(far.at[0], self.passed.at[0], net.right)]
        self.fars[1].wait_recv()
        far[1] = add(far[1], part[self.left, :, self.two]).astype(BF16)
        passes.append(net.copy(far.at[1], self.passed.at[1], net.left))
        self.last = [*self.nears, *passes, self.crossed]

    def finish(self):
        for made in self.last:
            made.wait_recv()
        part, near, passed, came = self.part, self.near_in, self.passed, self.came
        one, two = self.one, self.two
        return jnp.concatenate(
            [
                add(part[self.own, :, one], passed[0], near[1], came[:, one]),
                add(part[self.own, :, two], passed[1], near[0], came[:, two]),
            ],
            axis=1,
        )


class Reduce:
    def __init__(self, net, grad, pair, ring, out, turned=None):
        self.net, self.grad, self.out, self.turned = net, grad, out, turned
        self.sent, self.work = pair
        self.near_in, self.far_in, self.passed, self.kept, self.came = ring
        width = grad.shape[-1]
        cut = max(width // 256, 1) * 128 if width != 384 else 256
        self.one, self.two = pl.ds(0, cut), pl.ds(cut, width - cut)
        self.mine = pl.ds(net.core * 4, 4)
        self.q = net.core * 4 + net.y
        self.at_up, self.at_facing, self.at_down = (lax.rem(net.y + k, 4) for k in (1, 2, 3))

    def core(self):
        net = self.net
        self.moved = net.copy(self.grad.at[pl.ds((1 - net.core) * 4, 4)], self.sent, net.twin)

    def ring(self):
        net, work, near, far = self.net, self.work, self.near_in, self.far_in
        one, two = self.one, self.two
        self.moved.wait_recv()
        work[...] = add(self.grad[self.mine], self.sent[...]).astype(BF16)
        self.fars = [
            net.copy(work.at[self.at_facing, :, one], far.at[:, one], net.up),
            net.copy(work.at[self.at_facing, :, two], far.at[:, two], net.down),
        ]
        self.nears = [
            net.copy(work.at[self.at_up, :, two], near.at[:, two], net.up),
            net.copy(work.at[self.at_down, :, one], near.at[:, one], net.down),
        ]

    def relay(self):
        net, far = self.net, self.far_in
        steps = ((self.one, self.at_up, net.up), (self.two, self.at_down, net.down))
        for k, (part, block, to) in enumerate(steps):
            self.fars[k].wait_recv()
            far[:, part] = add(far[:, part], self.work[block, :, part]).astype(BF16)
            self.nears.append(net.copy(far.at[:, part], self.passed.at[:, part], to))

    def beside(self):
        net = self.net
        for made in self.nears:
            made.wait_recv()
        self.kept[...] = add(self.work[net.y], self.near_in[...], self.passed[...]).astype(BF16)
        self.over = net.copy(self.kept, self.came, net.beside)

    def place(self, q, eighths=1):
        rows = self.out.shape[0] // 8
        return pl.ds(pl.multiple_of(q * rows, 16), rows * eighths)

    def cross(self):
        net = self.net
        self.over.wait_recv()
        total = add(self.kept[...], self.came[...]).astype(BF16)
        if self.turned is None:
            self.out[self.place(self.q)] = total
            return
        away, back = self.turned
        away[...] = total.reshape(away.shape)
        self.crossed = [
            net.copy(away.at[to["shard"]], back.at[net.s], to) for to in net.peers
        ]
        back[net.s] = away[net.s]

    def back(self):
        net, out = self.net, self.out
        own = self.place(self.q)
        if self.turned is not None:
            for made in self.crossed:
                made.wait_recv()
            incoming = self.turned[1]
            blocks = [incoming[t] for t in range(8)]
            width = blocks[0].shape[-1]
            for i in range(width // 128 if width == 384 else 1):
                size = 128 if width == 384 else width
                for t in range(8):
                    at = i * D + t * size
                    out[own, at : at + size] = blocks[t][:, i * 128 : i * 128 + size]
        part = out.at[own]
        self.shared = [net.copy(part, part, net.up), net.copy(part, part, net.down)]

    def back_relay(self):
        net, out = self.net, self.out
        half = out.shape[1] // 2
        self.lasts = []
        steps = ((0, self.at_down, net.up), (half, self.at_up, net.down))
        for k, (at, block, to) in enumerate(steps):
            self.shared[k].wait_recv()
            part = out.at[self.place(net.core * 4 + block), pl.ds(at, half)]
            self.lasts.append(net.copy(part, part, to))

    def swap(self):
        for made in self.lasts:
            made.wait_recv()
        part = self.out.at[self.place(self.net.core * 4, 4)]
        self.ended = self.net.copy(part, part, self.net.twin)

    def end(self):
        self.ended.wait_recv()


def layer_kernel(
    tokens,
    cotangent,
    vectors,
    qkv_weight,
    up_weight,
    out_weight,
    down_weight,
    block_out,
    input_grad,
    down_sum,
    out_sum,
    up_sum,
    qkv_sum,
    small_sum,
    down_grad,
    out_grad,
    up_grad,
    qkv_grad,
    all_vectors,
    columns,
    first,
    cot,
    second,
    branch,
    mixed,
    qkv_low,
    heads,
    lse,
    attended,
    active,
    grad_upper,
    grad_qkv,
    resid_ref,
    grad_resid_ref,
    small,
    fours,
    fours_in,
    parts,
    hop,
    side,
    near,
    far,
    passed,
    kept,
    came,
    small_low,
    small_ring,
    down_pair,
    down_ring,
    out_pair,
    out_ring,
    up_pair,
    up_ring,
    up_turned,
    qkv_pair,
    qkv_ring,
    qkv_turned,
    send,
    recv,
):
    net = Net(send, recv)
    s, core = net.s, net.core
    net.barrier([*net.peers, *net.replicas])

    def reduce(grad, pair, ring, out, turned=None):
        split = lambda ref, n: [ref.at[i] for i in range(n)]
        turned = None if turned is None else split(turned, 2)
        return Reduce(net, grad, split(pair, 2), split(ring, 5), out, turned)

    down_all = reduce(down_grad, down_pair, down_ring, down_sum)
    out_all = reduce(out_grad, out_pair, out_ring, out_sum)
    up_all = reduce(up_grad, up_pair, up_ring, up_sum, up_turned)
    qkv_all = reduce(qkv_grad, qkv_pair, qkv_ring, qkv_sum, qkv_turned)
    mine = pl.ds(pl.multiple_of(core * 64, 64), 64)
    sixteen = pl.ds(pl.multiple_of(core * 64 + net.y * 16, 16), 16)

    def scatter(i):
        buffers = (hop, side, near, far, passed, kept, came)
        return Scatter(net, parts.at[i % 3], *(buffer.at[i] for buffer in buffers))

    def each(work, least, end, carry=0):
        def step(i, carry):
            row, j = i // 4, lax.rem(i, 4)
            same = j + j // 2 - 2 * (j // 3)
            cross = lax.rem(2 * j, 3) + 3 * (j // 3)
            h = net.h + row - 2 * net.h * row
            return work(net.at(h, net.x + (1 - row) * same + row * cross), carry)

        return lax.fori_loop(least, end, step, carry)

    def each_sent(rs, work, carry):
        carry = each(work, 5, 6, carry)
        rs.hop()
        carry = each(work, 6, 8, carry)
        rs.side()
        carry = each(work, 1, 3, carry)
        rs.near()
        carry = each(work, 3, 5, carry)
        rs.far()
        return each(work, 0, 1, carry)

    vec = [net.copy(vectors, all_vectors.at[s], to) for to in net.peers]
    all_vectors[s] = vectors[...]
    qkv_in, up_in = [], []
    thirds = [
        lambda t, i=i: qkv_weight.at[sixteen, pl.ds(pl.multiple_of(i * D + t * 128, 128), 128)]
        for i in range(3)
    ]
    quarter = lambda t: up_weight.at[sixteen, pl.ds(pl.multiple_of(t * 512, 512), 512)]
    for to in net.peers:
        for i in range(3):
            there = columns.at[s, sixteen, pl.ds(i * 128, 128)]
            qkv_in.append(net.copy(thirds[i](to["shard"]), there, to))
    for to in net.peers:
        there = columns.at[s, sixteen, pl.ds(384, 512)]
        up_in.append(net.copy(quarter(to["shard"]), there, to))
    for i in range(3):
        columns[s, sixteen, i * 128 : (i + 1) * 128] = thirds[i](s)[...]
    columns[s, sixteen, 384:896] = quarter(s)[...]

    def share(arrived, at):
        for made in arrived:
            made.wait_recv()
        part = columns.at[:, sixteen, at]
        return [net.copy(part, part, to) for to in (net.up, net.down, net.facing)]

    def share_twin(arrived, at):
        for made in arrived:
            made.wait_recv()
        part = columns.at[:, mine, at]
        return net.copy(part, part, net.twin)

    cot[s] = cotangent[...]
    x = tokens[...].astype(F32)
    unit1, inverse1 = norm_unit(x)
    for made in vec:
        made.wait_recv()
    table = [all_vectors[j].astype(F32) for j in range(8)]
    gain1, shift1, gain2, shift2, bias_out, bias_down = (
        jnp.concatenate([t[i : i + 1] for t in table], axis=1) for i in range(6)
    )
    first[s] = (unit1 * gain1 + shift1).astype(BF16)
    ag = Gather(net, first)
    qkv_at, up_at = pl.ds(0, 384), pl.ds(384, 512)
    qkv_in = share(qkv_in, qkv_at)
    ag.relay_one()
    up_in = share(up_in, up_at)
    ag.relay_two()
    qkv_pass = share_twin(qkv_in, qkv_at)
    own = vectors[...].astype(F32)
    qkv_bias = jnp.concatenate([own[6:7], jnp.zeros((1, 128), F32), own[7:8]], axis=1)
    up_bias = jnp.concatenate([own[k : k + 1] for k in range(8, 12)], axis=1)
    qkv_pass.wait_recv()
    ag.row()

    def project(b, carry):
        value = dot(first[b], columns[:, :, 0:384].reshape(D, 384)) + qkv_bias
        at = pl.multiple_of(b * 72, 8)
        mixed[0, pl.ds(at, 72), :] = value[0:72]
        mixed[1, pl.ds(at, 72), :] = value[72:144]
        return carry

    each(project, 0, 5)
    ag.finish()
    ag_cot = Gather(net, cot)
    each(project, 5, 8)
    qkv_low[...] = mixed[...].astype(BF16)
    ag_cot.relay_one()

    def attend(image, carry):
        q, k, v = (qkv_low[image, :, i * 128 : (i + 1) * 128] for i in range(3))
        zero = jnp.zeros_like(q)
        total = jnp.zeros(q.shape, F32)
        for h, mask in enumerate(head_masks(q.shape)):
            score = dot_last(jnp.where(mask, q, zero), k) * SCALE
            top = jnp.max(score, -1, keepdims=True)
            e = jnp.exp(score - top)
            row = jnp.sum(e, -1, keepdims=True)
            p = (e * (1.0 / row)).astype(BF16)
            total += dot(p, jnp.where(mask, v, zero))
            lse[image, :, h : h + 1] = top + jnp.log(row)
        heads[image] = total
        return carry

    lax.fori_loop(0, 2, attend, 0)
    up_pass = share_twin(up_in, up_at)

    def by_device(ref, b):
        at = pl.multiple_of(b * 72, 8)
        both = [ref[i, pl.ds(at, 72), :] for i in range(2)]
        return jnp.concatenate(both, axis=0).astype(BF16)

    def outward(b, carry):
        value = by_device(heads, b)
        attended[b] = value
        parts[0, b] = dot(value, out_weight[...]).astype(BF16)
        return carry

    rs = rs_branch = scatter(0)
    each_sent(rs, outward, 0)
    rs.over()
    rs.relay()
    ag_cot.relay_two()
    resid = tokens[...].astype(F32) + (rs.finish() + bias_out)
    resid_ref[...] = resid
    unit2, inverse2 = norm_unit(resid)
    second[s] = (unit2 * gain2 + shift2).astype(BF16)
    ag = Gather(net, second)
    up_pass.wait_recv()

    def feed(b, total):
        up = columns[:, :, 384:896].reshape(D, 512)
        u = dot(second[b], up) + up_bias
        square = u * u
        t = jnp.tanh(GELU * (u + 0.044715 * u * square))
        act = (0.5 * u * (1.0 + t)).astype(BF16)
        slope = 0.5 * (1.0 + t) + (0.5 * GELU) * u * (1.0 - t * t) * (
            1.0 + 0.134145 * square
        )
        active[b] = act
        gu = (dot_last(cot[b], down_weight[...]) * slope).astype(BF16)
        grad_upper[b] = gu
        parts[1, b] = dot_last(gu, up).astype(BF16)
        parts[2, b] = dot(act, down_weight[...]).astype(BF16)
        return total + jnp.sum(gu.astype(F32), 0, keepdims=True)

    ag.relay_one()
    ag_cot.row()
    ag_cot.finish()
    up_bias_grad = each(feed, 0, 1, jnp.zeros((1, 512), F32))
    ag.relay_two()
    ag.row()
    up_bias_grad = each(feed, 1, 5, up_bias_grad)
    ag.finish()
    rs = scatter(1)
    up_bias_grad = each(feed, 5, 6, up_bias_grad)
    rs.hop()
    up_bias_grad = each(feed, 6, 8, up_bias_grad)
    rs.side()
    rs.near()
    own = pl.ds(pl.multiple_of(s * 128, 128), 128)
    small[...] = jnp.zeros_like(small)
    for i in range(4):
        small[8 + i : 9 + i, :] = up_bias_grad[:, i * 128 : (i + 1) * 128]
    small[7:8, :] = jnp.sum(cot[:, :, own].astype(F32).reshape(1152, 128), 0, keepdims=True)

    def down_tile(i):
        at = pl.ds(i * 256, 256)
        value = dot_first(
            active[...].reshape(1152, 512), cot[:, :, at].reshape(1152, 256)
        ).astype(BF16)
        for q in range(8):
            down_grad[q, :, at] = value[q * 64 : (q + 1) * 64]

    down_tile(0)
    rs.far()
    down_tile(1)
    rs.over()
    rs.relay()
    down_tile(2)
    down_tile(3)
    down_all.core()
    grad_second = rs.finish()
    unit2, inverse2 = norm_unit(resid_ref[...])
    grad_resid = cotangent[...].astype(F32) + norm_back(grad_second, unit2, inverse2, gain2)
    grad_resid_ref[...] = grad_resid
    branch[s] = grad_resid.astype(BF16)
    ag = Gather(net, branch)
    gain2_grad = jnp.sum(grad_second * unit2, 0, keepdims=True)
    shift2_grad = jnp.sum(grad_second, 0, keepdims=True)

    def up_tile(i):
        value = dot_first(
            second[:, :, i * 256 : (i + 1) * 256].reshape(1152, 256),
            grad_upper[...].reshape(1152, 512),
        ).astype(BF16)
        for j in range(2):
            for q in range(8):
                up_grad[q, (2 * i + j) * 16 : (2 * i + j + 1) * 16, :] = value[
                    j * 128 + q * 16 : j * 128 + (q + 1) * 16
                ]

    ag.relay_one()
    down_all.ring()
    up_tile(0)
    ag.relay_two()
    ag.row()
    up_tile(1)
    down_all.relay()
    up_tile(2)
    ag.finish()
    rs_out = scatter(2)
    rs_out.hop()
    rs_out.side()
    rs_out.near()
    down_all.beside()

    def back_heads(b, carry):
        value = dot_last(branch[b], out_weight[...])
        at = pl.multiple_of(b * 72, 8)
        heads[0, pl.ds(at, 72), :] = value[0:72]
        heads[1, pl.ds(at, 72), :] = value[72:144]
        return carry

    each(back_heads, 0, 8)
    up_tile(3)
    value = dot_first(attended[...].reshape(1152, 128), branch[...].reshape(1152, D)).astype(BF16)
    for q in range(8):
        out_grad[q] = value[q * 16 : (q + 1) * 16]
    rs_out.far()
    up_all.core()
    out_all.core()
    down_all.cross()
    down_all.back()

    def attend_back(image, carry):
        q, k, v = (qkv_low[image, :, i * 128 : (i + 1) * 128] for i in range(3))
        grad = heads[image].astype(BF16)
        zero = jnp.zeros_like(q)
        dq = jnp.zeros(q.shape, F32)
        dk, dv = dq, dq
        for h, mask in enumerate(head_masks(q.shape)):
            qh, kh, gh = (jnp.where(mask, a, zero) for a in (q, k, grad))
            p = jnp.exp(dot_last(qh, k) * SCALE - lse[image, :, h : h + 1])
            dp = dot_last(gh, v)
            inner = jnp.sum(p * dp, -1, keepdims=True)
            ds = (p * (dp - inner)).astype(BF16)
            dq += dot(ds, kh)
            dk += dot_first(ds, qh)
            dv += dot_first(p.astype(BF16), gh)
        mixed[image, :, 0:128] = dq * SCALE
        mixed[image, :, 128:256] = dk * SCALE
        mixed[image, :, 256:384] = dv
        return carry

    lax.fori_loop(0, 1, attend_back, 0)
    up_all.ring()
    out_all.ring()
    rs_out.over()
    lax.fori_loop(1, 2, attend_back, 0)
    rs_out.relay()
    down_all.back_relay()
    up_all.relay()
    out_all.relay()

    def back_first(b, total):
        value = by_device(mixed, b)
        grad_qkv[b] = value
        parts[0, b] = dot_last(value, columns[:, :, 0:384].reshape(D, 384)).astype(BF16)
        return total + jnp.sum(value.astype(F32), 0, keepdims=True)

    net.settle([rs_branch.hopped, *rs_branch.sides, *rs_branch.nears])
    rs = scatter(3)
    qkv_bias_grad = each_sent(rs, back_first, jnp.zeros((1, 384), F32))
    small[4:5, :] = qkv_bias_grad[:, 0:128]
    small[5:6, :] = qkv_bias_grad[:, 256:384]
    small[6:7, :] = jnp.sum(branch[:, :, own].astype(F32).reshape(1152, 128), 0, keepdims=True)

    def qkv_tile(i):
        value = dot_first(
            first[:, :, i * 256 : (i + 1) * 256].reshape(1152, 256),
            grad_qkv[...].reshape(1152, 384),
        ).astype(BF16)
        for j in range(2):
            for q in range(8):
                qkv_grad[q, (2 * i + j) * 16 : (2 * i + j + 1) * 16, :] = value[
                    j * 128 + q * 16 : j * 128 + (q + 1) * 16
                ]

    qkv_tile(0)
    up_all.beside()
    out_all.beside()
    qkv_tile(1)
    rs.over()
    qkv_tile(2)
    down_all.swap()
    qkv_tile(3)
    qkv_all.core()
    rs.relay()
    block_out[...] = (resid_ref[...] + (rs_out.finish() + bias_down)).astype(BF16)
    qkv_all.ring()
    up_all.cross()
    out_all.cross()
    out_all.back()
    qkv_all.relay()
    up_all.back()
    out_all.back_relay()
    qkv_all.beside()
    grad_first = rs.finish()
    unit1, inverse1 = norm_unit(tokens[...].astype(F32))
    input_grad[...] = (
        grad_resid_ref[...] + norm_back(grad_first, unit1, inverse1, gain1)
    ).astype(BF16)
    gain1_grad = jnp.sum(grad_first * unit1, 0, keepdims=True)
    shift1_grad = jnp.sum(grad_first, 0, keepdims=True)
    four = jnp.concatenate(
        [gain1_grad, shift1_grad, gain2_grad, shift2_grad, jnp.zeros((12, D), F32)], axis=0
    ).astype(BF16)
    for t in range(8):
        fours[t] = four[:, t * 128 : (t + 1) * 128]
    moved = [net.copy(fours.at[to["shard"]], fours_in.at[s], to) for to in net.peers]
    fours_in[s] = fours[s]
    qkv_all.cross()
    up_all.back_relay()
    out_all.swap()
    for made in moved:
        made.wait_recv()
    total = jnp.sum(fours_in[...].astype(F32), 0)
    small[0:4, :] = total[0:4]
    small_low[...] = small[...].astype(BF16)
    moved = [net.copy(small_low, small_ring.at[net.r], to) for to in net.replicas]
    small_ring[net.r] = small_low[...]
    qkv_all.back()
    up_all.swap()
    qkv_all.back_relay()
    for made in moved:
        made.wait_recv()
    small_sum[...] = add(*(small_ring[k] for k in range(16)))
    qkv_all.swap()
    for every in (down_all, out_all, up_all, qkv_all):
        every.end()
    net.drain()


def layer(*arguments):
    vmem = lambda *shape: pltpu.VMEM(shape, BF16)
    wide = lambda *shape: pltpu.VMEM(shape, F32)
    space = pl.BlockSpec(memory_space=pltpu.VMEM)
    shape = lambda *sizes: jax.ShapeDtypeStruct(sizes, BF16)
    return pl.pallas_call(
        layer_kernel,
        out_shape=[
            shape(ROWS, D),
            shape(ROWS, D),
            shape(512, D),
            shape(128, D),
            shape(128, 4096),
            shape(128, 3 * D),
            jax.ShapeDtypeStruct((16, 128), F32),
        ],
        in_specs=[space] * 7,
        out_specs=[space] * 7,
        scratch_shapes=[
            vmem(8, 64, D),
            vmem(8, 16, D),
            vmem(8, 128, 512),
            vmem(8, 128, 384),
            vmem(8, 16, 128),
            vmem(8, 128, 896),
            vmem(8, ROWS, D),
            vmem(8, ROWS, D),
            vmem(8, ROWS, D),
            vmem(8, ROWS, D),
            wide(2, 576, 384),
            vmem(2, 576, 384),
            wide(2, 576, 128),
            wide(2, 576, 128),
            vmem(8, ROWS, 128),
            vmem(8, ROWS, 512),
            vmem(8, ROWS, 512),
            vmem(8, ROWS, 384),
            wide(ROWS, D),
            wide(ROWS, D),
            wide(16, 128),
            vmem(8, 16, 128),
            vmem(8, 16, 128),
            vmem(3, 8, ROWS, D),
            vmem(4, ROWS, D),
            vmem(4, 2, ROWS, D),
            vmem(4, 2, ROWS, HALF),
            vmem(4, 2, ROWS, HALF),
            vmem(4, 2, ROWS, HALF),
            vmem(4, ROWS, D),
            vmem(4, ROWS, D),
            vmem(16, 128),
            vmem(16, 16, 128),
            vmem(2, 4, 64, D),
            vmem(5, 64, D),
            vmem(2, 4, 16, D),
            vmem(5, 16, D),
            vmem(2, 4, 128, 512),
            vmem(5, 128, 512),
            vmem(2, 8, 16, 512),
            vmem(2, 4, 128, 384),
            vmem(5, 128, 384),
            vmem(2, 8, 16, 384),
            pltpu.SemaphoreType.DMA((240,)),
            pltpu.SemaphoreType.DMA((240,)),
        ],
        name="layer",
        cost_estimate=pl.CostEstimate(
            flops=11 * 10**9, bytes_accessed=12 * 10**6, transcendentals=0
        ),
        compiler_params=pltpu.CompilerParams(
            collective_id=1, has_side_effects=True, vmem_limit_bytes=62 << 20
        ),
    )(*arguments)


def cast_kernel(down, out, up, qkv, small, *outs):
    for source, target in zip((down, out, up, qkv), outs[:4]):
        target[...] = source[...].astype(F32)
    for k, target in enumerate(outs[4:12]):
        target[...] = small[k]
    for k in range(4):
        outs[12][k * 128 : (k + 1) * 128] = small[8 + k]


def cast(down, out, up, qkv, small):
    steps = 4
    block = lambda a: pl.BlockSpec((a.shape[0] // steps, a.shape[1]), lambda i: (i, 0))
    whole = lambda *sizes: pl.BlockSpec(sizes, lambda i: (0,) * len(sizes))
    shape = lambda *sizes: jax.ShapeDtypeStruct(sizes, F32)
    large = (down, out, up, qkv)
    return pl.pallas_call(
        cast_kernel,
        grid=(steps,),
        out_shape=[
            *(shape(*a.shape) for a in large),
            *(shape(128) for _ in range(8)),
            shape(512),
        ],
        in_specs=[*map(block, large), whole(16, 128)],
        out_specs=[*map(block, large), *(whole(128) for _ in range(8)), whole(512)],
        name="cast",
        compiler_params=pltpu.CompilerParams(vmem_limit_bytes=62 << 20),
    )(*large, small)


def body(
    tokens,
    cotangent,
    attn_gain,
    attn_shift,
    qkv_weight,
    query_bias,
    value_bias,
    out_weight,
    out_bias,
    mlp_gain,
    mlp_shift,
    up_weight,
    up_bias,
    down_weight,
    down_bias,
):
    vectors = [attn_gain, attn_shift, mlp_gain, mlp_shift, out_bias, down_bias]
    vectors = [a.reshape(-1, 128) for a in (*vectors, query_bias, value_bias, up_bias)]
    vectors = jnp.concatenate([*vectors, jnp.zeros((4, 128), BF16)], axis=0)
    block_out, input_grad, *sums = layer(
        tokens.reshape(ROWS, D),
        cotangent.reshape(ROWS, D),
        vectors,
        qkv_weight,
        up_weight,
        out_weight,
        down_weight,
    )
    down_grad, out_grad, up_grad, qkv_grad, *small, up_bias_grad = cast(*sums)
    return (
        block_out.reshape(2, 72, D),
        input_grad.reshape(2, 72, D),
        small[0],
        small[1],
        qkv_grad,
        small[4],
        small[5],
        out_grad,
        small[6],
        small[2],
        small[3],
        up_grad,
        up_bias_grad,
        down_grad,
        small[7],
    )


def solution(mesh):
    row, cube, flat = P("shard"), P("replica", "shard", None), P("shard", None)
    return jax.shard_map(
        body,
        mesh=mesh,
        in_specs=(cube, cube, row, row, flat, row, row, flat, row, row, row, flat, row, flat, row),
        out_specs=(cube, cube, row, row, flat, row, row, flat, row, row, row, flat, row, flat, row),
        check_vma=False,
    )
```

```python
import jax
import jax.numpy as jnp
from jax import lax
from jax.experimental import pallas as pl
from jax.experimental.pallas import tpu as pltpu
from jax.sharding import PartitionSpec as P

HEAD_DIM = 64
EPS = 1e-06
F32 = jnp.float32
BF16 = jnp.bfloat16
SCALE = HEAD_DIM ** (-0.5)
MESH = pl.DeviceIdType.MESH
D = 1024
ROWS = 144
HALF = 512
GELU = 0.7978845608028654


def dot(a, b):
    return lax.dot_general(a, b, (((1,), (0,)), ((), ())), preferred_element_type=F32)


def dot_last(a, b):
    return lax.dot_general(a, b, (((1,), (1,)), ((), ())), preferred_element_type=F32)


def dot_first(a, b):
    return lax.dot_general(a, b, (((0,), (0,)), ((), ())), preferred_element_type=F32)


def norm_unit(v):
    mean = jnp.mean(v, -1, keepdims=True)
    centred = v - mean
    inverse = lax.rsqrt(jnp.mean(centred * centred, -1, keepdims=True) + EPS)
    return centred * inverse, inverse


def norm_back(grad, unit, inverse, gain):
    gn = grad * gain
    inner = jnp.mean(gn * unit, -1, keepdims=True)
    return inverse * (gn - jnp.mean(gn, -1, keepdims=True) - unit * inner)


def head_masks(shape):
    low = lax.broadcasted_iota(jnp.int32, shape, 1) < HEAD_DIM
    return (low, jnp.logical_not(low))


def add(*terms):
    total = terms[0].astype(F32)
    for term in terms[1:]:
        total = total + term.astype(F32)
    return total


class Net:
    def __init__(self, send, recv):
        self.send, self.recv, self.count, self.open = send, recv, 0, []
        self.s = lax.axis_index("shard")
        self.h, self.x = self.s // 4, lax.rem(self.s, 4)
        r = lax.axis_index("replica")
        self.core, self.y = lax.rem(r, 2), lax.rem(r // 2, 4)
        zlow = r // 8
        base = r - self.y * 2
        self.right = {"shard": self.at(self.h, self.x + 1)}
        self.left = {"shard": self.at(self.h, self.x + 3)}
        self.across = {"shard": self.at(1 - self.h, self.x)}
        self.twin = {"replica": r + 1 - 2 * self.core}
        self.up = {"replica": base + lax.rem(self.y + 1, 4) * 2}
        self.down = {"replica": base + lax.rem(self.y + 3, 4) * 2}
        self.facing = {"replica": base + lax.rem(self.y + 2, 4) * 2}
        self.beside = {"replica": r + 8 - 16 * zlow}
        self.replicas = [{"replica": lax.rem(r + k, 16)} for k in range(1, 16)]
        self.r = r
        self.peers = [{"shard": lax.rem(self.s + k, 8)} for k in range(1, 8)]

    def at(self, h, x):
        return h * 4 + lax.rem(x, 4)

    def copy(self, src, dst, to):
        i = self.count
        self.count += 1
        made = pltpu.make_async_remote_copy(
            src_ref=src,
            dst_ref=dst,
            send_sem=self.send.at[i],
            recv_sem=self.recv.at[i],
            device_id=to,
            device_id_type=MESH,
        )
        made.start()
        self.open.append(made)
        return made

    def drain(self):
        for made in self.open:
            made.wait_send()
        self.open = []

    def settle(self, copies):
        for made in copies:
            made.wait_send()
            self.open = [other for other in self.open if other is not made]

    def barrier(self, others):
        semaphore = pltpu.get_barrier_semaphore()
        for other in others:
            pl.semaphore_signal(semaphore, inc=1, device_id=other, device_id_type=MESH)
        pl.semaphore_wait(semaphore, len(others))


class Gather:
    def __init__(self, net, whole):
        self.net, self.whole = net, whole
        self.a = self.piece(net.s, 0, net.right)
        self.b = self.piece(net.s, 1, net.left)
        own = whole.at[net.s]
        self.z = net.copy(own, own, net.across)
        self.more = [self.piece(net.s, 1, net.right), self.piece(net.s, 0, net.left)]

    def piece(self, block, second, to):
        part = self.whole.at[block, :, pl.ds(second * HALF, HALF)]
        return self.net.copy(part, part, to)

    def relay_one(self):
        net = self.net
        self.a.wait_recv()
        self.c = self.piece(net.at(net.h, net.x + 3), 0, net.right)
        self.b.wait_recv()
        self.d = self.piece(net.at(net.h, net.x + 1), 1, net.left)

    def relay_two(self):
        net = self.net
        self.z.wait_recv()
        part = self.whole.at[net.at(1 - net.h, net.x)]
        self.rest = [net.copy(part, part, net.right), net.copy(part, part, net.left)]
        block = net.at(net.h, net.x + 2)
        self.c.wait_recv()
        self.rest.append(self.piece(block, 0, net.across))
        self.d.wait_recv()
        self.rest.append(self.piece(block, 1, net.across))

    def row(self):
        for made in self.more:
            made.wait_recv()

    def finish(self):
        for made in self.rest:
            made.wait_recv()


class Scatter:
    def __init__(self, net, part, hop, side, near, far, passed, kept, came):
        self.net, self.part, self.hop_in, self.side_in = net, part, hop, side
        self.near_in, self.far_in, self.passed, self.kept, self.came = near, far, passed, kept, came
        self.one, self.two = pl.ds(0, HALF), pl.ds(HALF, HALF)
        h, x = net.h, net.x
        self.own, self.facing = net.s, net.at(h, x + 2)
        self.right, self.left = net.at(h, x + 1), net.at(h, x + 3)
        self.other = [net.at(1 - h, x + k) for k in range(4)]

    def hop(self):
        self.hopped = self.net.copy(self.part.at[self.other[2]], self.hop_in, self.net.across)

    def side(self):
        net, part = self.net, self.part
        self.sides = [
            net.copy(part.at[self.other[1]], self.side_in.at[0], net.right),
            net.copy(part.at[self.other[3]], self.side_in.at[1], net.left),
        ]

    def near(self):
        net, part = self.net, self.part
        self.nears = [
            net.copy(part.at[self.right, :, self.two], self.near_in.at[0], net.right),
            net.copy(part.at[self.left, :, self.one], self.near_in.at[1], net.left),
        ]

    def far(self):
        net, hop = self.net, self.hop_in
        self.hopped.wait_recv()
        hop[...] = add(hop[...], self.part[self.facing]).astype(BF16)
        self.fars = [
            net.copy(hop.at[:, self.one], self.far_in.at[0], net.right),
            net.copy(hop.at[:, self.two], self.far_in.at[1], net.left),
        ]

    def over(self):
        for made in self.sides:
            made.wait_recv()
        self.kept[...] = add(
            self.part[self.other[0]], self.side_in[0], self.side_in[1]
        ).astype(BF16)
        self.crossed = self.net.copy(self.kept, self.came, self.net.across)

    def relay(self):
        net, part, far = self.net, self.part, self.far_in
        self.fars[0].wait_recv()
        far[0] = add(far[0], part[self.right, :, self.one]).astype(BF16)
        passes = [net.copy(far.at[0], self.passed.at[0], net.right)]
        self.fars[1].wait_recv()
        far[1] = add(far[1], part[self.left, :, self.two]).astype(BF16)
        passes.append(net.copy(far.at[1], self.passed.at[1], net.left))
        self.last = [*self.nears, *passes, self.crossed]

    def finish(self):
        for made in self.last:
            made.wait_recv()
        part, near, passed, came = self.part, self.near_in, self.passed, self.came
        one, two = self.one, self.two
        return jnp.concatenate(
            [
                add(part[self.own, :, one], passed[0], near[1], came[:, one]),
                add(part[self.own, :, two], passed[1], near[0], came[:, two]),
            ],
            axis=1,
        )


class Reduce:
    def __init__(self, net, grad, pair, ring, out, turned=None):
        self.net, self.grad, self.out, self.turned = net, grad, out, turned
        self.sent, self.work = pair
        self.near_in, self.far_in, self.passed, self.kept, self.came = ring
        width = grad.shape[-1]
        cut = max(width // 256, 1) * 128 if width != 384 else 256
        self.one, self.two = pl.ds(0, cut), pl.ds(cut, width - cut)
        self.mine = pl.ds(net.core * 4, 4)
        self.q = net.core * 4 + net.y
        self.at_up, self.at_facing, self.at_down = (lax.rem(net.y + k, 4) for k in (1, 2, 3))

    def core(self):
        net = self.net
        self.moved = net.copy(self.grad.at[pl.ds((1 - net.core) * 4, 4)], self.sent, net.twin)

    def ring(self):
        net, work, near, far = self.net, self.work, self.near_in, self.far_in
        one, two = self.one, self.two
        self.moved.wait_recv()
        work[...] = add(self.grad[self.mine], self.sent[...]).astype(BF16)
        self.fars = [
            net.copy(work.at[self.at_facing, :, one], far.at[:, one], net.up),
            net.copy(work.at[self.at_facing, :, two], far.at[:, two], net.down),
        ]
        self.nears = [
            net.copy(work.at[self.at_up, :, two], near.at[:, two], net.up),
            net.copy(work.at[self.at_down, :, one], near.at[:, one], net.down),
        ]

    def relay(self):
        net, far = self.net, self.far_in
        steps = ((self.one, self.at_up, net.up), (self.two, self.at_down, net.down))
        for k, (part, block, to) in enumerate(steps):
            self.fars[k].wait_recv()
            far[:, part] = add(far[:, part], self.work[block, :, part]).astype(BF16)
            self.nears.append(net.copy(far.at[:, part], self.passed.at[:, part], to))

    def beside(self):
        net = self.net
        for made in self.nears:
            made.wait_recv()
        self.kept[...] = add(self.work[net.y], self.near_in[...], self.passed[...]).astype(BF16)
        self.over = net.copy(self.kept, self.came, net.beside)

    def place(self, q, eighths=1):
        rows = self.out.shape[0] // 8
        return pl.ds(pl.multiple_of(q * rows, 16), rows * eighths)

    def cross(self):
        net = self.net
        self.over.wait_recv()
        total = add(self.kept[...], self.came[...]).astype(BF16)
        if self.turned is None:
            self.out[self.place(self.q)] = total
            return
        away, back = self.turned
        away[...] = total.reshape(away.shape)
        self.crossed = [
            net.copy(away.at[to["shard"]], back.at[net.s], to) for to in net.peers
        ]
        back[net.s] = away[net.s]

    def back(self):
        net, out = self.net, self.out
        own = self.place(self.q)
        if self.turned is not None:
            for made in self.crossed:
                made.wait_recv()
            incoming = self.turned[1]
            blocks = [incoming[t] for t in range(8)]
            width = blocks[0].shape[-1]
            for i in range(width // 128 if width == 384 else 1):
                size = 128 if width == 384 else width
                for t in range(8):
                    at = i * D + t * size
                    out[own, at : at + size] = blocks[t][:, i * 128 : i * 128 + size]
        part = out.at[own]
        self.shared = [net.copy(part, part, net.up), net.copy(part, part, net.down)]

    def back_relay(self):
        net, out = self.net, self.out
        half = out.shape[1] // 2
        self.lasts = []
        steps = ((0, self.at_down, net.up), (half, self.at_up, net.down))
        for k, (at, block, to) in enumerate(steps):
            self.shared[k].wait_recv()
            part = out.at[self.place(net.core * 4 + block), pl.ds(at, half)]
            self.lasts.append(net.copy(part, part, to))

    def swap(self):
        for made in self.lasts:
            made.wait_recv()
        part = self.out.at[self.place(self.net.core * 4, 4)]
        self.ended = self.net.copy(part, part, self.net.twin)

    def end(self):
        self.ended.wait_recv()


def layer_kernel(*refs):
    layer_steps(*refs[:2], refs[2:8], *refs[8:])


def layer_steps(
    tokens,
    cotangent,
    singles,
    query_bias,
    value_bias,
    up_bias,
    qkv_weight,
    up_weight,
    out_weight,
    down_weight,
    block_out,
    input_grad,
    down_sum,
    out_sum,
    up_sum,
    qkv_sum,
    small_sum,
    down_grad,
    out_grad,
    up_grad,
    qkv_grad,
    wide_vectors,
    vectors,
    all_vectors,
    columns,
    first,
    cot,
    second,
    branch,
    mixed,
    qkv_low,
    heads,
    lse,
    attended,
    active,
    grad_upper,
    grad_qkv,
    resid_ref,
    grad_resid_ref,
    small,
    fours,
    fours_in,
    parts,
    hop,
    side,
    near,
    far,
    passed,
    kept,
    came,
    small_low,
    small_ring,
    down_pair,
    down_ring,
    out_pair,
    out_ring,
    up_pair,
    up_ring,
    up_turned,
    qkv_pair,
    qkv_ring,
    qkv_turned,
    send,
    recv,
):
    net = Net(send, recv)
    s, core = net.s, net.core
    net.barrier([*net.peers, *net.replicas])

    def reduce(grad, pair, ring, out, turned=None):
        split = lambda ref, n: [ref.at[i] for i in range(n)]
        turned = None if turned is None else split(turned, 2)
        return Reduce(net, grad, split(pair, 2), split(ring, 5), out, turned)

    down_all = reduce(down_grad, down_pair, down_ring, down_sum)
    out_all = reduce(out_grad, out_pair, out_ring, out_sum)
    up_all = reduce(up_grad, up_pair, up_ring, up_sum, up_turned)
    qkv_all = reduce(qkv_grad, qkv_pair, qkv_ring, qkv_sum, qkv_turned)
    mine = pl.ds(pl.multiple_of(core * 64, 64), 64)
    sixteen = pl.ds(pl.multiple_of(core * 64 + net.y * 16, 16), 16)

    def scatter(i):
        buffers = (hop, side, near, far, passed, kept, came)
        return Scatter(net, parts.at[i % 3], *(buffer.at[i] for buffer in buffers))

    def each(work, least, end, carry=0):
        def step(i, carry):
            row, j = i // 4, lax.rem(i, 4)
            same = j + j // 2 - 2 * (j // 3)
            cross = lax.rem(2 * j, 3) + 3 * (j // 3)
            h = net.h + row - 2 * net.h * row
            return work(net.at(h, net.x + (1 - row) * same + row * cross), carry)

        return lax.fori_loop(least, end, step, carry)

    def each_sent(rs, work, carry):
        carry = each(work, 5, 6, carry)
        rs.hop()
        carry = each(work, 6, 8, carry)
        rs.side()
        carry = each(work, 1, 3, carry)
        rs.near()
        carry = each(work, 3, 5, carry)
        rs.far()
        return each(work, 0, 1, carry)

    wide_vectors[...] = jnp.zeros_like(wide_vectors)
    for k, single in enumerate(singles):
        wide_vectors[k : k + 1, :] = single[...].astype(F32)
    vectors[...] = wide_vectors[...].astype(BF16)
    vec = [net.copy(vectors, all_vectors.at[s], to) for to in net.peers]
    all_vectors[s] = vectors[...]
    cot[s] = cotangent[...]
    ag_cot = Gather(net, cot)
    qkv_in, up_in = [], []
    thirds = [
        lambda t, i=i: qkv_weight.at[sixteen, pl.ds(pl.multiple_of(i * D + t * 128, 128), 128)]
        for i in range(3)
    ]
    quarter = lambda t: up_weight.at[sixteen, pl.ds(pl.multiple_of(t * 512, 512), 512)]
    for to in net.peers:
        for i in range(3):
            there = columns.at[s, sixteen, pl.ds(i * 128, 128)]
            qkv_in.append(net.copy(thirds[i](to["shard"]), there, to))
    for to in net.peers:
        there = columns.at[s, sixteen, pl.ds(384, 512)]
        up_in.append(net.copy(quarter(to["shard"]), there, to))
    for i in range(3):
        columns[s, sixteen, i * 128 : (i + 1) * 128] = thirds[i](s)[...]
    columns[s, sixteen, 384:896] = quarter(s)[...]

    def share(arrived, at):
        for made in arrived:
            made.wait_recv()
        part = columns.at[:, sixteen, at]
        return [net.copy(part, part, to) for to in (net.up, net.down, net.facing)]

    def share_twin(arrived, at):
        for made in arrived:
            made.wait_recv()
        part = columns.at[:, mine, at]
        return net.copy(part, part, net.twin)

    x = tokens[...].astype(F32)
    unit1, inverse1 = norm_unit(x)
    for made in vec:
        made.wait_recv()
    table = [all_vectors[j].astype(F32) for j in range(8)]
    gain1, shift1, gain2, shift2, bias_out, bias_down = (
        jnp.concatenate([t[i : i + 1] for t in table], axis=1) for i in range(6)
    )
    first[s] = (unit1 * gain1 + shift1).astype(BF16)
    ag = Gather(net, first)
    qkv_at, up_at = pl.ds(0, 384), pl.ds(384, 512)
    qkv_in = share(qkv_in, qkv_at)
    ag.relay_one()
    up_in = share(up_in, up_at)
    ag.relay_two()
    qkv_pass = share_twin(qkv_in, qkv_at)
    qkv_bias = jnp.concatenate(
        [query_bias[...].astype(F32), jnp.zeros((1, 128), F32), value_bias[...].astype(F32)], axis=1
    )
    up_bias = up_bias[...].astype(F32)
    qkv_pass.wait_recv()
    ag.row()

    def project(b, carry):
        value = dot(first[b], columns[:, :, 0:384].reshape(D, 384)) + qkv_bias
        at = pl.multiple_of(b * 72, 8)
        mixed[0, pl.ds(at, 72), :] = value[0:72]
        mixed[1, pl.ds(at, 72), :] = value[72:144]
        return carry

    each(project, 0, 5)
    ag_cot.relay_one()
    ag.finish()
    ag_cot.relay_two()
    each(project, 5, 8)
    qkv_low[...] = mixed[...].astype(BF16)

    def attend(image, carry):
        q, k, v = (qkv_low[image, :, i * 128 : (i + 1) * 128] for i in range(3))
        zero = jnp.zeros_like(q)
        total = jnp.zeros(q.shape, F32)
        for h, mask in enumerate(head_masks(q.shape)):
            score = dot_last(jnp.where(mask, q, zero), k) * SCALE
            top = jnp.max(score, -1, keepdims=True)
            e = jnp.exp(score - top)
            row = jnp.sum(e, -1, keepdims=True)
            p = (e * (1.0 / row)).astype(BF16)
            total += dot(p, jnp.where(mask, v, zero))
            lse[image, :, h : h + 1] = top + jnp.log(row)
        heads[image] = total
        return carry

    lax.fori_loop(0, 2, attend, 0)
    up_pass = share_twin(up_in, up_at)

    def by_device(ref, b):
        at = pl.multiple_of(b * 72, 8)
        both = [ref[i, pl.ds(at, 72), :] for i in range(2)]
        return jnp.concatenate(both, axis=0).astype(BF16)

    def outward(b, carry):
        value = by_device(heads, b)
        attended[b] = value
        parts[0, b] = dot(value, out_weight[...]).astype(BF16)
        return carry

    rs = rs_branch = scatter(0)
    each_sent(rs, outward, 0)
    rs.over()
    rs.relay()
    resid = tokens[...].astype(F32) + (rs.finish() + bias_out)
    resid_ref[...] = resid
    unit2, inverse2 = norm_unit(resid)
    second[s] = (unit2 * gain2 + shift2).astype(BF16)
    ag = Gather(net, second)
    up_pass.wait_recv()

    def feed(b, total):
        up = columns[:, :, 384:896].reshape(D, 512)
        u = dot(second[b], up) + up_bias
        square = u * u
        t = jnp.tanh(GELU * (u + 0.044715 * u * square))
        act = (0.5 * u * (1.0 + t)).astype(BF16)
        slope = 0.5 * (1.0 + t) + (0.5 * GELU) * u * (1.0 - t * t) * (
            1.0 + 0.134145 * square
        )
        active[b] = act
        gu = (dot_last(cot[b], down_weight[...]) * slope).astype(BF16)
        grad_upper[b] = gu
        parts[1, b] = dot_last(gu, up).astype(BF16)
        parts[2, b] = dot(act, down_weight[...]).astype(BF16)
        return total + jnp.sum(gu.astype(F32), 0, keepdims=True)

    ag.relay_one()
    ag_cot.row()
    ag_cot.finish()
    up_bias_grad = each(feed, 0, 1, jnp.zeros((1, 512), F32))
    ag.relay_two()
    ag.row()
    up_bias_grad = each(feed, 1, 5, up_bias_grad)
    ag.finish()
    rs = scatter(1)
    up_bias_grad = each(feed, 5, 6, up_bias_grad)
    rs.hop()
    up_bias_grad = each(feed, 6, 8, up_bias_grad)
    rs.side()
    rs.near()
    own = pl.ds(pl.multiple_of(s * 128, 128), 128)
    small[...] = jnp.zeros_like(small)
    for i in range(4):
        small[8 + i : 9 + i, :] = up_bias_grad[:, i * 128 : (i + 1) * 128]
    small[7:8, :] = jnp.sum(cot[:, :, own].astype(F32).reshape(1152, 128), 0, keepdims=True)

    def down_tile(i):
        at = pl.ds(i * 256, 256)
        value = dot_first(
            active[...].reshape(1152, 512), cot[:, :, at].reshape(1152, 256)
        ).astype(BF16)
        for q in range(8):
            down_grad[q, :, at] = value[q * 64 : (q + 1) * 64]

    down_tile(0)
    rs.far()
    down_tile(1)
    rs.over()
    rs.relay()
    down_tile(2)
    down_tile(3)
    down_all.core()
    grad_second = rs.finish()
    unit2, inverse2 = norm_unit(resid_ref[...])
    grad_resid = cotangent[...].astype(F32) + norm_back(grad_second, unit2, inverse2, gain2)
    grad_resid_ref[...] = grad_resid
    branch[s] = grad_resid.astype(BF16)
    ag = Gather(net, branch)
    gain2_grad = jnp.sum(grad_second * unit2, 0, keepdims=True)
    shift2_grad = jnp.sum(grad_second, 0, keepdims=True)

    def up_tile(i):
        value = dot_first(
            second[:, :, i * 256 : (i + 1) * 256].reshape(1152, 256),
            grad_upper[...].reshape(1152, 512),
        ).astype(BF16)
        for j in range(2):
            for q in range(8):
                up_grad[q, (2 * i + j) * 16 : (2 * i + j + 1) * 16, :] = value[
                    j * 128 + q * 16 : j * 128 + (q + 1) * 16
                ]

    def back_heads(b, carry):
        value = dot_last(branch[b], out_weight[...])
        at = pl.multiple_of(b * 72, 8)
        heads[0, pl.ds(at, 72), :] = value[0:72]
        heads[1, pl.ds(at, 72), :] = value[72:144]
        return carry

    ag.relay_one()
    down_all.ring()
    up_tile(0)
    ag.relay_two()
    up_tile(1)
    ag.row()
    down_all.relay()
    up_tile(2)
    up_tile(3)
    up_all.core()
    each(back_heads, 0, 5)
    ag.finish()
    rs_out = scatter(2)
    rs_out.hop()
    rs_out.side()
    rs_out.near()
    down_all.beside()
    each(back_heads, 5, 8)
    def attend_back(image, carry):
        q, k, v = (qkv_low[image, :, i * 128 : (i + 1) * 128] for i in range(3))
        grad = heads[image].astype(BF16)
        zero = jnp.zeros_like(q)
        dq = jnp.zeros(q.shape, F32)
        dk, dv = dq, dq
        for h, mask in enumerate(head_masks(q.shape)):
            qh, kh, gh = (jnp.where(mask, a, zero) for a in (q, k, grad))
            p = jnp.exp(dot_last(qh, k) * SCALE - lse[image, :, h : h + 1])
            dp = dot_last(gh, v)
            inner = jnp.sum(p * dp, -1, keepdims=True)
            ds = (p * (dp - inner)).astype(BF16)
            dq += dot(ds, kh)
            dk += dot_first(ds, qh)
            dv += dot_first(p.astype(BF16), gh)
        mixed[image, :, 0:128] = dq * SCALE
        mixed[image, :, 128:256] = dk * SCALE
        mixed[image, :, 256:384] = dv
        return carry

    lax.fori_loop(0, 1, attend_back, 0)
    up_all.ring()
    rs_out.far()
    down_all.cross()
    down_all.back()
    lax.fori_loop(1, 2, attend_back, 0)
    rs_out.over()

    def back_first(b, total):
        value = by_device(mixed, b)
        grad_qkv[b] = value
        parts[0, b] = dot_last(value, columns[:, :, 0:384].reshape(D, 384)).astype(BF16)
        return total + jnp.sum(value.astype(F32), 0, keepdims=True)

    net.settle([rs_branch.hopped, *rs_branch.sides, *rs_branch.nears])
    rs = scatter(3)
    qkv_bias_grad = each_sent(rs, back_first, jnp.zeros((1, 384), F32))
    up_all.relay()
    rs_out.relay()
    down_all.back_relay()
    small[4:5, :] = qkv_bias_grad[:, 0:128]
    small[5:6, :] = qkv_bias_grad[:, 256:384]
    small[6:7, :] = jnp.sum(branch[:, :, own].astype(F32).reshape(1152, 128), 0, keepdims=True)

    def qkv_tile(i):
        value = dot_first(
            first[:, :, i * 256 : (i + 1) * 256].reshape(1152, 256),
            grad_qkv[...].reshape(1152, 384),
        ).astype(BF16)
        for j in range(2):
            for q in range(8):
                qkv_grad[q, (2 * i + j) * 16 : (2 * i + j + 1) * 16, :] = value[
                    j * 128 + q * 16 : j * 128 + (q + 1) * 16
                ]

    qkv_tile(0)
    qkv_tile(1)
    up_all.beside()
    qkv_tile(2)
    qkv_tile(3)
    qkv_all.core()
    value = dot_first(attended[...].reshape(1152, 128), branch[...].reshape(1152, D)).astype(BF16)
    for q in range(8):
        out_grad[q] = value[q * 16 : (q + 1) * 16]
    out_all.core()
    rs.over()
    qkv_all.ring()
    up_all.cross()
    out_all.ring()
    rs.relay()
    down_all.swap()
    qkv_all.relay()
    out_all.relay()
    up_all.back()
    qkv_all.beside()
    out_all.beside()
    block_out[...] = (resid_ref[...] + (rs_out.finish() + bias_down)).astype(BF16)
    up_all.back_relay()
    qkv_all.cross()
    out_all.cross()
    out_all.back()
    grad_first = rs.finish()
    unit1, inverse1 = norm_unit(tokens[...].astype(F32))
    gain1_grad = jnp.sum(grad_first * unit1, 0, keepdims=True)
    shift1_grad = jnp.sum(grad_first, 0, keepdims=True)
    four = jnp.concatenate(
        [gain1_grad, shift1_grad, gain2_grad, shift2_grad, jnp.zeros((12, D), F32)], axis=0
    ).astype(BF16)
    for t in range(8):
        fours[t] = four[:, t * 128 : (t + 1) * 128]
    moved = [net.copy(fours.at[to["shard"]], fours_in.at[s], to) for to in net.peers]
    fours_in[s] = fours[s]
    qkv_all.back()
    input_grad[...] = (
        grad_resid_ref[...] + norm_back(grad_first, unit1, inverse1, gain1)
    ).astype(BF16)
    out_all.back_relay()
    up_all.swap()
    for made in moved:
        made.wait_recv()
    total = jnp.sum(fours_in[...].astype(F32), 0)
    small[0:4, :] = total[0:4]
    small_low[...] = small[...].astype(BF16)
    moved = [net.copy(small_low, small_ring.at[net.r], to) for to in net.replicas]
    small_ring[net.r] = small_low[...]
    qkv_all.back_relay()
    out_all.swap()
    for made in moved:
        made.wait_recv()
    small_sum[...] = add(*(small_ring[k] for k in range(16)))
    qkv_all.swap()
    for every in (down_all, out_all, up_all, qkv_all):
        every.end()
    net.drain()


def layer(*arguments):
    vmem = lambda *shape: pltpu.VMEM(shape, BF16)
    wide = lambda *shape: pltpu.VMEM(shape, F32)
    space = pl.BlockSpec(memory_space=pltpu.VMEM)
    shape = lambda *sizes: jax.ShapeDtypeStruct(sizes, BF16)
    return pl.pallas_call(
        layer_kernel,
        out_shape=[
            shape(ROWS, D),
            shape(ROWS, D),
            shape(512, D),
            shape(128, D),
            shape(128, 4096),
            shape(128, 3 * D),
            jax.ShapeDtypeStruct((16, 128), F32),
        ],
        in_specs=[space] * 15,
        out_specs=[space] * 7,
        scratch_shapes=[
            vmem(8, 64, D),
            vmem(8, 16, D),
            vmem(8, 128, 512),
            vmem(8, 128, 384),
            wide(16, 128),
            vmem(16, 128),
            vmem(8, 16, 128),
            vmem(8, 128, 896),
            vmem(8, ROWS, D),
            vmem(8, ROWS, D),
            vmem(8, ROWS, D),
            vmem(8, ROWS, D),
            wide(2, 576, 384),
            vmem(2, 576, 384),
            wide(2, 576, 128),
            wide(2, 576, 128),
            vmem(8, ROWS, 128),
            vmem(8, ROWS, 512),
            vmem(8, ROWS, 512),
            vmem(8, ROWS, 384),
            wide(ROWS, D),
            wide(ROWS, D),
            wide(16, 128),
            vmem(8, 16, 128),
            vmem(8, 16, 128),
            vmem(3, 8, ROWS, D),
            vmem(4, ROWS, D),
            vmem(4, 2, ROWS, D),
            vmem(4, 2, ROWS, HALF),
            vmem(4, 2, ROWS, HALF),
            vmem(4, 2, ROWS, HALF),
            vmem(4, ROWS, D),
            vmem(4, ROWS, D),
            vmem(16, 128),
            vmem(16, 16, 128),
            vmem(2, 4, 64, D),
            vmem(5, 64, D),
            vmem(2, 4, 16, D),
            vmem(5, 16, D),
            vmem(2, 4, 128, 512),
            vmem(5, 128, 512),
            vmem(2, 8, 16, 512),
            vmem(2, 4, 128, 384),
            vmem(5, 128, 384),
            vmem(2, 8, 16, 384),
            pltpu.SemaphoreType.DMA((240,)),
            pltpu.SemaphoreType.DMA((240,)),
        ],
        name="layer",
        cost_estimate=pl.CostEstimate(
            flops=11 * 10**9, bytes_accessed=12 * 10**6, transcendentals=0
        ),
        compiler_params=pltpu.CompilerParams(
            collective_id=1, has_side_effects=True, vmem_limit_bytes=62 << 20
        ),
    )(*arguments)


def cast_kernel(down, out, up, qkv, small, *outs):
    for source, target in zip((down, out, up, qkv), outs[:4]):
        target[...] = source[...].astype(F32)
    for k, target in enumerate(outs[4:12]):
        target[...] = small[k]
    for k in range(4):
        outs[12][k * 128 : (k + 1) * 128] = small[8 + k]


def cast(down, out, up, qkv, small):
    steps = 8
    block = lambda a: pl.BlockSpec((a.shape[0] // steps, a.shape[1]), lambda i: (i, 0))
    whole = lambda *sizes: pl.BlockSpec(sizes, lambda i: (0,) * len(sizes))
    shape = lambda *sizes: jax.ShapeDtypeStruct(sizes, F32)
    large = (down, out, up, qkv)
    return pl.pallas_call(
        cast_kernel,
        grid=(steps,),
        out_shape=[
            *(shape(*a.shape) for a in large),
            *(shape(128) for _ in range(8)),
            shape(512),
        ],
        in_specs=[*map(block, large), whole(16, 128)],
        out_specs=[*map(block, large), *(whole(128) for _ in range(8)), whole(512)],
        name="cast",
        compiler_params=pltpu.CompilerParams(vmem_limit_bytes=62 << 20),
    )(*large, small)


def body(
    tokens,
    cotangent,
    attn_gain,
    attn_shift,
    qkv_weight,
    query_bias,
    value_bias,
    out_weight,
    out_bias,
    mlp_gain,
    mlp_shift,
    up_weight,
    up_bias,
    down_weight,
    down_bias,
):
    vectors = (attn_gain, attn_shift, mlp_gain, mlp_shift, out_bias, down_bias)
    vectors = (*vectors, query_bias, value_bias, up_bias)
    block_out, input_grad, *sums = layer(
        tokens.reshape(ROWS, D),
        cotangent.reshape(ROWS, D),
        *(a.reshape(1, -1) for a in vectors),
        qkv_weight,
        up_weight,
        out_weight,
        down_weight,
    )
    down_grad, out_grad, up_grad, qkv_grad, *small, up_bias_grad = cast(*sums)
    return (
        block_out.reshape(2, 72, D),
        input_grad.reshape(2, 72, D),
        small[0],
        small[1],
        qkv_grad,
        small[4],
        small[5],
        out_grad,
        small[6],
        small[2],
        small[3],
        up_grad,
        up_bias_grad,
        down_grad,
        small[7],
    )


def solution(mesh):
    row, cube, flat = P("shard"), P("replica", "shard", None), P("shard", None)
    return jax.shard_map(
        body,
        mesh=mesh,
        in_specs=(cube, cube, row, row, flat, row, row, flat, row, row, row, flat, row, flat, row),
        out_specs=(cube, cube, row, row, flat, row, row, flat, row, row, row, flat, row, flat, row),
        check_vma=False,
    )
```

```python
import jax
import jax.numpy as jnp
from jax import lax
from jax.experimental import pallas as pl
from jax.experimental.pallas import tpu as pltpu
from jax.sharding import PartitionSpec as P

HEAD_DIM = 64
EPS = 1e-06
F32 = jnp.float32
BF16 = jnp.bfloat16
SCALE = HEAD_DIM ** (-0.5)
MESH = pl.DeviceIdType.MESH
D = 1024
ROWS = 144
HALF = 512
GELU = 0.7978845608028654


def dot(a, b):
    return lax.dot_general(a, b, (((1,), (0,)), ((), ())), preferred_element_type=F32)


def dot_last(a, b):
    return lax.dot_general(a, b, (((1,), (1,)), ((), ())), preferred_element_type=F32)


def dot_first(a, b):
    return lax.dot_general(a, b, (((0,), (0,)), ((), ())), preferred_element_type=F32)


def norm_unit(v):
    mean = jnp.mean(v, -1, keepdims=True)
    centred = v - mean
    inverse = lax.rsqrt(jnp.mean(centred * centred, -1, keepdims=True) + EPS)
    return centred * inverse, inverse


def norm_back(grad, unit, inverse, gain):
    gn = grad * gain
    inner = jnp.mean(gn * unit, -1, keepdims=True)
    return inverse * (gn - jnp.mean(gn, -1, keepdims=True) - unit * inner)


def head_masks(shape):
    low = lax.broadcasted_iota(jnp.int32, shape, 1) < HEAD_DIM
    return (low, jnp.logical_not(low))


def add(*terms):
    total = terms[0].astype(F32)
    for term in terms[1:]:
        total = total + term.astype(F32)
    return total


class Net:
    def __init__(self, send, recv):
        self.send, self.recv, self.count, self.open = send, recv, 0, []
        self.s = lax.axis_index("shard")
        self.h, self.x = self.s // 4, lax.rem(self.s, 4)
        r = lax.axis_index("replica")
        self.core, self.y = lax.rem(r, 2), lax.rem(r // 2, 4)
        zlow = r // 8
        base = r - self.y * 2
        self.right = {"shard": self.at(self.h, self.x + 1)}
        self.left = {"shard": self.at(self.h, self.x + 3)}
        self.across = {"shard": self.at(1 - self.h, self.x)}
        self.twin = {"replica": r + 1 - 2 * self.core}
        self.up = {"replica": base + lax.rem(self.y + 1, 4) * 2}
        self.down = {"replica": base + lax.rem(self.y + 3, 4) * 2}
        self.facing = {"replica": base + lax.rem(self.y + 2, 4) * 2}
        self.beside = {"replica": r + 8 - 16 * zlow}
        self.replicas = [{"replica": lax.rem(r + k, 16)} for k in range(1, 16)]
        self.r = r
        self.peers = [{"shard": lax.rem(self.s + k, 8)} for k in range(1, 8)]

    def at(self, h, x):
        return h * 4 + lax.rem(x, 4)

    def copy(self, src, dst, to):
        i = self.count
        self.count += 1
        made = pltpu.make_async_remote_copy(
            src_ref=src,
            dst_ref=dst,
            send_sem=self.send.at[i],
            recv_sem=self.recv.at[i],
            device_id=to,
            device_id_type=MESH,
        )
        made.start()
        self.open.append(made)
        return made

    def drain(self):
        for made in self.open:
            made.wait_send()
        self.open = []

    def settle(self, copies):
        for made in copies:
            made.wait_send()
            self.open = [other for other in self.open if other is not made]

    def barrier(self, others):
        semaphore = pltpu.get_barrier_semaphore()
        for other in others:
            pl.semaphore_signal(semaphore, inc=1, device_id=other, device_id_type=MESH)
        pl.semaphore_wait(semaphore, len(others))


class Gather:
    def __init__(self, net, whole):
        self.net, self.whole = net, whole
        self.a = self.piece(net.s, 0, net.right)
        self.b = self.piece(net.s, 1, net.left)
        own = whole.at[net.s]
        self.z = net.copy(own, own, net.across)
        self.more = [self.piece(net.s, 1, net.right), self.piece(net.s, 0, net.left)]

    def piece(self, block, second, to):
        part = self.whole.at[block, :, pl.ds(second * HALF, HALF)]
        return self.net.copy(part, part, to)

    def relay_one(self):
        net = self.net
        self.a.wait_recv()
        self.c = self.piece(net.at(net.h, net.x + 3), 0, net.right)
        self.b.wait_recv()
        self.d = self.piece(net.at(net.h, net.x + 1), 1, net.left)

    def relay_two(self):
        net = self.net
        self.z.wait_recv()
        part = self.whole.at[net.at(1 - net.h, net.x)]
        self.rest = [net.copy(part, part, net.right), net.copy(part, part, net.left)]
        block = net.at(net.h, net.x + 2)
        self.c.wait_recv()
        self.rest.append(self.piece(block, 0, net.across))
        self.d.wait_recv()
        self.rest.append(self.piece(block, 1, net.across))

    def row(self):
        for made in self.more:
            made.wait_recv()

    def finish(self):
        for made in self.rest:
            made.wait_recv()


class Scatter:
    def __init__(self, net, part, hop, side, near, far, passed, kept, came):
        self.net, self.part, self.hop_in, self.side_in = net, part, hop, side
        self.near_in, self.far_in, self.passed, self.kept, self.came = near, far, passed, kept, came
        self.one, self.two = pl.ds(0, HALF), pl.ds(HALF, HALF)
        h, x = net.h, net.x
        self.own, self.facing = net.s, net.at(h, x + 2)
        self.right, self.left = net.at(h, x + 1), net.at(h, x + 3)
        self.other = [net.at(1 - h, x + k) for k in range(4)]

    def hop(self):
        self.hopped = self.net.copy(self.part.at[self.other[2]], self.hop_in, self.net.across)

    def side(self):
        net, part = self.net, self.part
        self.sides = [
            net.copy(part.at[self.other[1]], self.side_in.at[0], net.right),
            net.copy(part.at[self.other[3]], self.side_in.at[1], net.left),
        ]

    def near(self):
        net, part = self.net, self.part
        self.nears = [
            net.copy(part.at[self.right, :, self.two], self.near_in.at[0], net.right),
            net.copy(part.at[self.left, :, self.one], self.near_in.at[1], net.left),
        ]

    def far(self):
        net, hop = self.net, self.hop_in
        self.hopped.wait_recv()
        hop[...] = add(hop[...], self.part[self.facing]).astype(BF16)
        self.fars = [
            net.copy(hop.at[:, self.one], self.far_in.at[0], net.right),
            net.copy(hop.at[:, self.two], self.far_in.at[1], net.left),
        ]

    def over(self):
        for made in self.sides:
            made.wait_recv()
        self.kept[...] = add(
            self.part[self.other[0]], self.side_in[0], self.side_in[1]
        ).astype(BF16)
        self.crossed = self.net.copy(self.kept, self.came, self.net.across)

    def relay(self):
        net, part, far = self.net, self.part, self.far_in
        self.fars[0].wait_recv()
        far[0] = add(far[0], part[self.right, :, self.one]).astype(BF16)
        passes = [net.copy(far.at[0], self.passed.at[0], net.right)]
        self.fars[1].wait_recv()
        far[1] = add(far[1], part[self.left, :, self.two]).astype(BF16)
        passes.append(net.copy(far.at[1], self.passed.at[1], net.left))
        self.last = [*self.nears, *passes, self.crossed]

    def finish(self):
        for made in self.last:
            made.wait_recv()
        part, near, passed, came = self.part, self.near_in, self.passed, self.came
        one, two = self.one, self.two
        return jnp.concatenate(
            [
                add(part[self.own, :, one], passed[0], near[1], came[:, one]),
                add(part[self.own, :, two], passed[1], near[0], came[:, two]),
            ],
            axis=1,
        )


class Reduce:
    def __init__(self, net, grad, pair, ring, out, turned=None):
        self.net, self.grad, self.out, self.turned = net, grad, out, turned
        self.sent, self.work = pair
        *self.three, self.kept, self.came = ring
        self.mine = pl.ds(net.core * 4, 4)
        self.q = net.core * 4 + net.y
        self.at_up, self.at_facing, self.at_down = (lax.rem(net.y + k, 4) for k in (1, 2, 3))

    def core(self):
        net = self.net
        self.moved = net.copy(self.grad.at[pl.ds((1 - net.core) * 4, 4)], self.sent, net.twin)

    def ring(self):
        net, work = self.net, self.work
        self.moved.wait_recv()
        work[...] = add(self.grad[self.mine], self.sent[...]).astype(BF16)
        steps = ((self.at_up, net.up), (self.at_down, net.down), (self.at_facing, net.facing))
        self.nears = [
            net.copy(work.at[block], there, to) for there, (block, to) in zip(self.three, steps)
        ]

    def beside(self):
        net = self.net
        for made in self.nears:
            made.wait_recv()
        three = [part[...] for part in self.three]
        self.kept[...] = add(self.work[net.y], *three).astype(BF16)
        self.over = net.copy(self.kept, self.came, net.beside)

    def place(self, q, eighths=1):
        rows = self.out.shape[0] // 8
        return pl.ds(pl.multiple_of(q * rows, 16), rows * eighths)

    def cross(self):
        net = self.net
        self.over.wait_recv()
        total = add(self.kept[...], self.came[...]).astype(BF16)
        if self.turned is None:
            self.out[self.place(self.q)] = total
            return
        away, back = self.turned
        away[...] = total.reshape(away.shape)
        self.crossed = [
            net.copy(away.at[to["shard"]], back.at[net.s], to) for to in net.peers
        ]
        back[net.s] = away[net.s]

    def back(self):
        net, out = self.net, self.out
        own = self.place(self.q)
        if self.turned is not None:
            for made in self.crossed:
                made.wait_recv()
            incoming = self.turned[1]
            blocks = [incoming[t] for t in range(8)]
            width = blocks[0].shape[-1]
            for i in range(width // 128 if width == 384 else 1):
                size = 128 if width == 384 else width
                for t in range(8):
                    at = i * D + t * size
                    out[own, at : at + size] = blocks[t][:, i * 128 : i * 128 + size]
        part = out.at[own]
        self.shared = [net.copy(part, part, to) for to in (net.up, net.down, net.facing)]

    def swap(self):
        for made in self.shared:
            made.wait_recv()
        part = self.out.at[self.place(self.net.core * 4, 4)]
        self.ended = self.net.copy(part, part, self.net.twin)

    def end(self):
        self.ended.wait_recv()


def layer_kernel(*refs):
    layer_steps(*refs[:2], refs[2:8], *refs[8:])


def layer_steps(
    tokens,
    cotangent,
    singles,
    query_bias,
    value_bias,
    up_bias,
    qkv_weight,
    up_weight,
    out_weight,
    down_weight,
    block_out,
    input_grad,
    down_sum,
    out_sum,
    up_sum,
    qkv_sum,
    small_sum,
    down_grad,
    out_grad,
    up_grad,
    qkv_grad,
    wide_vectors,
    vectors,
    all_vectors,
    columns,
    first,
    cot,
    second,
    branch,
    mixed,
    qkv_low,
    heads,
    lse,
    attended,
    active,
    grad_upper,
    grad_qkv,
    resid_ref,
    grad_resid_ref,
    small,
    fours,
    fours_in,
    parts,
    hop,
    side,
    near,
    far,
    passed,
    kept,
    came,
    small_low,
    small_ring,
    down_pair,
    down_ring,
    out_pair,
    out_ring,
    up_pair,
    up_ring,
    up_turned,
    qkv_pair,
    qkv_ring,
    qkv_turned,
    send,
    recv,
):
    net = Net(send, recv)
    s, core = net.s, net.core
    net.barrier([*net.peers, *net.replicas])

    def reduce(grad, pair, ring, out, turned=None):
        split = lambda ref, n: [ref.at[i] for i in range(n)]
        turned = None if turned is None else split(turned, 2)
        return Reduce(net, grad, split(pair, 2), split(ring, 5), out, turned)

    down_all = reduce(down_grad, down_pair, down_ring, down_sum)
    out_all = reduce(out_grad, out_pair, out_ring, out_sum)
    up_all = reduce(up_grad, up_pair, up_ring, up_sum, up_turned)
    qkv_all = reduce(qkv_grad, qkv_pair, qkv_ring, qkv_sum, qkv_turned)
    mine = pl.ds(pl.multiple_of(core * 64, 64), 64)
    sixteen = pl.ds(pl.multiple_of(core * 64 + net.y * 16, 16), 16)

    def scatter(i):
        buffers = (hop, side, near, far, passed, kept, came)
        return Scatter(net, parts.at[i % 3], *(buffer.at[i] for buffer in buffers))

    def each(work, least, end, carry=0):
        def step(i, carry):
            row, j = i // 4, lax.rem(i, 4)
            same = j + j // 2 - 2 * (j // 3)
            cross = lax.rem(2 * j, 3) + 3 * (j // 3)
            h = net.h + row - 2 * net.h * row
            return work(net.at(h, net.x + (1 - row) * same + row * cross), carry)

        return lax.fori_loop(least, end, step, carry)

    def each_sent(rs, work, carry):
        carry = each(work, 5, 6, carry)
        rs.hop()
        carry = each(work, 6, 8, carry)
        rs.side()
        carry = each(work, 1, 3, carry)
        rs.near()
        carry = each(work, 3, 5, carry)
        rs.far()
        return each(work, 0, 1, carry)

    wide_vectors[...] = jnp.zeros_like(wide_vectors)
    for k, single in enumerate(singles):
        wide_vectors[k : k + 1, :] = single[...].astype(F32)
    vectors[...] = wide_vectors[...].astype(BF16)
    vec = [net.copy(vectors, all_vectors.at[s], to) for to in net.peers]
    all_vectors[s] = vectors[...]
    cot[s] = cotangent[...]
    qkv_in, up_in = [], []
    thirds = [
        lambda t, i=i: qkv_weight.at[sixteen, pl.ds(pl.multiple_of(i * D + t * 128, 128), 128)]
        for i in range(3)
    ]
    quarter = lambda t: up_weight.at[sixteen, pl.ds(pl.multiple_of(t * 512, 512), 512)]
    for to in net.peers:
        for i in range(3):
            there = columns.at[s, sixteen, pl.ds(i * 128, 128)]
            qkv_in.append(net.copy(thirds[i](to["shard"]), there, to))
    for to in net.peers:
        there = columns.at[s, sixteen, pl.ds(384, 512)]
        up_in.append(net.copy(quarter(to["shard"]), there, to))
    for i in range(3):
        columns[s, sixteen, i * 128 : (i + 1) * 128] = thirds[i](s)[...]
    columns[s, sixteen, 384:896] = quarter(s)[...]

    def share(arrived, at):
        for made in arrived:
            made.wait_recv()
        part = columns.at[:, sixteen, at]
        return [net.copy(part, part, to) for to in (net.up, net.down, net.facing)]

    def share_twin(arrived, at):
        for made in arrived:
            made.wait_recv()
        part = columns.at[:, mine, at]
        return net.copy(part, part, net.twin)

    x = tokens[...].astype(F32)
    unit1, inverse1 = norm_unit(x)
    for made in vec:
        made.wait_recv()
    table = [all_vectors[j].astype(F32) for j in range(8)]
    gain1, shift1, gain2, shift2, bias_out, bias_down = (
        jnp.concatenate([t[i : i + 1] for t in table], axis=1) for i in range(6)
    )
    first[s] = (unit1 * gain1 + shift1).astype(BF16)
    ag = Gather(net, first)
    qkv_at, up_at = pl.ds(0, 384), pl.ds(384, 512)
    qkv_in = share(qkv_in, qkv_at)
    ag.relay_one()
    up_in = share(up_in, up_at)
    ag.relay_two()
    qkv_pass = share_twin(qkv_in, qkv_at)
    qkv_bias = jnp.concatenate(
        [query_bias[...].astype(F32), jnp.zeros((1, 128), F32), value_bias[...].astype(F32)], axis=1
    )
    up_bias = up_bias[...].astype(F32)
    up_bias = jnp.concatenate([up_bias[k : k + 1] for k in range(4)], axis=1)
    qkv_pass.wait_recv()
    ag.row()

    def project(b, carry):
        value = dot(first[b], columns[:, :, 0:384].reshape(D, 384)) + qkv_bias
        at = pl.multiple_of(b * 72, 8)
        mixed[0, pl.ds(at, 72), :] = value[0:72]
        mixed[1, pl.ds(at, 72), :] = value[72:144]
        return carry

    each(project, 0, 5)
    ag.finish()
    ag_cot = Gather(net, cot)
    each(project, 5, 8)
    qkv_low[...] = mixed[...].astype(BF16)
    ag_cot.relay_one()

    def attend(image, carry):
        q, k, v = (qkv_low[image, :, i * 128 : (i + 1) * 128] for i in range(3))
        zero = jnp.zeros_like(q)
        total = jnp.zeros(q.shape, F32)
        for h, mask in enumerate(head_masks(q.shape)):
            score = dot_last(jnp.where(mask, q, zero), k) * SCALE
            top = jnp.max(score, -1, keepdims=True)
            e = jnp.exp(score - top)
            row = jnp.sum(e, -1, keepdims=True)
            p = (e * (1.0 / row)).astype(BF16)
            total += dot(p, jnp.where(mask, v, zero))
            lse[image, :, h : h + 1] = top + jnp.log(row)
        heads[image] = total
        return carry

    lax.fori_loop(0, 2, attend, 0)
    up_pass = share_twin(up_in, up_at)

    def by_device(ref, b):
        at = pl.multiple_of(b * 72, 8)
        both = [ref[i, pl.ds(at, 72), :] for i in range(2)]
        return jnp.concatenate(both, axis=0).astype(BF16)

    def outward(b, carry):
        value = by_device(heads, b)
        attended[b] = value
        parts[0, b] = dot(value, out_weight[...]).astype(BF16)
        return carry

    rs = rs_branch = scatter(0)
    each_sent(rs, outward, 0)
    rs.over()
    rs.relay()
    ag_cot.relay_two()
    resid = tokens[...].astype(F32) + (rs.finish() + bias_out)
    resid_ref[...] = resid
    unit2, inverse2 = norm_unit(resid)
    second[s] = (unit2 * gain2 + shift2).astype(BF16)
    ag = Gather(net, second)
    up_pass.wait_recv()

    def feed(b, total):
        up = columns[:, :, 384:896].reshape(D, 512)
        u = dot(second[b], up) + up_bias
        square = u * u
        t = jnp.tanh(GELU * (u + 0.044715 * u * square))
        act = (0.5 * u * (1.0 + t)).astype(BF16)
        slope = 0.5 * (1.0 + t) + (0.5 * GELU) * u * (1.0 - t * t) * (
            1.0 + 0.134145 * square
        )
        active[b] = act
        gu = (dot_last(cot[b], down_weight[...]) * slope).astype(BF16)
        grad_upper[b] = gu
        parts[1, b] = dot_last(gu, up).astype(BF16)
        parts[2, b] = dot(act, down_weight[...]).astype(BF16)
        return total + jnp.sum(gu.astype(F32), 0, keepdims=True)

    ag.relay_one()
    ag_cot.row()
    ag_cot.finish()
    up_bias_grad = each(feed, 0, 1, jnp.zeros((1, 512), F32))
    ag.relay_two()
    ag.row()
    up_bias_grad = each(feed, 1, 5, up_bias_grad)
    ag.finish()
    rs = scatter(1)
    up_bias_grad = each(feed, 5, 6, up_bias_grad)
    rs.hop()
    up_bias_grad = each(feed, 6, 8, up_bias_grad)
    rs.side()
    rs.near()
    own = pl.ds(pl.multiple_of(s * 128, 128), 128)
    small[...] = jnp.zeros_like(small)
    for i in range(4):
        small[8 + i : 9 + i, :] = up_bias_grad[:, i * 128 : (i + 1) * 128]
    small[7:8, :] = jnp.sum(cot[:, :, own].astype(F32).reshape(1152, 128), 0, keepdims=True)

    def down_tile(i):
        at = pl.ds(i * 256, 256)
        value = dot_first(
            active[...].reshape(1152, 512), cot[:, :, at].reshape(1152, 256)
        ).astype(BF16)
        for q in range(8):
            down_grad[q, :, at] = value[q * 64 : (q + 1) * 64]

    down_tile(0)
    rs.far()
    down_tile(1)
    rs.over()
    rs.relay()
    down_tile(2)
    down_tile(3)
    down_all.core()
    grad_second = rs.finish()
    unit2, inverse2 = norm_unit(resid_ref[...])
    grad_resid = cotangent[...].astype(F32) + norm_back(grad_second, unit2, inverse2, gain2)
    grad_resid_ref[...] = grad_resid
    branch[s] = grad_resid.astype(BF16)
    ag = Gather(net, branch)
    gain2_grad = jnp.sum(grad_second * unit2, 0, keepdims=True)
    shift2_grad = jnp.sum(grad_second, 0, keepdims=True)

    def up_tile(i):
        value = dot_first(
            second[:, :, i * 256 : (i + 1) * 256].reshape(1152, 256),
            grad_upper[...].reshape(1152, 512),
        ).astype(BF16)
        for j in range(2):
            for q in range(8):
                up_grad[q, (2 * i + j) * 16 : (2 * i + j + 1) * 16, :] = value[
                    j * 128 + q * 16 : j * 128 + (q + 1) * 16
                ]

    def back_heads(b, carry):
        value = dot_last(branch[b], out_weight[...])
        at = pl.multiple_of(b * 72, 8)
        heads[0, pl.ds(at, 72), :] = value[0:72]
        heads[1, pl.ds(at, 72), :] = value[72:144]
        return carry

    ag.relay_one()
    down_all.ring()
    up_tile(0)
    ag.relay_two()
    up_tile(1)
    ag.row()
    up_tile(2)
    up_tile(3)
    up_all.core()
    each(back_heads, 0, 5)
    ag.finish()
    rs_out = scatter(2)
    rs_out.hop()
    rs_out.side()
    rs_out.near()
    down_all.beside()
    each(back_heads, 5, 8)
    def attend_back(image, carry):
        q, k, v = (qkv_low[image, :, i * 128 : (i + 1) * 128] for i in range(3))
        grad = heads[image].astype(BF16)
        zero = jnp.zeros_like(q)
        dq = jnp.zeros(q.shape, F32)
        dk, dv = dq, dq
        for h, mask in enumerate(head_masks(q.shape)):
            qh, kh, gh = (jnp.where(mask, a, zero) for a in (q, k, grad))
            p = jnp.exp(dot_last(qh, k) * SCALE - lse[image, :, h : h + 1])
            dp = dot_last(gh, v)
            inner = jnp.sum(p * dp, -1, keepdims=True)
            ds = (p * (dp - inner)).astype(BF16)
            dq += dot(ds, kh)
            dk += dot_first(ds, qh)
            dv += dot_first(p.astype(BF16), gh)
        mixed[image, :, 0:128] = dq * SCALE
        mixed[image, :, 128:256] = dk * SCALE
        mixed[image, :, 256:384] = dv
        return carry

    lax.fori_loop(0, 1, attend_back, 0)
    up_all.ring()
    rs_out.far()
    down_all.cross()
    down_all.back()
    lax.fori_loop(1, 2, attend_back, 0)
    rs_out.over()

    def back_first(b, total):
        value = by_device(mixed, b)
        grad_qkv[b] = value
        parts[0, b] = dot_last(value, columns[:, :, 0:384].reshape(D, 384)).astype(BF16)
        return total + jnp.sum(value.astype(F32), 0, keepdims=True)

    net.settle([rs_branch.hopped, *rs_branch.sides, *rs_branch.nears])
    rs = scatter(3)
    qkv_bias_grad = each_sent(rs, back_first, jnp.zeros((1, 384), F32))
    small[4:5, :] = qkv_bias_grad[:, 0:128]
    small[5:6, :] = qkv_bias_grad[:, 256:384]
    small[6:7, :] = jnp.sum(branch[:, :, own].astype(F32).reshape(1152, 128), 0, keepdims=True)

    def qkv_tile(i):
        value = dot_first(
            first[:, :, i * 256 : (i + 1) * 256].reshape(1152, 256),
            grad_qkv[...].reshape(1152, 384),
        ).astype(BF16)
        for j in range(2):
            for q in range(8):
                qkv_grad[q, (2 * i + j) * 16 : (2 * i + j + 1) * 16, :] = value[
                    j * 128 + q * 16 : j * 128 + (q + 1) * 16
                ]

    qkv_tile(0)
    qkv_tile(1)
    qkv_tile(2)
    qkv_tile(3)
    qkv_all.core()
    rs_out.relay()
    up_all.beside()
    rs.over()
    qkv_all.ring()
    value = dot_first(attended[...].reshape(1152, 128), branch[...].reshape(1152, D)).astype(BF16)
    for q in range(8):
        out_grad[q] = value[q * 16 : (q + 1) * 16]
    out_all.core()
    rs.relay()
    up_all.cross()
    down_all.swap()
    qkv_all.beside()
    out_all.ring()
    up_all.back()
    grad_first = rs.finish()
    unit1, inverse1 = norm_unit(tokens[...].astype(F32))
    gain1_grad = jnp.sum(grad_first * unit1, 0, keepdims=True)
    shift1_grad = jnp.sum(grad_first, 0, keepdims=True)
    four = jnp.concatenate(
        [gain1_grad, shift1_grad, gain2_grad, shift2_grad, jnp.zeros((12, D), F32)], axis=0
    ).astype(BF16)
    for t in range(8):
        fours[t] = four[:, t * 128 : (t + 1) * 128]
    moved = [net.copy(fours.at[to["shard"]], fours_in.at[s], to) for to in net.peers]
    fours_in[s] = fours[s]
    qkv_all.cross()
    out_all.beside()
    input_grad[...] = (
        grad_resid_ref[...] + norm_back(grad_first, unit1, inverse1, gain1)
    ).astype(BF16)
    for made in moved:
        made.wait_recv()
    total = jnp.sum(fours_in[...].astype(F32), 0)
    small[0:4, :] = total[0:4]
    small_low[...] = small[...].astype(BF16)
    moved = [net.copy(small_low, small_ring.at[net.r], to) for to in net.replicas]
    small_ring[net.r] = small_low[...]
    qkv_all.back()
    out_all.cross()
    out_all.back()
    up_all.swap()
    block_out[...] = (resid_ref[...] + (rs_out.finish() + bias_down)).astype(BF16)
    for made in moved:
        made.wait_recv()
    small_sum[...] = add(*(small_ring[k] for k in range(16)))
    qkv_all.swap()
    out_all.swap()
    for every in (down_all, out_all, up_all, qkv_all):
        every.end()
    net.drain()


def layer(*arguments):
    vmem = lambda *shape: pltpu.VMEM(shape, BF16)
    wide = lambda *shape: pltpu.VMEM(shape, F32)
    space = pl.BlockSpec(memory_space=pltpu.VMEM)
    shape = lambda *sizes: jax.ShapeDtypeStruct(sizes, BF16)
    return pl.pallas_call(
        layer_kernel,
        out_shape=[
            shape(ROWS, D),
            shape(ROWS, D),
            shape(512, D),
            shape(128, D),
            shape(128, 4096),
            shape(128, 3 * D),
            jax.ShapeDtypeStruct((16, 128), F32),
        ],
        in_specs=[space] * 15,
        out_specs=[space] * 7,
        scratch_shapes=[
            vmem(8, 64, D),
            vmem(8, 16, D),
            vmem(8, 128, 512),
            vmem(8, 128, 384),
            wide(16, 128),
            vmem(16, 128),
            vmem(8, 16, 128),
            vmem(8, 128, 896),
            vmem(8, ROWS, D),
            vmem(8, ROWS, D),
            vmem(8, ROWS, D),
            vmem(8, ROWS, D),
            wide(2, 576, 384),
            vmem(2, 576, 384),
            wide(2, 576, 128),
            wide(2, 576, 128),
            vmem(8, ROWS, 128),
            vmem(8, ROWS, 512),
            vmem(8, ROWS, 512),
            vmem(8, ROWS, 384),
            wide(ROWS, D),
            wide(ROWS, D),
            wide(16, 128),
            vmem(8, 16, 128),
            vmem(8, 16, 128),
            vmem(3, 8, ROWS, D),
            vmem(4, ROWS, D),
            vmem(4, 2, ROWS, D),
            vmem(4, 2, ROWS, HALF),
            vmem(4, 2, ROWS, HALF),
            vmem(4, 2, ROWS, HALF),
            vmem(4, ROWS, D),
            vmem(4, ROWS, D),
            vmem(16, 128),
            vmem(16, 16, 128),
            vmem(2, 4, 64, D),
            vmem(5, 64, D),
            vmem(2, 4, 16, D),
            vmem(5, 16, D),
            vmem(2, 4, 128, 512),
            vmem(5, 128, 512),
            vmem(2, 8, 16, 512),
            vmem(2, 4, 128, 384),
            vmem(5, 128, 384),
            vmem(2, 8, 16, 384),
            pltpu.SemaphoreType.DMA((240,)),
            pltpu.SemaphoreType.DMA((240,)),
        ],
        name="layer",
        cost_estimate=pl.CostEstimate(
            flops=11 * 10**9, bytes_accessed=12 * 10**6, transcendentals=0
        ),
        compiler_params=pltpu.CompilerParams(
            collective_id=1, has_side_effects=True, vmem_limit_bytes=62 << 20
        ),
    )(*arguments)


def cast_kernel(down, out, up, qkv, small, *outs):
    for source, target in zip((down, out, up, qkv), outs[:4]):
        target[...] = source[...].astype(F32)
    for k, target in enumerate(outs[4:12]):
        target[...] = small[k]
    for k in range(4):
        outs[12][k * 128 : (k + 1) * 128] = small[8 + k]


def cast(down, out, up, qkv, small):
    steps = 1
    block = lambda a: pl.BlockSpec((a.shape[0] // steps, a.shape[1]), lambda i: (i, 0))
    whole = lambda *sizes: pl.BlockSpec(sizes, lambda i: (0,) * len(sizes))
    shape = lambda *sizes: jax.ShapeDtypeStruct(sizes, F32)
    large = (down, out, up, qkv)
    return pl.pallas_call(
        cast_kernel,
        grid=(steps,),
        out_shape=[
            *(shape(*a.shape) for a in large),
            *(shape(128) for _ in range(8)),
            shape(512),
        ],
        in_specs=[*map(block, large), whole(16, 128)],
        out_specs=[*map(block, large), *(whole(128) for _ in range(8)), whole(512)],
        name="cast",
        compiler_params=pltpu.CompilerParams(vmem_limit_bytes=62 << 20),
    )(*large, small)


def body(
    tokens,
    cotangent,
    attn_gain,
    attn_shift,
    qkv_weight,
    query_bias,
    value_bias,
    out_weight,
    out_bias,
    mlp_gain,
    mlp_shift,
    up_weight,
    up_bias,
    down_weight,
    down_bias,
):
    vectors = (attn_gain, attn_shift, mlp_gain, mlp_shift, out_bias, down_bias)
    vectors = (*vectors, query_bias, value_bias, up_bias)
    block_out, input_grad, *sums = layer(
        tokens.reshape(ROWS, D),
        cotangent.reshape(ROWS, D),
        *(a.reshape(-1, 128) for a in vectors),
        qkv_weight,
        up_weight,
        out_weight,
        down_weight,
    )
    down_grad, out_grad, up_grad, qkv_grad, *small, up_bias_grad = cast(*sums)
    return (
        block_out.reshape(2, 72, D),
        input_grad.reshape(2, 72, D),
        small[0],
        small[1],
        qkv_grad,
        small[4],
        small[5],
        out_grad,
        small[6],
        small[2],
        small[3],
        up_grad,
        up_bias_grad,
        down_grad,
        small[7],
    )


def solution(mesh):
    row, cube, flat = P("shard"), P("replica", "shard", None), P("shard", None)
    return jax.shard_map(
        body,
        mesh=mesh,
        in_specs=(cube, cube, row, row, flat, row, row, flat, row, row, row, flat, row, flat, row),
        out_specs=(cube, cube, row, row, flat, row, row, flat, row, row, row, flat, row, flat, row),
        check_vma=False,
    )
```

```python
import jax
import jax.numpy as jnp
from jax import lax
from jax.experimental import pallas as pl
from jax.experimental.pallas import tpu as pltpu
from jax.sharding import PartitionSpec as P

HEAD_DIM = 64
EPS = 1e-06
F32 = jnp.float32
BF16 = jnp.bfloat16
SCALE = HEAD_DIM ** (-0.5)
MESH = pl.DeviceIdType.MESH
D = 1024
ROWS = 144
HALF = 512
GELU = 0.7978845608028654


def dot(a, b):
    return lax.dot_general(a, b, (((1,), (0,)), ((), ())), preferred_element_type=F32)


def dot_last(a, b):
    return lax.dot_general(a, b, (((1,), (1,)), ((), ())), preferred_element_type=F32)


def dot_first(a, b):
    return lax.dot_general(a, b, (((0,), (0,)), ((), ())), preferred_element_type=F32)


def norm_unit(v):
    mean = jnp.mean(v, -1, keepdims=True)
    centred = v - mean
    inverse = lax.rsqrt(jnp.mean(centred * centred, -1, keepdims=True) + EPS)
    return centred * inverse, inverse


def norm_back(grad, unit, inverse, gain):
    gn = grad * gain
    inner = jnp.mean(gn * unit, -1, keepdims=True)
    return inverse * (gn - jnp.mean(gn, -1, keepdims=True) - unit * inner)


def head_masks(shape):
    low = lax.broadcasted_iota(jnp.int32, shape, 1) < HEAD_DIM
    return (low, jnp.logical_not(low))


def add(*terms):
    total = terms[0].astype(F32)
    for term in terms[1:]:
        total = total + term.astype(F32)
    return total


class Net:
    def __init__(self, send, recv):
        self.send, self.recv, self.count, self.open = send, recv, 0, []
        self.s = lax.axis_index("shard")
        self.h, self.x = self.s // 4, lax.rem(self.s, 4)
        r = lax.axis_index("replica")
        self.core, self.y = lax.rem(r, 2), lax.rem(r // 2, 4)
        zlow = r // 8
        base = r - self.y * 2
        self.right = {"shard": self.at(self.h, self.x + 1)}
        self.left = {"shard": self.at(self.h, self.x + 3)}
        self.across = {"shard": self.at(1 - self.h, self.x)}
        self.twin = {"replica": r + 1 - 2 * self.core}
        self.up = {"replica": base + lax.rem(self.y + 1, 4) * 2}
        self.down = {"replica": base + lax.rem(self.y + 3, 4) * 2}
        self.facing = {"replica": base + lax.rem(self.y + 2, 4) * 2}
        self.beside = {"replica": r + 8 - 16 * zlow}
        self.replicas = [{"replica": lax.rem(r + k, 16)} for k in range(1, 16)]
        self.r = r
        self.peers = [{"shard": lax.rem(self.s + k, 8)} for k in range(1, 8)]

    def at(self, h, x):
        return h * 4 + lax.rem(x, 4)

    def copy(self, src, dst, to):
        i = self.count
        self.count += 1
        made = pltpu.make_async_remote_copy(
            src_ref=src,
            dst_ref=dst,
            send_sem=self.send.at[i],
            recv_sem=self.recv.at[i],
            device_id=to,
            device_id_type=MESH,
        )
        made.start()
        self.open.append(made)
        return made

    def drain(self):
        for made in self.open:
            made.wait_send()
        self.open = []

    def settle(self, copies):
        for made in copies:
            made.wait_send()
            self.open = [other for other in self.open if other is not made]

    def barrier(self, others):
        semaphore = pltpu.get_barrier_semaphore()
        for other in others:
            pl.semaphore_signal(semaphore, inc=1, device_id=other, device_id_type=MESH)
        pl.semaphore_wait(semaphore, len(others))


class Gather:
    def __init__(self, net, whole):
        self.net, self.whole = net, whole
        self.a = self.piece(net.s, 0, net.right)
        self.b = self.piece(net.s, 1, net.left)
        own = whole.at[net.s]
        self.z = net.copy(own, own, net.across)
        self.more = [self.piece(net.s, 1, net.right), self.piece(net.s, 0, net.left)]

    def piece(self, block, second, to):
        part = self.whole.at[block, :, pl.ds(second * HALF, HALF)]
        return self.net.copy(part, part, to)

    def relay_one(self):
        net = self.net
        self.a.wait_recv()
        self.c = self.piece(net.at(net.h, net.x + 3), 0, net.right)
        self.b.wait_recv()
        self.d = self.piece(net.at(net.h, net.x + 1), 1, net.left)

    def relay_two(self):
        net = self.net
        self.z.wait_recv()
        part = self.whole.at[net.at(1 - net.h, net.x)]
        self.rest = [net.copy(part, part, net.right), net.copy(part, part, net.left)]
        block = net.at(net.h, net.x + 2)
        self.c.wait_recv()
        self.rest.append(self.piece(block, 0, net.across))
        self.d.wait_recv()
        self.rest.append(self.piece(block, 1, net.across))

    def row(self):
        for made in self.more:
            made.wait_recv()

    def finish(self):
        for made in self.rest:
            made.wait_recv()


class Scatter:
    def __init__(self, net, part, hop, side, near, far, passed, kept, came):
        self.net, self.part, self.hop_in, self.side_in = net, part, hop, side
        self.near_in, self.far_in, self.passed, self.kept, self.came = near, far, passed, kept, came
        self.one, self.two = pl.ds(0, HALF), pl.ds(HALF, HALF)
        h, x = net.h, net.x
        self.own, self.facing = net.s, net.at(h, x + 2)
        self.right, self.left = net.at(h, x + 1), net.at(h, x + 3)
        self.other = [net.at(1 - h, x + k) for k in range(4)]

    def hop(self):
        self.hopped = self.net.copy(self.part.at[self.other[2]], self.hop_in, self.net.across)

    def side(self):
        net, part = self.net, self.part
        self.sides = [
            net.copy(part.at[self.other[1]], self.side_in.at[0], net.right),
            net.copy(part.at[self.other[3]], self.side_in.at[1], net.left),
        ]

    def near(self):
        net, part = self.net, self.part
        self.nears = [
            net.copy(part.at[self.right, :, self.two], self.near_in.at[0], net.right),
            net.copy(part.at[self.left, :, self.one], self.near_in.at[1], net.left),
        ]

    def far(self):
        net, hop = self.net, self.hop_in
        self.hopped.wait_recv()
        hop[...] = add(hop[...], self.part[self.facing]).astype(BF16)
        self.fars = [
            net.copy(hop.at[:, self.one], self.far_in.at[0], net.right),
            net.copy(hop.at[:, self.two], self.far_in.at[1], net.left),
        ]

    def over(self):
        for made in self.sides:
            made.wait_recv()
        self.kept[...] = add(
            self.part[self.other[0]], self.side_in[0], self.side_in[1]
        ).astype(BF16)
        self.crossed = self.net.copy(self.kept, self.came, self.net.across)

    def relay(self):
        net, part, far = self.net, self.part, self.far_in
        self.fars[0].wait_recv()
        far[0] = add(far[0], part[self.right, :, self.one]).astype(BF16)
        passes = [net.copy(far.at[0], self.passed.at[0], net.right)]
        self.fars[1].wait_recv()
        far[1] = add(far[1], part[self.left, :, self.two]).astype(BF16)
        passes.append(net.copy(far.at[1], self.passed.at[1], net.left))
        self.last = [*self.nears, *passes, self.crossed]

    def finish(self):
        for made in self.last:
            made.wait_recv()
        part, near, passed, came = self.part, self.near_in, self.passed, self.came
        one, two = self.one, self.two
        return jnp.concatenate(
            [
                add(part[self.own, :, one], passed[0], near[1], came[:, one]),
                add(part[self.own, :, two], passed[1], near[0], came[:, two]),
            ],
            axis=1,
        )


class Reduce:
    def __init__(self, net, grad, pair, ring, out, turned=None):
        self.net, self.grad, self.out, self.turned = net, grad, out, turned
        self.sent, self.work = pair
        *self.three, self.kept, self.came = ring
        self.mine = pl.ds(net.core * 4, 4)
        self.q = net.core * 4 + net.y
        self.at_up, self.at_facing, self.at_down = (lax.rem(net.y + k, 4) for k in (1, 2, 3))

    def core(self):
        net = self.net
        self.moved = net.copy(self.grad.at[pl.ds((1 - net.core) * 4, 4)], self.sent, net.twin)

    def ring(self):
        net, work = self.net, self.work
        self.moved.wait_recv()
        work[...] = add(self.grad[self.mine], self.sent[...]).astype(BF16)
        steps = ((self.at_up, net.up), (self.at_down, net.down), (self.at_facing, net.facing))
        self.nears = [
            net.copy(work.at[block], there, to) for there, (block, to) in zip(self.three, steps)
        ]

    def beside(self):
        net = self.net
        for made in self.nears:
            made.wait_recv()
        three = [part[...] for part in self.three]
        self.kept[...] = add(self.work[net.y], *three).astype(BF16)
        self.over = net.copy(self.kept, self.came, net.beside)

    def place(self, q, eighths=1):
        rows = self.out.shape[0] // 8
        return pl.ds(pl.multiple_of(q * rows, 16), rows * eighths)

    def cross(self):
        net = self.net
        self.over.wait_recv()
        total = add(self.kept[...], self.came[...]).astype(BF16)
        if self.turned is None:
            self.out[self.place(self.q)] = total
            return
        away, back = self.turned
        away[...] = total.reshape(away.shape)
        self.crossed = [
            net.copy(away.at[to["shard"]], back.at[net.s], to) for to in net.peers
        ]
        back[net.s] = away[net.s]

    def back(self):
        net, out = self.net, self.out
        own = self.place(self.q)
        if self.turned is not None:
            for made in self.crossed:
                made.wait_recv()
            incoming = self.turned[1]
            blocks = [incoming[t] for t in range(8)]
            width = blocks[0].shape[-1]
            for i in range(width // 128 if width == 384 else 1):
                size = 128 if width == 384 else width
                for t in range(8):
                    at = i * D + t * size
                    out[own, at : at + size] = blocks[t][:, i * 128 : i * 128 + size]
        part = out.at[own]
        self.shared = [net.copy(part, part, to) for to in (net.up, net.down, net.facing)]

    def swap(self):
        for made in self.shared:
            made.wait_recv()
        part = self.out.at[self.place(self.net.core * 4, 4)]
        self.ended = self.net.copy(part, part, self.net.twin)

    def end(self):
        self.ended.wait_recv()


def layer_kernel(*refs):
    layer_steps(*refs[:2], refs[2:8], *refs[8:])


def layer_steps(
    tokens,
    cotangent,
    singles,
    query_bias,
    value_bias,
    up_bias,
    qkv_weight,
    up_weight,
    out_source,
    down_source,
    block_out,
    input_grad,
    down_sum,
    out_sum,
    up_sum,
    qkv_sum,
    small_sum,
    down_grad,
    out_grad,
    up_grad,
    qkv_grad,
    wide_vectors,
    vectors,
    all_vectors,
    columns,
    first,
    cot,
    second,
    branch,
    mixed,
    qkv_low,
    heads,
    lse,
    attended,
    active,
    grad_upper,
    grad_qkv,
    resid_ref,
    grad_resid_ref,
    small,
    fours,
    fours_in,
    parts,
    hop,
    side,
    near,
    far,
    passed,
    kept,
    came,
    small_low,
    small_ring,
    down_pair,
    down_ring,
    out_pair,
    out_ring,
    up_pair,
    up_ring,
    up_turned,
    qkv_pair,
    qkv_ring,
    qkv_turned,
    out_weight,
    down_weight,
    load,
    send,
    recv,
):
    net = Net(send, recv)
    s, core = net.s, net.core
    net.barrier([*net.peers, *net.replicas])

    def reduce(grad, pair, ring, out, turned=None):
        split = lambda ref, n: [ref.at[i] for i in range(n)]
        turned = None if turned is None else split(turned, 2)
        return Reduce(net, grad, split(pair, 2), split(ring, 5), out, turned)

    down_all = reduce(down_grad, down_pair, down_ring, down_sum)
    out_all = reduce(out_grad, out_pair, out_ring, out_sum)
    up_all = reduce(up_grad, up_pair, up_ring, up_sum, up_turned)
    qkv_all = reduce(qkv_grad, qkv_pair, qkv_ring, qkv_sum, qkv_turned)
    mine = pl.ds(pl.multiple_of(core * 64, 64), 64)
    sixteen = pl.ds(pl.multiple_of(core * 64 + net.y * 16, 16), 16)

    def scatter(i):
        buffers = (hop, side, near, far, passed, kept, came)
        return Scatter(net, parts.at[i % 3], *(buffer.at[i] for buffer in buffers))

    def each(work, least, end, carry=0):
        def step(i, carry):
            row, j = i // 4, lax.rem(i, 4)
            same = j + j // 2 - 2 * (j // 3)
            cross = lax.rem(2 * j, 3) + 3 * (j // 3)
            h = net.h + row - 2 * net.h * row
            return work(net.at(h, net.x + (1 - row) * same + row * cross), carry)

        return lax.fori_loop(least, end, step, carry)

    def each_sent(rs, work, carry, beside=None):
        carry = each(work, 5, 6, carry)
        rs.hop()
        carry = each(work, 6, 8, carry)
        rs.side()
        carry = each(work, 1, 3, carry)
        rs.near()
        carry = each(work, 3, 5, carry)
        if beside is None:
            rs.far()
            return each(work, 0, 1, carry)
        carry = each(work, 0, 1, carry)
        beside()
        rs.far()
        return carry

    wide_vectors[...] = jnp.zeros_like(wide_vectors)
    for k, single in enumerate(singles):
        wide_vectors[k : k + 1, :] = single[...].astype(F32)
    vectors[...] = wide_vectors[...].astype(BF16)
    vec = [net.copy(vectors, all_vectors.at[s], to) for to in net.peers]
    all_vectors[s] = vectors[...]
    cot[s] = cotangent[...]
    qkv_in, up_in = [], []
    thirds = [
        lambda t, i=i: qkv_weight.at[sixteen, pl.ds(pl.multiple_of(i * D + t * 128, 128), 128)]
        for i in range(3)
    ]
    quarter = lambda t: up_weight.at[sixteen, pl.ds(pl.multiple_of(t * 512, 512), 512)]
    for to in net.peers:
        for i in range(3):
            there = columns.at[s, sixteen, pl.ds(i * 128, 128)]
            qkv_in.append(net.copy(thirds[i](to["shard"]), there, to))
    for to in net.peers:
        there = columns.at[s, sixteen, pl.ds(384, 512)]
        up_in.append(net.copy(quarter(to["shard"]), there, to))
    loads = [
        (thirds[i](s), columns.at[s, sixteen, pl.ds(i * 128, 128)]) for i in range(3)
    ]
    loads += [
        (quarter(s), columns.at[s, sixteen, pl.ds(384, 512)]),
        (out_source, out_weight),
        (down_source, down_weight),
    ]
    loads = [pltpu.make_async_copy(*pair, load.at[i]) for i, pair in enumerate(loads)]
    for made in loads:
        made.start()

    def share(arrived, at):
        for made in arrived:
            made.wait_recv()
        part = columns.at[:, sixteen, at]
        return [net.copy(part, part, to) for to in (net.up, net.down, net.facing)]

    def share_twin(arrived, at):
        for made in arrived:
            made.wait_recv()
        part = columns.at[:, mine, at]
        return net.copy(part, part, net.twin)

    x = tokens[...].astype(F32)
    unit1, inverse1 = norm_unit(x)
    for made in vec:
        made.wait_recv()
    table = [all_vectors[j].astype(F32) for j in range(8)]
    gain1, shift1, gain2, shift2, bias_out, bias_down = (
        jnp.concatenate([t[i : i + 1] for t in table], axis=1) for i in range(6)
    )
    first[s] = (unit1 * gain1 + shift1).astype(BF16)
    ag = Gather(net, first)
    qkv_at, up_at = pl.ds(0, 384), pl.ds(384, 512)
    for made in loads[:4]:
        made.wait()
    qkv_in = share(qkv_in, qkv_at)
    ag.relay_one()
    up_in = share(up_in, up_at)
    ag.relay_two()
    qkv_pass = share_twin(qkv_in, qkv_at)
    qkv_bias = jnp.concatenate(
        [query_bias[...].astype(F32), jnp.zeros((1, 128), F32), value_bias[...].astype(F32)], axis=1
    )
    up_bias = up_bias[...].astype(F32)
    up_bias = jnp.concatenate([up_bias[k : k + 1] for k in range(4)], axis=1)
    qkv_pass.wait_recv()
    ag.row()

    def project(b, carry):
        value = dot(first[b], columns[:, :, 0:384].reshape(D, 384)) + qkv_bias
        at = pl.multiple_of(b * 72, 8)
        mixed[0, pl.ds(at, 72), :] = value[0:72]
        mixed[1, pl.ds(at, 72), :] = value[72:144]
        return carry

    each(project, 0, 5)
    ag.finish()
    ag_cot = Gather(net, cot)
    each(project, 5, 8)
    qkv_low[...] = mixed[...].astype(BF16)
    ag_cot.relay_one()

    def attend(image, carry):
        q, k, v = (qkv_low[image, :, i * 128 : (i + 1) * 128] for i in range(3))
        zero = jnp.zeros_like(q)
        total = jnp.zeros(q.shape, F32)
        for h, mask in enumerate(head_masks(q.shape)):
            score = dot_last(jnp.where(mask, q, zero), k) * SCALE
            top = jnp.max(score, -1, keepdims=True)
            e = jnp.exp(score - top)
            row = jnp.sum(e, -1, keepdims=True)
            p = (e * (1.0 / row)).astype(BF16)
            total += dot(p, jnp.where(mask, v, zero))
            lse[image, :, h : h + 1] = top + jnp.log(row)
        heads[image] = total
        return carry

    lax.fori_loop(0, 2, attend, 0)
    up_pass = share_twin(up_in, up_at)

    def by_device(ref, b):
        at = pl.multiple_of(b * 72, 8)
        both = [ref[i, pl.ds(at, 72), :] for i in range(2)]
        return jnp.concatenate(both, axis=0).astype(BF16)

    def outward(b, carry):
        value = by_device(heads, b)
        attended[b] = value
        parts[0, b] = dot(value, out_weight[...]).astype(BF16)
        return carry

    for made in loads[4:]:
        made.wait()
    rs = rs_branch = scatter(0)
    each_sent(rs, outward, 0)
    rs.over()
    rs.relay()
    ag_cot.relay_two()
    resid = tokens[...].astype(F32) + (rs.finish() + bias_out)
    resid_ref[...] = resid
    unit2, inverse2 = norm_unit(resid)
    second[s] = (unit2 * gain2 + shift2).astype(BF16)
    ag = Gather(net, second)
    up_pass.wait_recv()

    def feed(b, total):
        up = columns[:, :, 384:896].reshape(D, 512)
        u = dot(second[b], up) + up_bias
        square = u * u
        t = jnp.tanh(GELU * (u + 0.044715 * u * square))
        act = (0.5 * u * (1.0 + t)).astype(BF16)
        slope = 0.5 * (1.0 + t) + (0.5 * GELU) * u * (1.0 - t * t) * (
            1.0 + 0.134145 * square
        )
        active[b] = act
        gu = (dot_last(cot[b], down_weight[...]) * slope).astype(BF16)
        grad_upper[b] = gu
        parts[1, b] = dot_last(gu, up).astype(BF16)
        parts[2, b] = dot(act, down_weight[...]).astype(BF16)
        return total + jnp.sum(gu.astype(F32), 0, keepdims=True)

    ag.relay_one()
    ag_cot.row()
    ag_cot.finish()
    up_bias_grad = each(feed, 0, 1, jnp.zeros((1, 512), F32))
    ag.relay_two()
    ag.row()
    up_bias_grad = each(feed, 1, 5, up_bias_grad)
    ag.finish()
    rs = scatter(1)
    up_bias_grad = each(feed, 5, 6, up_bias_grad)
    rs.hop()
    up_bias_grad = each(feed, 6, 8, up_bias_grad)
    rs.side()
    rs.near()
    own = pl.ds(pl.multiple_of(s * 128, 128), 128)
    small[...] = jnp.zeros_like(small)
    for i in range(4):
        small[8 + i : 9 + i, :] = up_bias_grad[:, i * 128 : (i + 1) * 128]
    small[7:8, :] = jnp.sum(cot[:, :, own].astype(F32).reshape(1152, 128), 0, keepdims=True)

    def down_tile(i):
        at = pl.ds(i * 256, 256)
        value = dot_first(
            active[...].reshape(1152, 512), cot[:, :, at].reshape(1152, 256)
        ).astype(BF16)
        for q in range(8):
            down_grad[q, :, at] = value[q * 64 : (q + 1) * 64]

    down_tile(0)
    rs.far()
    down_tile(1)
    rs.over()
    rs.relay()
    down_tile(2)
    down_tile(3)
    down_all.core()
    grad_second = rs.finish()
    unit2, inverse2 = norm_unit(resid_ref[...])
    grad_resid = cotangent[...].astype(F32) + norm_back(grad_second, unit2, inverse2, gain2)
    grad_resid_ref[...] = grad_resid
    branch[s] = grad_resid.astype(BF16)
    ag = Gather(net, branch)
    gain2_grad = jnp.sum(grad_second * unit2, 0, keepdims=True)
    shift2_grad = jnp.sum(grad_second, 0, keepdims=True)

    def up_tile(i):
        value = dot_first(
            second[:, :, i * 256 : (i + 1) * 256].reshape(1152, 256),
            grad_upper[...].reshape(1152, 512),
        ).astype(BF16)
        for j in range(2):
            for q in range(8):
                up_grad[q, (2 * i + j) * 16 : (2 * i + j + 1) * 16, :] = value[
                    j * 128 + q * 16 : j * 128 + (q + 1) * 16
                ]

    def back_heads(b, carry):
        value = dot_last(branch[b], out_weight[...])
        at = pl.multiple_of(b * 72, 8)
        heads[0, pl.ds(at, 72), :] = value[0:72]
        heads[1, pl.ds(at, 72), :] = value[72:144]
        return carry

    ag.relay_one()
    down_all.ring()
    up_tile(0)
    ag.relay_two()
    up_tile(1)
    ag.row()
    up_tile(2)
    up_tile(3)
    up_all.core()
    each(back_heads, 0, 5)
    ag.finish()
    rs_out = scatter(2)
    rs_out.hop()
    rs_out.side()
    rs_out.near()
    down_all.beside()
    each(back_heads, 5, 8)
    def attend_back(image, carry):
        q, k, v = (qkv_low[image, :, i * 128 : (i + 1) * 128] for i in range(3))
        grad = heads[image].astype(BF16)
        zero = jnp.zeros_like(q)
        dq = jnp.zeros(q.shape, F32)
        dk, dv = dq, dq
        for h, mask in enumerate(head_masks(q.shape)):
            qh, kh, gh = (jnp.where(mask, a, zero) for a in (q, k, grad))
            p = jnp.exp(dot_last(qh, k) * SCALE - lse[image, :, h : h + 1])
            dp = dot_last(gh, v)
            inner = jnp.sum(p * dp, -1, keepdims=True)
            ds = (p * (dp - inner)).astype(BF16)
            dq += dot(ds, kh)
            dk += dot_first(ds, qh)
            dv += dot_first(p.astype(BF16), gh)
        mixed[image, :, 0:128] = dq * SCALE
        mixed[image, :, 128:256] = dk * SCALE
        mixed[image, :, 256:384] = dv
        return carry

    lax.fori_loop(0, 1, attend_back, 0)
    up_all.ring()
    lax.fori_loop(1, 2, attend_back, 0)
    rs_out.far()
    down_all.cross()
    down_all.back()

    def back_first(b, total):
        value = by_device(mixed, b)
        grad_qkv[b] = value
        parts[0, b] = dot_last(value, columns[:, :, 0:384].reshape(D, 384)).astype(BF16)
        return total + jnp.sum(value.astype(F32), 0, keepdims=True)

    def qkv_tile(i):
        value = dot_first(
            first[:, :, i * 256 : (i + 1) * 256].reshape(1152, 256),
            grad_qkv[...].reshape(1152, 384),
        ).astype(BF16)
        for j in range(2):
            for q in range(8):
                qkv_grad[q, (2 * i + j) * 16 : (2 * i + j + 1) * 16, :] = value[
                    j * 128 + q * 16 : j * 128 + (q + 1) * 16
                ]

    def two_tiles():
        qkv_tile(0)
        qkv_tile(1)

    net.settle([rs_branch.hopped, *rs_branch.sides, *rs_branch.nears])
    rs = scatter(3)
    qkv_bias_grad = each_sent(rs, back_first, jnp.zeros((1, 384), F32), two_tiles)
    small[4:5, :] = qkv_bias_grad[:, 0:128]
    small[5:6, :] = qkv_bias_grad[:, 256:384]
    small[6:7, :] = jnp.sum(branch[:, :, own].astype(F32).reshape(1152, 128), 0, keepdims=True)

    qkv_tile(2)
    qkv_tile(3)
    qkv_all.core()
    rs_out.over()
    up_all.beside()
    rs.over()
    qkv_all.ring()
    value = dot_first(attended[...].reshape(1152, 128), branch[...].reshape(1152, D)).astype(BF16)
    for q in range(8):
        out_grad[q] = value[q * 16 : (q + 1) * 16]
    out_all.core()
    rs_out.relay()
    rs.relay()
    up_all.cross()
    down_all.swap()
    qkv_all.beside()
    out_all.ring()
    up_all.back()
    grad_first = rs.finish()
    unit1, inverse1 = norm_unit(tokens[...].astype(F32))
    gain1_grad = jnp.sum(grad_first * unit1, 0, keepdims=True)
    shift1_grad = jnp.sum(grad_first, 0, keepdims=True)
    four = jnp.concatenate(
        [gain1_grad, shift1_grad, gain2_grad, shift2_grad, jnp.zeros((12, D), F32)], axis=0
    ).astype(BF16)
    for t in range(8):
        fours[t] = four[:, t * 128 : (t + 1) * 128]
    moved = [net.copy(fours.at[to["shard"]], fours_in.at[s], to) for to in net.peers]
    fours_in[s] = fours[s]
    qkv_all.cross()
    out_all.beside()
    input_grad[...] = (
        grad_resid_ref[...] + norm_back(grad_first, unit1, inverse1, gain1)
    ).astype(BF16)
    for made in moved:
        made.wait_recv()
    total = jnp.sum(fours_in[...].astype(F32), 0)
    small[0:4, :] = total[0:4]
    small_low[...] = small[...].astype(BF16)
    moved = [net.copy(small_low, small_ring.at[net.r], to) for to in net.replicas]
    small_ring[net.r] = small_low[...]
    qkv_all.back()
    out_all.cross()
    out_all.back()
    up_all.swap()
    block_out[...] = (resid_ref[...] + (rs_out.finish() + bias_down)).astype(BF16)
    for made in moved:
        made.wait_recv()
    small_sum[...] = add(*(small_ring[k] for k in range(16)))
    qkv_all.swap()
    out_all.swap()
    for every in (down_all, out_all, up_all, qkv_all):
        every.end()
    net.drain()


def layer(*arguments):
    vmem = lambda *shape: pltpu.VMEM(shape, BF16)
    wide = lambda *shape: pltpu.VMEM(shape, F32)
    space = pl.BlockSpec(memory_space=pltpu.VMEM)
    shape = lambda *sizes: jax.ShapeDtypeStruct(sizes, BF16)
    return pl.pallas_call(
        layer_kernel,
        out_shape=[
            shape(ROWS, D),
            shape(ROWS, D),
            shape(512, D),
            shape(128, D),
            shape(128, 4096),
            shape(128, 3 * D),
            jax.ShapeDtypeStruct((16, 128), F32),
        ],
        in_specs=[space] * 11 + [pl.BlockSpec(memory_space=pl.ANY)] * 4,
        out_specs=[space] * 7,
        scratch_shapes=[
            vmem(8, 64, D),
            vmem(8, 16, D),
            vmem(8, 128, 512),
            vmem(8, 128, 384),
            wide(16, 128),
            vmem(16, 128),
            vmem(8, 16, 128),
            vmem(8, 128, 896),
            vmem(8, ROWS, D),
            vmem(8, ROWS, D),
            vmem(8, ROWS, D),
            vmem(8, ROWS, D),
            wide(2, 576, 384),
            vmem(2, 576, 384),
            wide(2, 576, 128),
            wide(2, 576, 128),
            vmem(8, ROWS, 128),
            vmem(8, ROWS, 512),
            vmem(8, ROWS, 512),
            vmem(8, ROWS, 384),
            wide(ROWS, D),
            wide(ROWS, D),
            wide(16, 128),
            vmem(8, 16, 128),
            vmem(8, 16, 128),
            vmem(3, 8, ROWS, D),
            vmem(4, ROWS, D),
            vmem(4, 2, ROWS, D),
            vmem(4, 2, ROWS, HALF),
            vmem(4, 2, ROWS, HALF),
            vmem(4, 2, ROWS, HALF),
            vmem(4, ROWS, D),
            vmem(4, ROWS, D),
            vmem(16, 128),
            vmem(16, 16, 128),
            vmem(2, 4, 64, D),
            vmem(5, 64, D),
            vmem(2, 4, 16, D),
            vmem(5, 16, D),
            vmem(2, 4, 128, 512),
            vmem(5, 128, 512),
            vmem(2, 8, 16, 512),
            vmem(2, 4, 128, 384),
            vmem(5, 128, 384),
            vmem(2, 8, 16, 384),
            vmem(128, D),
            vmem(512, D),
            pltpu.SemaphoreType.DMA((6,)),
            pltpu.SemaphoreType.DMA((240,)),
            pltpu.SemaphoreType.DMA((240,)),
        ],
        name="layer",
        cost_estimate=pl.CostEstimate(
            flops=11 * 10**9, bytes_accessed=12 * 10**6, transcendentals=0
        ),
        compiler_params=pltpu.CompilerParams(
            collective_id=1, has_side_effects=True, vmem_limit_bytes=62 << 20
        ),
    )(*arguments)


def cast_kernel(block, grad, down, out, up, qkv, small, *outs):
    for source, target in zip((block, grad), outs[:2]):
        target[...] = source[...].astype(F32).reshape(2, 72, D).astype(BF16)
    for source, target in zip((down, out, up, qkv), outs[2:6]):
        target[...] = source[...].astype(F32)
    for k, target in enumerate(outs[6:14]):
        target[...] = small[k]
    for k in range(4):
        outs[14][k * 128 : (k + 1) * 128] = small[8 + k]


def cast(*arrays):
    space = pl.BlockSpec(memory_space=pltpu.VMEM)
    shape = lambda *sizes: jax.ShapeDtypeStruct(sizes, F32)
    return pl.pallas_call(
        cast_kernel,
        out_shape=[
            *(jax.ShapeDtypeStruct((2, 72, D), BF16) for _ in range(2)),
            *(shape(*a.shape) for a in arrays[2:6]),
            *(shape(128) for _ in range(8)),
            shape(512),
        ],
        in_specs=[space] * 7,
        out_specs=[space] * 15,
        name="cast",
        compiler_params=pltpu.CompilerParams(vmem_limit_bytes=62 << 20),
    )(*arrays)


def body(
    tokens,
    cotangent,
    attn_gain,
    attn_shift,
    qkv_weight,
    query_bias,
    value_bias,
    out_weight,
    out_bias,
    mlp_gain,
    mlp_shift,
    up_weight,
    up_bias,
    down_weight,
    down_bias,
):
    vectors = (attn_gain, attn_shift, mlp_gain, mlp_shift, out_bias, down_bias)
    vectors = (*vectors, query_bias, value_bias, up_bias)
    sums = layer(
        tokens.reshape(ROWS, D),
        cotangent.reshape(ROWS, D),
        *(a.reshape(-1, 128) for a in vectors),
        qkv_weight,
        up_weight,
        out_weight,
        down_weight,
    )
    block_out, input_grad, down_grad, out_grad, up_grad, qkv_grad, *small = cast(*sums)
    up_bias_grad = small.pop()
    return (
        block_out,
        input_grad,
        small[0],
        small[1],
        qkv_grad,
        small[4],
        small[5],
        out_grad,
        small[6],
        small[2],
        small[3],
        up_grad,
        up_bias_grad,
        down_grad,
        small[7],
    )


def solution(mesh):
    row, cube, flat = P("shard"), P("replica", "shard", None), P("shard", None)
    return jax.shard_map(
        body,
        mesh=mesh,
        in_specs=(cube, cube, row, row, flat, row, row, flat, row, row, row, flat, row, flat, row),
        out_specs=(cube, cube, row, row, flat, row, row, flat, row, row, row, flat, row, flat, row),
        check_vma=False,
    )
```

```python
import jax
import jax.numpy as jnp
from jax import lax
from jax.experimental import pallas as pl
from jax.experimental.pallas import tpu as pltpu
from jax.sharding import PartitionSpec as P

HEAD_DIM = 64
EPS = 1e-06
F32 = jnp.float32
BF16 = jnp.bfloat16
SCALE = HEAD_DIM ** (-0.5)
MESH = pl.DeviceIdType.MESH
D = 1024
ROWS = 144
HALF = 512
GELU = 0.7978845608028654


def dot(a, b):
    return lax.dot_general(a, b, (((1,), (0,)), ((), ())), preferred_element_type=F32)


def dot_last(a, b):
    return lax.dot_general(a, b, (((1,), (1,)), ((), ())), preferred_element_type=F32)


def dot_first(a, b):
    return lax.dot_general(a, b, (((0,), (0,)), ((), ())), preferred_element_type=F32)


def norm_unit(v):
    mean = jnp.mean(v, -1, keepdims=True)
    centred = v - mean
    inverse = lax.rsqrt(jnp.mean(centred * centred, -1, keepdims=True) + EPS)
    return centred * inverse, inverse


def norm_back(grad, unit, inverse, gain):
    gn = grad * gain
    inner = jnp.mean(gn * unit, -1, keepdims=True)
    return inverse * (gn - jnp.mean(gn, -1, keepdims=True) - unit * inner)


def head_masks(shape):
    low = lax.broadcasted_iota(jnp.int32, shape, 1) < HEAD_DIM
    return (low, jnp.logical_not(low))


def add(*terms):
    total = terms[0].astype(F32)
    for term in terms[1:]:
        total = total + term.astype(F32)
    return total


class Net:
    def __init__(self, send, recv):
        self.send, self.recv, self.count, self.open = send, recv, 0, []
        self.s = lax.axis_index("shard")
        self.h, self.x = self.s // 4, lax.rem(self.s, 4)
        r = lax.axis_index("replica")
        self.core, self.y = lax.rem(r, 2), lax.rem(r // 2, 4)
        zlow = r // 8
        base = r - self.y * 2
        self.right = {"shard": self.at(self.h, self.x + 1)}
        self.left = {"shard": self.at(self.h, self.x + 3)}
        self.across = {"shard": self.at(1 - self.h, self.x)}
        self.twin = {"replica": r + 1 - 2 * self.core}
        self.up = {"replica": base + lax.rem(self.y + 1, 4) * 2}
        self.down = {"replica": base + lax.rem(self.y + 3, 4) * 2}
        self.facing = {"replica": base + lax.rem(self.y + 2, 4) * 2}
        self.beside = {"replica": r + 8 - 16 * zlow}
        self.replicas = [{"replica": lax.rem(r + k, 16)} for k in range(1, 16)]
        self.r = r
        self.peers = [{"shard": lax.rem(self.s + k, 8)} for k in range(1, 8)]

    def at(self, h, x):
        return h * 4 + lax.rem(x, 4)

    def copy(self, src, dst, to):
        i = self.count
        self.count += 1
        made = pltpu.make_async_remote_copy(
            src_ref=src,
            dst_ref=dst,
            send_sem=self.send.at[i],
            recv_sem=self.recv.at[i],
            device_id=to,
            device_id_type=MESH,
        )
        made.start()
        self.open.append(made)
        return made

    def drain(self):
        for made in self.open:
            made.wait_send()
        self.open = []

    def settle(self, copies):
        for made in copies:
            made.wait_send()
            self.open = [other for other in self.open if other is not made]

    def barrier(self, others):
        semaphore = pltpu.get_barrier_semaphore()
        for other in others:
            pl.semaphore_signal(semaphore, inc=1, device_id=other, device_id_type=MESH)
        pl.semaphore_wait(semaphore, len(others))


class Gather:
    def __init__(self, net, whole):
        self.net, self.whole = net, whole
        self.a = self.piece(net.s, 0, net.right)
        self.b = self.piece(net.s, 1, net.left)
        own = whole.at[net.s]
        self.z = net.copy(own, own, net.across)
        self.more = [self.piece(net.s, 1, net.right), self.piece(net.s, 0, net.left)]

    def piece(self, block, second, to):
        part = self.whole.at[block, :, pl.ds(second * HALF, HALF)]
        return self.net.copy(part, part, to)

    def relay_one(self):
        net = self.net
        self.a.wait_recv()
        self.c = self.piece(net.at(net.h, net.x + 3), 0, net.right)
        self.b.wait_recv()
        self.d = self.piece(net.at(net.h, net.x + 1), 1, net.left)

    def relay_two(self):
        net = self.net
        self.z.wait_recv()
        part = self.whole.at[net.at(1 - net.h, net.x)]
        self.rest = [net.copy(part, part, net.right), net.copy(part, part, net.left)]
        block = net.at(net.h, net.x + 2)
        self.c.wait_recv()
        self.rest.append(self.piece(block, 0, net.across))
        self.d.wait_recv()
        self.rest.append(self.piece(block, 1, net.across))

    def row(self):
        for made in self.more:
            made.wait_recv()

    def finish(self):
        for made in self.rest:
            made.wait_recv()


class Scatter:
    def __init__(self, net, part, hop, side, near, far, passed, kept, came):
        self.net, self.part, self.hop_in, self.side_in = net, part, hop, side
        self.near_in, self.far_in, self.passed, self.kept, self.came = near, far, passed, kept, came
        self.one, self.two = pl.ds(0, HALF), pl.ds(HALF, HALF)
        h, x = net.h, net.x
        self.own, self.facing = net.s, net.at(h, x + 2)
        self.right, self.left = net.at(h, x + 1), net.at(h, x + 3)
        self.other = [net.at(1 - h, x + k) for k in range(4)]

    def hop(self):
        self.hopped = self.net.copy(self.part.at[self.other[2]], self.hop_in, self.net.across)

    def side(self):
        net, part = self.net, self.part
        self.sides = [
            net.copy(part.at[self.other[1]], self.side_in.at[0], net.right),
            net.copy(part.at[self.other[3]], self.side_in.at[1], net.left),
        ]

    def near(self):
        net, part = self.net, self.part
        self.nears = [
            net.copy(part.at[self.right, :, self.two], self.near_in.at[0], net.right),
            net.copy(part.at[self.left, :, self.one], self.near_in.at[1], net.left),
        ]

    def far(self):
        net, hop = self.net, self.hop_in
        self.hopped.wait_recv()
        hop[...] = add(hop[...], self.part[self.facing]).astype(BF16)
        self.fars = [
            net.copy(hop.at[:, self.one], self.far_in.at[0], net.right),
            net.copy(hop.at[:, self.two], self.far_in.at[1], net.left),
        ]

    def over(self):
        for made in self.sides:
            made.wait_recv()
        self.kept[...] = add(
            self.part[self.other[0]], self.side_in[0], self.side_in[1]
        ).astype(BF16)
        self.crossed = self.net.copy(self.kept, self.came, self.net.across)

    def relay(self):
        net, part, far = self.net, self.part, self.far_in
        self.fars[0].wait_recv()
        far[0] = add(far[0], part[self.right, :, self.one]).astype(BF16)
        passes = [net.copy(far.at[0], self.passed.at[0], net.right)]
        self.fars[1].wait_recv()
        far[1] = add(far[1], part[self.left, :, self.two]).astype(BF16)
        passes.append(net.copy(far.at[1], self.passed.at[1], net.left))
        self.last = [*self.nears, *passes, self.crossed]

    def finish(self):
        for made in self.last:
            made.wait_recv()
        part, near, passed, came = self.part, self.near_in, self.passed, self.came
        one, two = self.one, self.two
        return jnp.concatenate(
            [
                add(part[self.own, :, one], passed[0], near[1], came[:, one]),
                add(part[self.own, :, two], passed[1], near[0], came[:, two]),
            ],
            axis=1,
        )


class Reduce:
    def __init__(self, net, grad, pair, ring, out, turned=None):
        self.net, self.grad, self.out, self.turned = net, grad, out, turned
        self.sent, self.work = pair
        *self.three, self.kept, self.came = ring
        self.mine = pl.ds(net.core * 4, 4)
        self.q = net.core * 4 + net.y
        self.at_up, self.at_facing, self.at_down = (lax.rem(net.y + k, 4) for k in (1, 2, 3))

    def core(self):
        net = self.net
        self.moved = net.copy(self.grad.at[pl.ds((1 - net.core) * 4, 4)], self.sent, net.twin)

    def ring(self):
        net, work = self.net, self.work
        self.moved.wait_recv()
        work[...] = add(self.grad[self.mine], self.sent[...]).astype(BF16)
        steps = ((self.at_up, net.up), (self.at_down, net.down), (self.at_facing, net.facing))
        self.nears = [
            net.copy(work.at[block], there, to) for there, (block, to) in zip(self.three, steps)
        ]

    def beside(self):
        net = self.net
        for made in self.nears:
            made.wait_recv()
        three = [part[...] for part in self.three]
        self.kept[...] = add(self.work[net.y], *three).astype(BF16)
        self.over = net.copy(self.kept, self.came, net.beside)

    def place(self, q, eighths=1):
        rows = self.out.shape[0] // 8
        return pl.ds(pl.multiple_of(q * rows, 16), rows * eighths)

    def cross(self):
        net = self.net
        self.over.wait_recv()
        total = add(self.kept[...], self.came[...]).astype(BF16)
        if self.turned is None:
            self.out[self.place(self.q)] = total
            return
        away, back = self.turned
        away[...] = total.reshape(away.shape)
        self.crossed = [
            net.copy(away.at[to["shard"]], back.at[net.s], to) for to in net.peers
        ]
        back[net.s] = away[net.s]

    def back(self):
        net, out = self.net, self.out
        own = self.place(self.q)
        if self.turned is not None:
            for made in self.crossed:
                made.wait_recv()
            incoming = self.turned[1]
            blocks = [incoming[t] for t in range(8)]
            width = blocks[0].shape[-1]
            for i in range(width // 128 if width == 384 else 1):
                size = 128 if width == 384 else width
                for t in range(8):
                    at = i * D + t * size
                    out[own, at : at + size] = blocks[t][:, i * 128 : i * 128 + size]
        part = out.at[own]
        self.shared = [net.copy(part, part, to) for to in (net.up, net.down, net.facing)]

    def swap(self):
        for made in self.shared:
            made.wait_recv()
        part = self.out.at[self.place(self.net.core * 4, 4)]
        self.ended = self.net.copy(part, part, self.net.twin)

    def end(self):
        self.ended.wait_recv()


def layer_kernel(*refs):
    layer_steps(*refs[:2], refs[2:8], *refs[8:])


def layer_steps(
    tokens,
    cotangent,
    singles,
    query_bias,
    value_bias,
    up_bias,
    qkv_weight,
    up_weight,
    out_source,
    down_source,
    block_out,
    input_grad,
    down_sum,
    out_sum,
    up_sum,
    qkv_sum,
    small_sum,
    down_grad,
    out_grad,
    up_grad,
    qkv_grad,
    wide_vectors,
    vectors,
    all_vectors,
    columns,
    first,
    cot,
    second,
    branch,
    mixed,
    qkv_low,
    heads,
    lse,
    attended,
    active,
    grad_upper,
    grad_qkv,
    resid_ref,
    grad_resid_ref,
    small,
    fours,
    fours_in,
    parts,
    hop,
    side,
    near,
    far,
    passed,
    kept,
    came,
    small_low,
    small_ring,
    down_pair,
    down_ring,
    out_pair,
    out_ring,
    up_pair,
    up_ring,
    up_turned,
    qkv_pair,
    qkv_ring,
    qkv_turned,
    out_weight,
    down_weight,
    load,
    send,
    recv,
):
    net = Net(send, recv)
    s, core = net.s, net.core
    net.barrier([*net.peers, *net.replicas])

    def reduce(grad, pair, ring, out, turned=None):
        split = lambda ref, n: [ref.at[i] for i in range(n)]
        turned = None if turned is None else split(turned, 2)
        return Reduce(net, grad, split(pair, 2), split(ring, 5), out, turned)

    down_all = reduce(down_grad, down_pair, down_ring, down_sum)
    out_all = reduce(out_grad, out_pair, out_ring, out_sum)
    up_all = reduce(up_grad, up_pair, up_ring, up_sum, up_turned)
    qkv_all = reduce(qkv_grad, qkv_pair, qkv_ring, qkv_sum, qkv_turned)
    mine = pl.ds(pl.multiple_of(core * 64, 64), 64)
    sixteen = pl.ds(pl.multiple_of(core * 64 + net.y * 16, 16), 16)

    def scatter(i):
        buffers = (hop, side, near, far, passed, kept, came)
        return Scatter(net, parts.at[i % 3], *(buffer.at[i] for buffer in buffers))

    def each(work, least, end, carry=0):
        def step(i, carry):
            row, j = i // 4, lax.rem(i, 4)
            same = j + j // 2 - 2 * (j // 3)
            cross = lax.rem(2 * j, 3) + 3 * (j // 3)
            h = net.h + row - 2 * net.h * row
            return work(net.at(h, net.x + (1 - row) * same + row * cross), carry)

        return lax.fori_loop(least, end, step, carry)

    def each_sent(rs, work, carry, beside=None):
        carry = each(work, 5, 6, carry)
        rs.hop()
        carry = each(work, 6, 8, carry)
        rs.side()
        carry = each(work, 1, 3, carry)
        rs.near()
        carry = each(work, 3, 5, carry)
        if beside is None:
            rs.far()
            return each(work, 0, 1, carry)
        carry = each(work, 0, 1, carry)
        beside()
        rs.far()
        return carry

    parts[1, s] = tokens[...]
    raw = parts.at[1]
    ag_raw = Gather(net, raw)

    wide_vectors[...] = jnp.zeros_like(wide_vectors)
    for k, single in enumerate(singles):
        wide_vectors[k : k + 1, :] = single[...].astype(F32)
    vectors[...] = wide_vectors[...].astype(BF16)
    vec = [net.copy(vectors, all_vectors.at[s], to) for to in net.peers]
    all_vectors[s] = vectors[...]
    cot[s] = cotangent[...]
    qkv_in, up_in = [], []
    thirds = [
        lambda t, i=i: qkv_weight.at[sixteen, pl.ds(pl.multiple_of(i * D + t * 128, 128), 128)]
        for i in range(3)
    ]
    quarter = lambda t: up_weight.at[sixteen, pl.ds(pl.multiple_of(t * 512, 512), 512)]
    for to in net.peers:
        for i in range(3):
            there = columns.at[s, sixteen, pl.ds(i * 128, 128)]
            qkv_in.append(net.copy(thirds[i](to["shard"]), there, to))
    for to in net.peers:
        there = columns.at[s, sixteen, pl.ds(384, 512)]
        up_in.append(net.copy(quarter(to["shard"]), there, to))
    loads = [
        (thirds[i](s), columns.at[s, sixteen, pl.ds(i * 128, 128)]) for i in range(3)
    ]
    loads += [
        (quarter(s), columns.at[s, sixteen, pl.ds(384, 512)]),
        (out_source, out_weight),
        (down_source, down_weight),
    ]
    loads = [pltpu.make_async_copy(*pair, load.at[i]) for i, pair in enumerate(loads)]
    for made in loads:
        made.start()

    def share(arrived, at):
        for made in arrived:
            made.wait_recv()
        part = columns.at[:, sixteen, at]
        return [net.copy(part, part, to) for to in (net.up, net.down, net.facing)]

    def share_twin(arrived, at):
        for made in arrived:
            made.wait_recv()
        part = columns.at[:, mine, at]
        return net.copy(part, part, net.twin)

    qkv_at, up_at = pl.ds(0, 384), pl.ds(384, 512)
    for made in loads[:4]:
        made.wait()
    ag_raw.relay_one()
    qkv_in = share(qkv_in, qkv_at)
    ag_raw.relay_two()
    up_in = share(up_in, up_at)
    for made in vec:
        made.wait_recv()
    table = [all_vectors[j].astype(F32) for j in range(8)]
    gain1, shift1, gain2, shift2, bias_out, bias_down = (
        jnp.concatenate([t[i : i + 1] for t in table], axis=1) for i in range(6)
    )
    qkv_pass = share_twin(qkv_in, qkv_at)
    qkv_bias = jnp.concatenate(
        [query_bias[...].astype(F32), jnp.zeros((1, 128), F32), value_bias[...].astype(F32)], axis=1
    )
    up_bias = up_bias[...].astype(F32)
    up_bias = jnp.concatenate([up_bias[k : k + 1] for k in range(4)], axis=1)
    qkv_pass.wait_recv()
    ag_raw.row()

    def project(b, carry):
        unit, _ = norm_unit(raw[b].astype(F32))
        first[b] = (unit * gain1 + shift1).astype(BF16)
        value = dot(first[b], columns[:, :, 0:384].reshape(D, 384)) + qkv_bias
        at = pl.multiple_of(b * 72, 8)
        mixed[0, pl.ds(at, 72), :] = value[0:72]
        mixed[1, pl.ds(at, 72), :] = value[72:144]
        return carry

    each(project, 0, 5)
    ag_raw.finish()
    ag_cot = Gather(net, cot)
    each(project, 5, 8)
    qkv_low[...] = mixed[...].astype(BF16)
    ag_cot.relay_one()

    def attend(image, carry):
        q, k, v = (qkv_low[image, :, i * 128 : (i + 1) * 128] for i in range(3))
        zero = jnp.zeros_like(q)
        total = jnp.zeros(q.shape, F32)
        for h, mask in enumerate(head_masks(q.shape)):
            score = dot_last(jnp.where(mask, q, zero), k) * SCALE
            top = jnp.max(score, -1, keepdims=True)
            e = jnp.exp(score - top)
            row = jnp.sum(e, -1, keepdims=True)
            p = (e * (1.0 / row)).astype(BF16)
            total += dot(p, jnp.where(mask, v, zero))
            lse[image, :, h : h + 1] = top + jnp.log(row)
        heads[image] = total
        return carry

    lax.fori_loop(0, 2, attend, 0)
    up_pass = share_twin(up_in, up_at)

    def by_device(ref, b):
        at = pl.multiple_of(b * 72, 8)
        both = [ref[i, pl.ds(at, 72), :] for i in range(2)]
        return jnp.concatenate(both, axis=0).astype(BF16)

    def outward(b, carry):
        value = by_device(heads, b)
        attended[b] = value
        parts[0, b] = dot(value, out_weight[...]).astype(BF16)
        return carry

    for made in loads[4:]:
        made.wait()
    rs = rs_branch = scatter(0)
    each_sent(rs, outward, 0)
    rs.over()
    rs.relay()
    ag_cot.relay_two()
    resid = tokens[...].astype(F32) + (rs.finish() + bias_out)
    resid_ref[...] = resid
    unit2, inverse2 = norm_unit(resid)
    second[s] = (unit2 * gain2 + shift2).astype(BF16)
    ag = Gather(net, second)
    up_pass.wait_recv()

    def feed(b, total):
        up = columns[:, :, 384:896].reshape(D, 512)
        u = dot(second[b], up) + up_bias
        square = u * u
        t = jnp.tanh(GELU * (u + 0.044715 * u * square))
        act = (0.5 * u * (1.0 + t)).astype(BF16)
        slope = 0.5 * (1.0 + t) + (0.5 * GELU) * u * (1.0 - t * t) * (
            1.0 + 0.134145 * square
        )
        active[b] = act
        gu = (dot_last(cot[b], down_weight[...]) * slope).astype(BF16)
        grad_upper[b] = gu
        parts[1, b] = dot_last(gu, up).astype(BF16)
        parts[2, b] = dot(act, down_weight[...]).astype(BF16)
        return total + jnp.sum(gu.astype(F32), 0, keepdims=True)

    ag.relay_one()
    ag_cot.row()
    ag_cot.finish()
    net.settle([ag_raw.a, ag_raw.b, ag_raw.z, *ag_raw.more, ag_raw.c, ag_raw.d, *ag_raw.rest])
    up_bias_grad = each(feed, 0, 1, jnp.zeros((1, 512), F32))
    ag.relay_two()
    ag.row()
    up_bias_grad = each(feed, 1, 5, up_bias_grad)
    ag.finish()
    rs = scatter(1)
    up_bias_grad = each(feed, 5, 6, up_bias_grad)
    rs.hop()
    up_bias_grad = each(feed, 6, 8, up_bias_grad)
    rs.side()
    rs.near()
    own = pl.ds(pl.multiple_of(s * 128, 128), 128)
    small[...] = jnp.zeros_like(small)
    for i in range(4):
        small[8 + i : 9 + i, :] = up_bias_grad[:, i * 128 : (i + 1) * 128]
    small[7:8, :] = jnp.sum(cot[:, :, own].astype(F32).reshape(1152, 128), 0, keepdims=True)

    def down_tile(i):
        at = pl.ds(i * 256, 256)
        value = dot_first(
            active[...].reshape(1152, 512), cot[:, :, at].reshape(1152, 256)
        ).astype(BF16)
        for q in range(8):
            down_grad[q, :, at] = value[q * 64 : (q + 1) * 64]

    down_tile(0)
    rs.far()
    down_tile(1)
    rs.over()
    rs.relay()
    down_tile(2)
    down_tile(3)
    down_all.core()
    grad_second = rs.finish()
    unit2, inverse2 = norm_unit(resid_ref[...])
    grad_resid = cotangent[...].astype(F32) + norm_back(grad_second, unit2, inverse2, gain2)
    grad_resid_ref[...] = grad_resid
    branch[s] = grad_resid.astype(BF16)
    ag = Gather(net, branch)
    gain2_grad = jnp.sum(grad_second * unit2, 0, keepdims=True)
    shift2_grad = jnp.sum(grad_second, 0, keepdims=True)

    def up_tile(i):
        value = dot_first(
            second[:, :, i * 256 : (i + 1) * 256].reshape(1152, 256),
            grad_upper[...].reshape(1152, 512),
        ).astype(BF16)
        for j in range(2):
            for q in range(8):
                up_grad[q, (2 * i + j) * 16 : (2 * i + j + 1) * 16, :] = value[
                    j * 128 + q * 16 : j * 128 + (q + 1) * 16
                ]

    def back_heads(b, carry):
        value = dot_last(branch[b], out_weight[...])
        at = pl.multiple_of(b * 72, 8)
        heads[0, pl.ds(at, 72), :] = value[0:72]
        heads[1, pl.ds(at, 72), :] = value[72:144]
        return carry

    ag.relay_one()
    down_all.ring()
    up_tile(0)
    ag.relay_two()
    up_tile(1)
    ag.row()
    up_tile(2)
    up_tile(3)
    up_all.core()
    each(back_heads, 0, 5)
    ag.finish()
    rs_out = scatter(2)
    rs_out.hop()
    rs_out.side()
    rs_out.near()
    down_all.beside()
    each(back_heads, 5, 8)
    def attend_back(image, carry):
        q, k, v = (qkv_low[image, :, i * 128 : (i + 1) * 128] for i in range(3))
        grad = heads[image].astype(BF16)
        zero = jnp.zeros_like(q)
        dq = jnp.zeros(q.shape, F32)
        dk, dv = dq, dq
        for h, mask in enumerate(head_masks(q.shape)):
            qh, kh, gh = (jnp.where(mask, a, zero) for a in (q, k, grad))
            p = jnp.exp(dot_last(qh, k) * SCALE - lse[image, :, h : h + 1])
            dp = dot_last(gh, v)
            inner = jnp.sum(p * dp, -1, keepdims=True)
            ds = (p * (dp - inner)).astype(BF16)
            dq += dot(ds, kh)
            dk += dot_first(ds, qh)
            dv += dot_first(p.astype(BF16), gh)
        mixed[image, :, 0:128] = dq * SCALE
        mixed[image, :, 128:256] = dk * SCALE
        mixed[image, :, 256:384] = dv
        return carry

    lax.fori_loop(0, 1, attend_back, 0)
    up_all.ring()
    lax.fori_loop(1, 2, attend_back, 0)
    rs_out.far()

    def back_first(b, total):
        value = by_device(mixed, b)
        grad_qkv[b] = value
        parts[0, b] = dot_last(value, columns[:, :, 0:384].reshape(D, 384)).astype(BF16)
        return total + jnp.sum(value.astype(F32), 0, keepdims=True)

    def qkv_tile(i):
        value = dot_first(
            first[:, :, i * 256 : (i + 1) * 256].reshape(1152, 256),
            grad_qkv[...].reshape(1152, 384),
        ).astype(BF16)
        for j in range(2):
            for q in range(8):
                qkv_grad[q, (2 * i + j) * 16 : (2 * i + j + 1) * 16, :] = value[
                    j * 128 + q * 16 : j * 128 + (q + 1) * 16
                ]

    def two_tiles():
        qkv_tile(0)
        down_all.cross()
        down_all.back()
        qkv_tile(1)

    net.settle([rs_branch.hopped, *rs_branch.sides, *rs_branch.nears])
    rs = scatter(3)
    qkv_bias_grad = each_sent(rs, back_first, jnp.zeros((1, 384), F32), two_tiles)
    small[4:5, :] = qkv_bias_grad[:, 0:128]
    small[5:6, :] = qkv_bias_grad[:, 256:384]
    small[6:7, :] = jnp.sum(branch[:, :, own].astype(F32).reshape(1152, 128), 0, keepdims=True)

    qkv_tile(2)
    qkv_tile(3)
    qkv_all.core()
    rs_out.over()
    up_all.beside()
    rs.over()
    qkv_all.ring()
    value = dot_first(attended[...].reshape(1152, 128), branch[...].reshape(1152, D)).astype(BF16)
    for q in range(8):
        out_grad[q] = value[q * 16 : (q + 1) * 16]
    out_all.core()
    rs_out.relay()
    rs.relay()
    up_all.cross()
    down_all.swap()
    qkv_all.beside()
    out_all.ring()
    up_all.back()
    grad_first = rs.finish()
    unit1, inverse1 = norm_unit(tokens[...].astype(F32))
    gain1_grad = jnp.sum(grad_first * unit1, 0, keepdims=True)
    shift1_grad = jnp.sum(grad_first, 0, keepdims=True)
    four = jnp.concatenate(
        [gain1_grad, shift1_grad, gain2_grad, shift2_grad, jnp.zeros((12, D), F32)], axis=0
    ).astype(BF16)
    for t in range(8):
        fours[t] = four[:, t * 128 : (t + 1) * 128]
    moved = [net.copy(fours.at[to["shard"]], fours_in.at[s], to) for to in net.peers]
    fours_in[s] = fours[s]
    qkv_all.cross()
    out_all.beside()
    input_grad[...] = (
        grad_resid_ref[...] + norm_back(grad_first, unit1, inverse1, gain1)
    ).astype(BF16)
    for made in moved:
        made.wait_recv()
    total = jnp.sum(fours_in[...].astype(F32), 0)
    small[0:4, :] = total[0:4]
    small_low[...] = small[...].astype(BF16)
    moved = [net.copy(small_low, small_ring.at[net.r], to) for to in net.replicas]
    small_ring[net.r] = small_low[...]
    qkv_all.back()
    out_all.cross()
    out_all.back()
    up_all.swap()
    block_out[...] = (resid_ref[...] + (rs_out.finish() + bias_down)).astype(BF16)
    for made in moved:
        made.wait_recv()
    small_sum[...] = add(*(small_ring[k] for k in range(16)))
    qkv_all.swap()
    out_all.swap()
    for every in (down_all, out_all, up_all, qkv_all):
        every.end()
    net.drain()


def layer(*arguments):
    vmem = lambda *shape: pltpu.VMEM(shape, BF16)
    wide = lambda *shape: pltpu.VMEM(shape, F32)
    space = pl.BlockSpec(memory_space=pltpu.VMEM)
    shape = lambda *sizes: jax.ShapeDtypeStruct(sizes, BF16)
    return pl.pallas_call(
        layer_kernel,
        out_shape=[
            shape(ROWS, D),
            shape(ROWS, D),
            shape(512, D),
            shape(128, D),
            shape(128, 4096),
            shape(128, 3 * D),
            jax.ShapeDtypeStruct((16, 128), F32),
        ],
        in_specs=[space] * 11 + [pl.BlockSpec(memory_space=pl.ANY)] * 4,
        out_specs=[space] * 7,
        scratch_shapes=[
            vmem(8, 64, D),
            vmem(8, 16, D),
            vmem(8, 128, 512),
            vmem(8, 128, 384),
            wide(16, 128),
            vmem(16, 128),
            vmem(8, 16, 128),
            vmem(8, 128, 896),
            vmem(8, ROWS, D),
            vmem(8, ROWS, D),
            vmem(8, ROWS, D),
            vmem(8, ROWS, D),
            wide(2, 576, 384),
            vmem(2, 576, 384),
            wide(2, 576, 128),
            wide(2, 576, 128),
            vmem(8, ROWS, 128),
            vmem(8, ROWS, 512),
            vmem(8, ROWS, 512),
            vmem(8, ROWS, 384),
            wide(ROWS, D),
            wide(ROWS, D),
            wide(16, 128),
            vmem(8, 16, 128),
            vmem(8, 16, 128),
            vmem(3, 8, ROWS, D),
            vmem(4, ROWS, D),
            vmem(4, 2, ROWS, D),
            vmem(4, 2, ROWS, HALF),
            vmem(4, 2, ROWS, HALF),
            vmem(4, 2, ROWS, HALF),
            vmem(4, ROWS, D),
            vmem(4, ROWS, D),
            vmem(16, 128),
            vmem(16, 16, 128),
            vmem(2, 4, 64, D),
            vmem(5, 64, D),
            vmem(2, 4, 16, D),
            vmem(5, 16, D),
            vmem(2, 4, 128, 512),
            vmem(5, 128, 512),
            vmem(2, 8, 16, 512),
            vmem(2, 4, 128, 384),
            vmem(5, 128, 384),
            vmem(2, 8, 16, 384),
            vmem(128, D),
            vmem(512, D),
            pltpu.SemaphoreType.DMA((6,)),
            pltpu.SemaphoreType.DMA((240,)),
            pltpu.SemaphoreType.DMA((240,)),
        ],
        name="layer",
        cost_estimate=pl.CostEstimate(
            flops=11 * 10**9, bytes_accessed=12 * 10**6, transcendentals=0
        ),
        compiler_params=pltpu.CompilerParams(
            collective_id=1, has_side_effects=True, vmem_limit_bytes=62 << 20
        ),
    )(*arguments)


def cast_kernel(*refs):
    large, small, refs = refs[:6], refs[6], refs[7:]
    outs, little, refs = refs[:6], refs[6:15], refs[15:]
    held, wide, (load, store) = refs[:6], refs[6:12], refs[12:]
    loads = [pltpu.make_async_copy(*pair, load.at[i]) for i, pair in enumerate(zip(large, held))]
    stores = [pltpu.make_async_copy(*pair, store.at[i]) for i, pair in enumerate(zip(wide, outs))]
    for made in loads:
        made.start()
    for i in range(6):
        loads[i].wait()
        value = held[i][...].astype(F32)
        wide[i][...] = value if i < 4 else value.reshape(2, 72, D).astype(BF16)
        stores[i].start()
    for k in range(8):
        little[k][...] = small[k]
    for k in range(4):
        little[8][k * 128 : (k + 1) * 128] = small[8 + k]
    for made in stores:
        made.wait()


def cast(block, grad, *arrays):
    space = pl.BlockSpec(memory_space=pltpu.VMEM)
    far = pl.BlockSpec(memory_space=pl.ANY)
    shape = lambda *sizes: jax.ShapeDtypeStruct(sizes, F32)
    *grads, small = arrays
    results = [shape(*a.shape) for a in grads] + [jax.ShapeDtypeStruct((2, 72, D), BF16)] * 2
    large = (*grads, block, grad)
    return pl.pallas_call(
        cast_kernel,
        out_shape=[*results, *(shape(128) for _ in range(8)), shape(512)],
        in_specs=[far] * 6 + [space],
        out_specs=[far] * 6 + [space] * 9,
        scratch_shapes=[
            *(pltpu.VMEM(a.shape, a.dtype) for a in large),
            *(pltpu.VMEM(a.shape, a.dtype) for a in results),
            pltpu.SemaphoreType.DMA((6,)),
            pltpu.SemaphoreType.DMA((6,)),
        ],
        name="cast",
        compiler_params=pltpu.CompilerParams(vmem_limit_bytes=62 << 20),
    )(*large, small)


def body(
    tokens,
    cotangent,
    attn_gain,
    attn_shift,
    qkv_weight,
    query_bias,
    value_bias,
    out_weight,
    out_bias,
    mlp_gain,
    mlp_shift,
    up_weight,
    up_bias,
    down_weight,
    down_bias,
):
    vectors = (attn_gain, attn_shift, mlp_gain, mlp_shift, out_bias, down_bias)
    vectors = (*vectors, query_bias, value_bias, up_bias)
    sums = layer(
        tokens.reshape(ROWS, D),
        cotangent.reshape(ROWS, D),
        *(a.reshape(-1, 128) for a in vectors),
        qkv_weight,
        up_weight,
        out_weight,
        down_weight,
    )
    down_grad, out_grad, up_grad, qkv_grad, block_out, input_grad, *small = cast(*sums)
    up_bias_grad = small.pop()
    return (
        block_out,
        input_grad,
        small[0],
        small[1],
        qkv_grad,
        small[4],
        small[5],
        out_grad,
        small[6],
        small[2],
        small[3],
        up_grad,
        up_bias_grad,
        down_grad,
        small[7],
    )


def solution(mesh):
    row, cube, flat = P("shard"), P("replica", "shard", None), P("shard", None)
    return jax.shard_map(
        body,
        mesh=mesh,
        in_specs=(cube, cube, row, row, flat, row, row, flat, row, row, row, flat, row, flat, row),
        out_specs=(cube, cube, row, row, flat, row, row, flat, row, row, row, flat, row, flat, row),
        check_vma=False,
    )
```

```python
import jax
import jax.numpy as jnp
from jax import lax
from jax.experimental import pallas as pl
from jax.experimental.pallas import tpu as pltpu
from jax.sharding import PartitionSpec as P

HEAD_DIM = 64
EPS = 1e-06
F32 = jnp.float32
BF16 = jnp.bfloat16
SCALE = HEAD_DIM ** (-0.5)
MESH = pl.DeviceIdType.MESH
D = 1024
ROWS = 144
HALF = 512
GELU = 0.7978845608028654


def dot(a, b):
    return lax.dot_general(a, b, (((1,), (0,)), ((), ())), preferred_element_type=F32)


def dot_last(a, b):
    return lax.dot_general(a, b, (((1,), (1,)), ((), ())), preferred_element_type=F32)


def dot_first(a, b):
    return lax.dot_general(a, b, (((0,), (0,)), ((), ())), preferred_element_type=F32)


def norm_unit(v):
    mean = jnp.mean(v, -1, keepdims=True)
    centred = v - mean
    inverse = lax.rsqrt(jnp.mean(centred * centred, -1, keepdims=True) + EPS)
    return centred * inverse, inverse


def norm_back(grad, unit, inverse, gain):
    gn = grad * gain
    inner = jnp.mean(gn * unit, -1, keepdims=True)
    return inverse * (gn - jnp.mean(gn, -1, keepdims=True) - unit * inner)


def head_masks(shape):
    low = lax.broadcasted_iota(jnp.int32, shape, 1) < HEAD_DIM
    return (low, jnp.logical_not(low))


def add(*terms):
    total = terms[0].astype(F32)
    for term in terms[1:]:
        total = total + term.astype(F32)
    return total


class Net:
    def __init__(self, send, recv):
        self.send, self.recv, self.count, self.open = send, recv, 0, []
        self.s = lax.axis_index("shard")
        self.h, self.x = self.s // 4, lax.rem(self.s, 4)
        r = lax.axis_index("replica")
        self.core, self.y = lax.rem(r, 2), lax.rem(r // 2, 4)
        zlow = r // 8
        base = r - self.y * 2
        self.right = {"shard": self.at(self.h, self.x + 1)}
        self.left = {"shard": self.at(self.h, self.x + 3)}
        self.across = {"shard": self.at(1 - self.h, self.x)}
        self.twin = {"replica": r + 1 - 2 * self.core}
        self.up = {"replica": base + lax.rem(self.y + 1, 4) * 2}
        self.down = {"replica": base + lax.rem(self.y + 3, 4) * 2}
        self.facing = {"replica": base + lax.rem(self.y + 2, 4) * 2}
        self.beside = {"replica": r + 8 - 16 * zlow}
        self.replicas = [{"replica": lax.rem(r + k, 16)} for k in range(1, 16)]
        self.r = r
        self.peers = [{"shard": lax.rem(self.s + k, 8)} for k in range(1, 8)]

    def at(self, h, x):
        return h * 4 + lax.rem(x, 4)

    def copy(self, src, dst, to):
        i = self.count
        self.count += 1
        made = pltpu.make_async_remote_copy(
            src_ref=src,
            dst_ref=dst,
            send_sem=self.send.at[i],
            recv_sem=self.recv.at[i],
            device_id=to,
            device_id_type=MESH,
        )
        made.start()
        self.open.append(made)
        return made

    def drain(self):
        for made in self.open:
            made.wait_send()
        self.open = []

    def settle(self, copies):
        for made in copies:
            made.wait_send()
            self.open = [other for other in self.open if other is not made]

    def barrier(self, others):
        semaphore = pltpu.get_barrier_semaphore()
        for other in others:
            pl.semaphore_signal(semaphore, inc=1, device_id=other, device_id_type=MESH)
        pl.semaphore_wait(semaphore, len(others))


class Gather:
    def __init__(self, net, whole):
        self.net, self.whole = net, whole
        self.a = self.piece(net.s, 0, net.right)
        self.b = self.piece(net.s, 1, net.left)
        own = whole.at[net.s]
        self.z = net.copy(own, own, net.across)
        self.more = [self.piece(net.s, 1, net.right), self.piece(net.s, 0, net.left)]

    def piece(self, block, second, to):
        part = self.whole.at[block, :, pl.ds(second * HALF, HALF)]
        return self.net.copy(part, part, to)

    def relay_one(self):
        net = self.net
        self.a.wait_recv()
        self.c = self.piece(net.at(net.h, net.x + 3), 0, net.right)
        self.b.wait_recv()
        self.d = self.piece(net.at(net.h, net.x + 1), 1, net.left)

    def relay_two(self):
        net = self.net
        self.z.wait_recv()
        part = self.whole.at[net.at(1 - net.h, net.x)]
        self.rest = [net.copy(part, part, net.right), net.copy(part, part, net.left)]
        block = net.at(net.h, net.x + 2)
        self.c.wait_recv()
        self.rest.append(self.piece(block, 0, net.across))
        self.d.wait_recv()
        self.rest.append(self.piece(block, 1, net.across))

    def row(self):
        for made in self.more:
            made.wait_recv()

    def finish(self):
        for made in self.rest:
            made.wait_recv()


class Scatter:
    def __init__(self, net, part, hop, side, near, far, passed, kept, came):
        self.net, self.part, self.hop_in, self.side_in = net, part, hop, side
        self.near_in, self.far_in, self.passed, self.kept, self.came = near, far, passed, kept, came
        self.one, self.two = pl.ds(0, HALF), pl.ds(HALF, HALF)
        h, x = net.h, net.x
        self.own, self.facing = net.s, net.at(h, x + 2)
        self.right, self.left = net.at(h, x + 1), net.at(h, x + 3)
        self.other = [net.at(1 - h, x + k) for k in range(4)]

    def hop(self):
        self.hopped = self.net.copy(self.part.at[self.other[2]], self.hop_in, self.net.across)

    def side(self):
        net, part = self.net, self.part
        self.sides = [
            net.copy(part.at[self.other[1]], self.side_in.at[0], net.right),
            net.copy(part.at[self.other[3]], self.side_in.at[1], net.left),
        ]

    def near(self):
        net, part = self.net, self.part
        self.nears = [
            net.copy(part.at[self.right, :, self.two], self.near_in.at[0], net.right),
            net.copy(part.at[self.left, :, self.one], self.near_in.at[1], net.left),
        ]

    def far(self):
        net, hop = self.net, self.hop_in
        self.hopped.wait_recv()
        hop[...] = add(hop[...], self.part[self.facing]).astype(BF16)
        self.fars = [
            net.copy(hop.at[:, self.one], self.far_in.at[0], net.right),
            net.copy(hop.at[:, self.two], self.far_in.at[1], net.left),
        ]

    def over(self):
        for made in self.sides:
            made.wait_recv()
        self.kept[...] = add(
            self.part[self.other[0]], self.side_in[0], self.side_in[1]
        ).astype(BF16)
        self.crossed = self.net.copy(self.kept, self.came, self.net.across)

    def relay(self):
        net, part, far = self.net, self.part, self.far_in
        self.fars[0].wait_recv()
        far[0] = add(far[0], part[self.right, :, self.one]).astype(BF16)
        passes = [net.copy(far.at[0], self.passed.at[0], net.right)]
        self.fars[1].wait_recv()
        far[1] = add(far[1], part[self.left, :, self.two]).astype(BF16)
        passes.append(net.copy(far.at[1], self.passed.at[1], net.left))
        self.last = [*self.nears, *passes, self.crossed]

    def finish(self):
        for made in self.last:
            made.wait_recv()
        part, near, passed, came = self.part, self.near_in, self.passed, self.came
        one, two = self.one, self.two
        return jnp.concatenate(
            [
                add(part[self.own, :, one], passed[0], near[1], came[:, one]),
                add(part[self.own, :, two], passed[1], near[0], came[:, two]),
            ],
            axis=1,
        )


class Reduce:
    def __init__(self, net, grad, pair, ring, out, turned=None):
        self.net, self.grad, self.out, self.turned = net, grad, out, turned
        self.sent, self.work = pair
        *self.three, self.kept, self.came = ring
        self.mine = pl.ds(net.core * 4, 4)
        self.q = net.core * 4 + net.y
        self.at_up, self.at_facing, self.at_down = (lax.rem(net.y + k, 4) for k in (1, 2, 3))

    def core(self):
        net = self.net
        self.moved = net.copy(self.grad.at[pl.ds((1 - net.core) * 4, 4)], self.sent, net.twin)

    def ring(self):
        net, work = self.net, self.work
        self.moved.wait_recv()
        work[...] = add(self.grad[self.mine], self.sent[...]).astype(BF16)
        steps = ((self.at_up, net.up), (self.at_down, net.down), (self.at_facing, net.facing))
        self.nears = [
            net.copy(work.at[block], there, to) for there, (block, to) in zip(self.three, steps)
        ]

    def beside(self):
        net = self.net
        for made in self.nears:
            made.wait_recv()
        three = [part[...] for part in self.three]
        self.kept[...] = add(self.work[net.y], *three).astype(BF16)
        self.over = net.copy(self.kept, self.came, net.beside)

    def place(self, q, eighths=1):
        rows = self.out.shape[0] // 8
        return pl.ds(pl.multiple_of(q * rows, 16), rows * eighths)

    def cross(self):
        net = self.net
        self.over.wait_recv()
        total = add(self.kept[...], self.came[...]).astype(BF16)
        if self.turned is None:
            self.out[self.place(self.q)] = total
            return
        away, back = self.turned
        away[...] = total.reshape(away.shape)
        self.crossed = [
            net.copy(away.at[to["shard"]], back.at[net.s], to) for to in net.peers
        ]
        back[net.s] = away[net.s]

    def back(self):
        net, out = self.net, self.out
        own = self.place(self.q)
        if self.turned is not None:
            for made in self.crossed:
                made.wait_recv()
            incoming = self.turned[1]
            blocks = [incoming[t] for t in range(8)]
            width = blocks[0].shape[-1]
            for i in range(width // 128 if width == 384 else 1):
                size = 128 if width == 384 else width
                for t in range(8):
                    at = i * D + t * size
                    out[own, at : at + size] = blocks[t][:, i * 128 : i * 128 + size]
        part = out.at[own]
        self.shared = [net.copy(part, part, to) for to in (net.up, net.down, net.facing)]

    def swap(self):
        for made in self.shared:
            made.wait_recv()
        part = self.out.at[self.place(self.net.core * 4, 4)]
        self.ended = self.net.copy(part, part, self.net.twin)

    def end(self):
        self.ended.wait_recv()


def layer_kernel(*refs):
    layer_steps(*refs[:2], refs[2:8], *refs[8:])


def layer_steps(
    tokens,
    cotangent,
    singles,
    query_bias,
    value_bias,
    up_bias,
    qkv_weight,
    up_weight,
    out_source,
    down_source,
    block_out,
    input_grad,
    down_sum,
    out_sum,
    up_sum,
    qkv_sum,
    small_sum,
    down_grad,
    out_grad,
    up_grad,
    qkv_grad,
    wide_vectors,
    vectors,
    all_vectors,
    columns,
    first,
    cot,
    second,
    branch,
    mixed,
    qkv_low,
    heads,
    lse,
    attended,
    active,
    grad_upper,
    grad_qkv,
    resid_ref,
    grad_resid_ref,
    unit_ref,
    small,
    fours,
    fours_in,
    parts,
    hop,
    side,
    near,
    far,
    passed,
    kept,
    came,
    small_low,
    small_ring,
    down_pair,
    down_ring,
    out_pair,
    out_ring,
    up_pair,
    up_ring,
    up_turned,
    qkv_pair,
    qkv_ring,
    qkv_turned,
    out_weight,
    down_weight,
    load,
    send,
    recv,
):
    net = Net(send, recv)
    s, core = net.s, net.core
    net.barrier([*net.peers, *net.replicas])

    def reduce(grad, pair, ring, out, turned=None):
        split = lambda ref, n: [ref.at[i] for i in range(n)]
        turned = None if turned is None else split(turned, 2)
        return Reduce(net, grad, split(pair, 2), split(ring, 5), out, turned)

    down_all = reduce(down_grad, down_pair, down_ring, down_sum)
    out_all = reduce(out_grad, out_pair, out_ring, out_sum)
    up_all = reduce(up_grad, up_pair, up_ring, up_sum, up_turned)
    qkv_all = reduce(qkv_grad, qkv_pair, qkv_ring, qkv_sum, qkv_turned)
    mine = pl.ds(pl.multiple_of(core * 64, 64), 64)
    sixteen = pl.ds(pl.multiple_of(core * 64 + net.y * 16, 16), 16)

    def scatter(i):
        buffers = (hop, side, near, far, passed, kept, came)
        return Scatter(net, parts.at[i % 3], *(buffer.at[i] for buffer in buffers))

    def each(work, least, end, carry=0):
        def step(i, carry):
            row, j = i // 4, lax.rem(i, 4)
            same = j + j // 2 - 2 * (j // 3)
            cross = lax.rem(2 * j, 3) + 3 * (j // 3)
            h = net.h + row - 2 * net.h * row
            return work(net.at(h, net.x + (1 - row) * same + row * cross), carry)

        return lax.fori_loop(least, end, step, carry)

    def each_sent(rs, work, carry, beside=None):
        carry = each(work, 5, 6, carry)
        rs.hop()
        carry = each(work, 6, 8, carry)
        rs.side()
        carry = each(work, 1, 3, carry)
        rs.near()
        carry = each(work, 3, 5, carry)
        if beside is None:
            rs.far()
            return each(work, 0, 1, carry)
        carry = each(work, 0, 1, carry)
        beside()
        rs.far()
        return carry

    wide_vectors[...] = jnp.zeros_like(wide_vectors)
    for k, single in enumerate(singles):
        wide_vectors[k : k + 1, :] = single[...].astype(F32)
    vectors[...] = wide_vectors[...].astype(BF16)
    vec = [net.copy(vectors, all_vectors.at[s], to) for to in net.peers]
    all_vectors[s] = vectors[...]
    cot[s] = cotangent[...]
    qkv_in, up_in = [], []
    thirds = [
        lambda t, i=i: qkv_weight.at[sixteen, pl.ds(pl.multiple_of(i * D + t * 128, 128), 128)]
        for i in range(3)
    ]
    quarter = lambda t: up_weight.at[sixteen, pl.ds(pl.multiple_of(t * 512, 512), 512)]
    for to in net.peers:
        for i in range(3):
            there = columns.at[s, sixteen, pl.ds(i * 128, 128)]
            qkv_in.append(net.copy(thirds[i](to["shard"]), there, to))
    for to in net.peers:
        there = columns.at[s, sixteen, pl.ds(384, 512)]
        up_in.append(net.copy(quarter(to["shard"]), there, to))
    loads = [
        (thirds[i](s), columns.at[s, sixteen, pl.ds(i * 128, 128)]) for i in range(3)
    ]
    loads += [
        (quarter(s), columns.at[s, sixteen, pl.ds(384, 512)]),
        (out_source, out_weight),
        (down_source, down_weight),
    ]
    loads = [pltpu.make_async_copy(*pair, load.at[i]) for i, pair in enumerate(loads)]
    for made in loads:
        made.start()

    def share(arrived, at):
        for made in arrived:
            made.wait_recv()
        part = columns.at[:, sixteen, at]
        return [net.copy(part, part, to) for to in (net.up, net.down, net.facing)]

    def share_twin(arrived, at):
        for made in arrived:
            made.wait_recv()
        part = columns.at[:, mine, at]
        return net.copy(part, part, net.twin)

    x = tokens[...].astype(F32)
    unit1, inverse1 = norm_unit(x)
    for made in vec:
        made.wait_recv()
    table = [all_vectors[j].astype(F32) for j in range(8)]
    gain1, shift1, gain2, shift2, bias_out, bias_down = (
        jnp.concatenate([t[i : i + 1] for t in table], axis=1) for i in range(6)
    )
    first[s] = (unit1 * gain1 + shift1).astype(BF16)
    ag = Gather(net, first)
    qkv_at, up_at = pl.ds(0, 384), pl.ds(384, 512)
    for made in loads[:4]:
        made.wait()
    qkv_in = share(qkv_in, qkv_at)
    ag.relay_one()
    up_in = share(up_in, up_at)
    ag.relay_two()
    qkv_pass = share_twin(qkv_in, qkv_at)
    qkv_bias = jnp.concatenate(
        [query_bias[...].astype(F32), jnp.zeros((1, 128), F32), value_bias[...].astype(F32)], axis=1
    )
    up_bias = up_bias[...].astype(F32)
    up_bias = jnp.concatenate([up_bias[k : k + 1] for k in range(4)], axis=1)
    qkv_pass.wait_recv()
    ag.row()

    def project(b, carry):
        value = dot(first[b], columns[:, :, 0:384].reshape(D, 384)) + qkv_bias
        at = pl.multiple_of(b * 72, 8)
        mixed[0, pl.ds(at, 72), :] = value[0:72]
        mixed[1, pl.ds(at, 72), :] = value[72:144]
        return carry

    each(project, 0, 5)
    ag.finish()
    ag_cot = Gather(net, cot)
    each(project, 5, 8)
    qkv_low[...] = mixed[...].astype(BF16)
    ag_cot.relay_one()

    def attend(image, carry):
        q, k, v = (qkv_low[image, :, i * 128 : (i + 1) * 128] for i in range(3))
        zero = jnp.zeros_like(q)
        total = jnp.zeros(q.shape, F32)
        for h, mask in enumerate(head_masks(q.shape)):
            score = dot_last(jnp.where(mask, q, zero), k) * SCALE
            top = jnp.max(score, -1, keepdims=True)
            e = jnp.exp(score - top)
            row = jnp.sum(e, -1, keepdims=True)
            p = (e * (1.0 / row)).astype(BF16)
            total += dot(p, jnp.where(mask, v, zero))
            lse[image, :, h : h + 1] = top + jnp.log(row)
        heads[image] = total
        return carry

    lax.fori_loop(0, 2, attend, 0)
    up_pass = share_twin(up_in, up_at)

    def by_device(ref, b):
        at = pl.multiple_of(b * 72, 8)
        both = [ref[i, pl.ds(at, 72), :] for i in range(2)]
        return jnp.concatenate(both, axis=0).astype(BF16)

    def outward(b, carry):
        value = by_device(heads, b)
        attended[b] = value
        parts[0, b] = dot(value, out_weight[...]).astype(BF16)
        return carry

    for made in loads[4:]:
        made.wait()
    rs = rs_branch = scatter(0)
    each_sent(rs, outward, 0)
    rs.over()
    rs.relay()
    ag_cot.relay_two()
    resid = tokens[...].astype(F32) + (rs.finish() + bias_out)
    resid_ref[...] = resid
    unit2, inverse2 = norm_unit(resid)
    second[s] = (unit2 * gain2 + shift2).astype(BF16)
    ag = Gather(net, second)
    up_pass.wait_recv()

    def feed(b, total):
        up = columns[:, :, 384:896].reshape(D, 512)
        u = dot(second[b], up) + up_bias
        square = u * u
        t = jnp.tanh(GELU * (u + 0.044715 * u * square))
        act = (0.5 * u * (1.0 + t)).astype(BF16)
        slope = 0.5 * (1.0 + t) + (0.5 * GELU) * u * (1.0 - t * t) * (
            1.0 + 0.134145 * square
        )
        active[b] = act
        gu = (dot_last(cot[b], down_weight[...]) * slope).astype(BF16)
        grad_upper[b] = gu
        parts[1, b] = dot_last(gu, up).astype(BF16)
        parts[2, b] = dot(act, down_weight[...]).astype(BF16)
        return total + jnp.sum(gu.astype(F32), 0, keepdims=True)

    ag.relay_one()
    ag_cot.row()
    ag_cot.finish()
    up_bias_grad = each(feed, 0, 1, jnp.zeros((1, 512), F32))
    ag.relay_two()
    ag.row()
    up_bias_grad = each(feed, 1, 5, up_bias_grad)
    ag.finish()
    rs = scatter(1)
    up_bias_grad = each(feed, 5, 6, up_bias_grad)
    rs.hop()
    up_bias_grad = each(feed, 6, 8, up_bias_grad)
    rs.side()
    rs.near()
    own = pl.ds(pl.multiple_of(s * 128, 128), 128)
    small[...] = jnp.zeros_like(small)
    for i in range(4):
        small[8 + i : 9 + i, :] = up_bias_grad[:, i * 128 : (i + 1) * 128]
    small[7:8, :] = jnp.sum(cot[:, :, own].astype(F32).reshape(1152, 128), 0, keepdims=True)

    def down_tile(i):
        at = pl.ds(i * 256, 256)
        value = dot_first(
            active[...].reshape(1152, 512), cot[:, :, at].reshape(1152, 256)
        ).astype(BF16)
        for q in range(8):
            down_grad[q, :, at] = value[q * 64 : (q + 1) * 64]

    down_tile(0)
    rs.far()
    down_tile(1)
    rs.over()
    rs.relay()
    down_tile(2)
    down_tile(3)
    down_all.core()
    unit2, inverse2 = norm_unit(resid_ref[...])
    unit_ref[...] = unit2
    grad_second = rs.finish()
    unit2 = unit_ref[...]
    grad_resid = cotangent[...].astype(F32) + norm_back(grad_second, unit2, inverse2, gain2)
    grad_resid_ref[...] = grad_resid
    branch[s] = grad_resid.astype(BF16)
    ag = Gather(net, branch)
    gain2_grad = jnp.sum(grad_second * unit2, 0, keepdims=True)
    shift2_grad = jnp.sum(grad_second, 0, keepdims=True)

    def up_tile(i):
        value = dot_first(
            second[:, :, i * 256 : (i + 1) * 256].reshape(1152, 256),
            grad_upper[...].reshape(1152, 512),
        ).astype(BF16)
        for j in range(2):
            for q in range(8):
                up_grad[q, (2 * i + j) * 16 : (2 * i + j + 1) * 16, :] = value[
                    j * 128 + q * 16 : j * 128 + (q + 1) * 16
                ]

    def back_heads(b, carry):
        value = dot_last(branch[b], out_weight[...])
        at = pl.multiple_of(b * 72, 8)
        heads[0, pl.ds(at, 72), :] = value[0:72]
        heads[1, pl.ds(at, 72), :] = value[72:144]
        return carry

    ag.relay_one()
    down_all.ring()
    up_tile(0)
    ag.relay_two()
    up_tile(1)
    ag.row()
    up_tile(2)
    up_tile(3)
    up_all.core()
    each(back_heads, 0, 5)
    ag.finish()
    rs_out = scatter(2)
    rs_out.hop()
    rs_out.side()
    rs_out.near()
    down_all.beside()
    each(back_heads, 5, 8)
    def attend_back(image, carry):
        q, k, v = (qkv_low[image, :, i * 128 : (i + 1) * 128] for i in range(3))
        grad = heads[image].astype(BF16)
        zero = jnp.zeros_like(q)
        dq = jnp.zeros(q.shape, F32)
        dk, dv = dq, dq
        for h, mask in enumerate(head_masks(q.shape)):
            qh, kh, gh = (jnp.where(mask, a, zero) for a in (q, k, grad))
            p = jnp.exp(dot_last(qh, k) * SCALE - lse[image, :, h : h + 1])
            dp = dot_last(gh, v)
            inner = jnp.sum(p * dp, -1, keepdims=True)
            ds = (p * (dp - inner)).astype(BF16)
            dq += dot(ds, kh)
            dk += dot_first(ds, qh)
            dv += dot_first(p.astype(BF16), gh)
        mixed[image, :, 0:128] = dq * SCALE
        mixed[image, :, 128:256] = dk * SCALE
        mixed[image, :, 256:384] = dv
        return carry

    lax.fori_loop(0, 1, attend_back, 0)
    up_all.ring()
    lax.fori_loop(1, 2, attend_back, 0)
    rs_out.far()

    def back_first(b, total):
        value = by_device(mixed, b)
        grad_qkv[b] = value
        parts[0, b] = dot_last(value, columns[:, :, 0:384].reshape(D, 384)).astype(BF16)
        return total + jnp.sum(value.astype(F32), 0, keepdims=True)

    def qkv_tile(i):
        value = dot_first(
            first[:, :, i * 256 : (i + 1) * 256].reshape(1152, 256),
            grad_qkv[...].reshape(1152, 384),
        ).astype(BF16)
        for j in range(2):
            for q in range(8):
                qkv_grad[q, (2 * i + j) * 16 : (2 * i + j + 1) * 16, :] = value[
                    j * 128 + q * 16 : j * 128 + (q + 1) * 16
                ]

    def two_tiles():
        qkv_tile(0)
        down_all.cross()
        down_all.back()
        qkv_tile(1)

    net.settle([rs_branch.hopped, *rs_branch.sides, *rs_branch.nears])
    rs = scatter(3)
    qkv_bias_grad = each_sent(rs, back_first, jnp.zeros((1, 384), F32), two_tiles)
    small[4:5, :] = qkv_bias_grad[:, 0:128]
    small[5:6, :] = qkv_bias_grad[:, 256:384]
    small[6:7, :] = jnp.sum(branch[:, :, own].astype(F32).reshape(1152, 128), 0, keepdims=True)

    qkv_tile(2)
    qkv_tile(3)
    qkv_all.core()
    rs_out.over()
    up_all.beside()
    rs.over()
    qkv_all.ring()
    value = dot_first(attended[...].reshape(1152, 128), branch[...].reshape(1152, D)).astype(BF16)
    for q in range(8):
        out_grad[q] = value[q * 16 : (q + 1) * 16]
    out_all.core()
    rs_out.relay()
    rs.relay()
    up_all.cross()
    down_all.swap()
    qkv_all.beside()
    out_all.ring()
    up_all.back()
    unit1, inverse1 = norm_unit(tokens[...].astype(F32))
    unit_ref[...] = unit1
    grad_first = rs.finish()
    unit1 = unit_ref[...]
    gain1_grad = jnp.sum(grad_first * unit1, 0, keepdims=True)
    shift1_grad = jnp.sum(grad_first, 0, keepdims=True)
    four = jnp.concatenate(
        [gain1_grad, shift1_grad, gain2_grad, shift2_grad, jnp.zeros((12, D), F32)], axis=0
    ).astype(BF16)
    for t in range(8):
        fours[t] = four[:, t * 128 : (t + 1) * 128]
    moved = [net.copy(fours.at[to["shard"]], fours_in.at[s], to) for to in net.peers]
    fours_in[s] = fours[s]
    qkv_all.cross()
    out_all.beside()
    input_grad[...] = (
        grad_resid_ref[...] + norm_back(grad_first, unit1, inverse1, gain1)
    ).astype(BF16)
    for made in moved:
        made.wait_recv()
    total = jnp.sum(fours_in[...].astype(F32), 0)
    small[0:4, :] = total[0:4]
    small_low[...] = small[...].astype(BF16)
    moved = [net.copy(small_low, small_ring.at[net.r], to) for to in net.replicas]
    small_ring[net.r] = small_low[...]
    qkv_all.back()
    out_all.cross()
    out_all.back()
    up_all.swap()
    block_out[...] = (resid_ref[...] + (rs_out.finish() + bias_down)).astype(BF16)
    for made in moved:
        made.wait_recv()
    small_sum[...] = add(*(small_ring[k] for k in range(16)))
    qkv_all.swap()
    out_all.swap()
    for every in (down_all, out_all, up_all, qkv_all):
        every.end()
    net.drain()


def layer(*arguments):
    vmem = lambda *shape: pltpu.VMEM(shape, BF16)
    wide = lambda *shape: pltpu.VMEM(shape, F32)
    space = pl.BlockSpec(memory_space=pltpu.VMEM)
    shape = lambda *sizes: jax.ShapeDtypeStruct(sizes, BF16)
    return pl.pallas_call(
        layer_kernel,
        out_shape=[
            shape(ROWS, D),
            shape(ROWS, D),
            shape(512, D),
            shape(128, D),
            shape(128, 4096),
            shape(128, 3 * D),
            jax.ShapeDtypeStruct((16, 128), F32),
        ],
        in_specs=[space] * 11 + [pl.BlockSpec(memory_space=pl.ANY)] * 4,
        out_specs=[space] * 7,
        scratch_shapes=[
            vmem(8, 64, D),
            vmem(8, 16, D),
            vmem(8, 128, 512),
            vmem(8, 128, 384),
            wide(16, 128),
            vmem(16, 128),
            vmem(8, 16, 128),
            vmem(8, 128, 896),
            vmem(8, ROWS, D),
            vmem(8, ROWS, D),
            vmem(8, ROWS, D),
            vmem(8, ROWS, D),
            wide(2, 576, 384),
            vmem(2, 576, 384),
            wide(2, 576, 128),
            wide(2, 576, 128),
            vmem(8, ROWS, 128),
            vmem(8, ROWS, 512),
            vmem(8, ROWS, 512),
            vmem(8, ROWS, 384),
            wide(ROWS, D),
            wide(ROWS, D),
            wide(ROWS, D),
            wide(16, 128),
            vmem(8, 16, 128),
            vmem(8, 16, 128),
            vmem(3, 8, ROWS, D),
            vmem(4, ROWS, D),
            vmem(4, 2, ROWS, D),
            vmem(4, 2, ROWS, HALF),
            vmem(4, 2, ROWS, HALF),
            vmem(4, 2, ROWS, HALF),
            vmem(4, ROWS, D),
            vmem(4, ROWS, D),
            vmem(16, 128),
            vmem(16, 16, 128),
            vmem(2, 4, 64, D),
            vmem(5, 64, D),
            vmem(2, 4, 16, D),
            vmem(5, 16, D),
            vmem(2, 4, 128, 512),
            vmem(5, 128, 512),
            vmem(2, 8, 16, 512),
            vmem(2, 4, 128, 384),
            vmem(5, 128, 384),
            vmem(2, 8, 16, 384),
            vmem(128, D),
            vmem(512, D),
            pltpu.SemaphoreType.DMA((6,)),
            pltpu.SemaphoreType.DMA((240,)),
            pltpu.SemaphoreType.DMA((240,)),
        ],
        name="layer",
        cost_estimate=pl.CostEstimate(
            flops=11 * 10**9, bytes_accessed=12 * 10**6, transcendentals=0
        ),
        compiler_params=pltpu.CompilerParams(
            collective_id=1, has_side_effects=True, vmem_limit_bytes=62 << 20
        ),
    )(*arguments)


def cast_kernel(block, grad, down, out, up, qkv, small, *outs):
    for source, target in zip((block, grad), outs[:2]):
        target[...] = source[...].astype(F32).reshape(2, 72, D).astype(BF16)
    for source, target in zip((down, out, up, qkv), outs[2:6]):
        target[...] = source[...].astype(F32)
    for k, target in enumerate(outs[6:14]):
        target[...] = small[k]
    for k in range(4):
        outs[14][k * 128 : (k + 1) * 128] = small[8 + k]


def cast(*arrays):
    space = pl.BlockSpec(memory_space=pltpu.VMEM)
    shape = lambda *sizes: jax.ShapeDtypeStruct(sizes, F32)
    return pl.pallas_call(
        cast_kernel,
        out_shape=[
            *(jax.ShapeDtypeStruct((2, 72, D), BF16) for _ in range(2)),
            *(shape(*a.shape) for a in arrays[2:6]),
            *(shape(128) for _ in range(8)),
            shape(512),
        ],
        in_specs=[space] * 7,
        out_specs=[space] * 15,
        name="cast",
        compiler_params=pltpu.CompilerParams(vmem_limit_bytes=62 << 20),
    )(*arrays)


def body(
    tokens,
    cotangent,
    attn_gain,
    attn_shift,
    qkv_weight,
    query_bias,
    value_bias,
    out_weight,
    out_bias,
    mlp_gain,
    mlp_shift,
    up_weight,
    up_bias,
    down_weight,
    down_bias,
):
    vectors = (attn_gain, attn_shift, mlp_gain, mlp_shift, out_bias, down_bias)
    vectors = (*vectors, query_bias, value_bias, up_bias)
    sums = layer(
        tokens.reshape(ROWS, D),
        cotangent.reshape(ROWS, D),
        *(a.reshape(-1, 128) for a in vectors),
        qkv_weight,
        up_weight,
        out_weight,
        down_weight,
    )
    block_out, input_grad, down_grad, out_grad, up_grad, qkv_grad, *small = cast(*sums)
    up_bias_grad = small.pop()
    return (
        block_out,
        input_grad,
        small[0],
        small[1],
        qkv_grad,
        small[4],
        small[5],
        out_grad,
        small[6],
        small[2],
        small[3],
        up_grad,
        up_bias_grad,
        down_grad,
        small[7],
    )


def solution(mesh):
    row, cube, flat = P("shard"), P("replica", "shard", None), P("shard", None)
    return jax.shard_map(
        body,
        mesh=mesh,
        in_specs=(cube, cube, row, row, flat, row, row, flat, row, row, row, flat, row, flat, row),
        out_specs=(cube, cube, row, row, flat, row, row, flat, row, row, row, flat, row, flat, row),
        check_vma=False,
    )
```

```python
import jax
import jax.numpy as jnp
from jax import lax
from jax.experimental import pallas as pl
from jax.experimental.pallas import tpu as pltpu
from jax.sharding import PartitionSpec as P

HEAD_DIM = 64
EPS = 1e-06
F32 = jnp.float32
BF16 = jnp.bfloat16
SCALE = HEAD_DIM ** (-0.5)
MESH = pl.DeviceIdType.MESH
D = 1024
ROWS = 144
HALF = 512
GELU = 0.7978845608028654


def dot(a, b):
    return lax.dot_general(a, b, (((1,), (0,)), ((), ())), preferred_element_type=F32)


def dot_last(a, b):
    return lax.dot_general(a, b, (((1,), (1,)), ((), ())), preferred_element_type=F32)


def dot_first(a, b):
    return lax.dot_general(a, b, (((0,), (0,)), ((), ())), preferred_element_type=F32)


def norm_unit(v):
    mean = jnp.mean(v, -1, keepdims=True)
    centred = v - mean
    inverse = lax.rsqrt(jnp.mean(centred * centred, -1, keepdims=True) + EPS)
    return centred * inverse, inverse


def norm_back(grad, unit, inverse, gain):
    gn = grad * gain
    inner = jnp.mean(gn * unit, -1, keepdims=True)
    return inverse * (gn - jnp.mean(gn, -1, keepdims=True) - unit * inner)


def head_masks(shape):
    low = lax.broadcasted_iota(jnp.int32, shape, 1) < HEAD_DIM
    return (low, jnp.logical_not(low))


def add(*terms):
    total = terms[0].astype(F32)
    for term in terms[1:]:
        total = total + term.astype(F32)
    return total


class Net:
    def __init__(self, send, recv):
        self.send, self.recv, self.count, self.open = send, recv, 0, []
        self.s = lax.axis_index("shard")
        self.h, self.x = self.s // 4, lax.rem(self.s, 4)
        r = lax.axis_index("replica")
        self.core, self.y = lax.rem(r, 2), lax.rem(r // 2, 4)
        zlow = r // 8
        base = r - self.y * 2
        self.right = {"shard": self.at(self.h, self.x + 1)}
        self.left = {"shard": self.at(self.h, self.x + 3)}
        self.across = {"shard": self.at(1 - self.h, self.x)}
        self.twin = {"replica": r + 1 - 2 * self.core}
        self.up = {"replica": base + lax.rem(self.y + 1, 4) * 2}
        self.down = {"replica": base + lax.rem(self.y + 3, 4) * 2}
        self.facing = {"replica": base + lax.rem(self.y + 2, 4) * 2}
        self.beside = {"replica": r + 8 - 16 * zlow}
        self.replicas = [{"replica": lax.rem(r + k, 16)} for k in range(1, 16)]
        self.r = r
        self.peers = [{"shard": lax.rem(self.s + k, 8)} for k in range(1, 8)]

    def at(self, h, x):
        return h * 4 + lax.rem(x, 4)

    def copy(self, src, dst, to):
        i = self.count
        self.count += 1
        made = pltpu.make_async_remote_copy(
            src_ref=src,
            dst_ref=dst,
            send_sem=self.send.at[i],
            recv_sem=self.recv.at[i],
            device_id=to,
            device_id_type=MESH,
        )
        made.start()
        self.open.append(made)
        return made

    def drain(self):
        for made in self.open:
            made.wait_send()
        self.open = []

    def settle(self, copies):
        for made in copies:
            made.wait_send()
            self.open = [other for other in self.open if other is not made]

    def barrier(self, others):
        semaphore = pltpu.get_barrier_semaphore()
        for other in others:
            pl.semaphore_signal(semaphore, inc=1, device_id=other, device_id_type=MESH)
        pl.semaphore_wait(semaphore, len(others))


class Gather:
    def __init__(self, net, whole):
        self.net, self.whole = net, whole
        self.a = self.piece(net.s, 0, net.right)
        self.b = self.piece(net.s, 1, net.left)
        own = whole.at[net.s]
        self.z = net.copy(own, own, net.across)
        self.more = [self.piece(net.s, 1, net.right), self.piece(net.s, 0, net.left)]

    def piece(self, block, second, to):
        part = self.whole.at[block, :, pl.ds(second * HALF, HALF)]
        return self.net.copy(part, part, to)

    def relay_one(self):
        net = self.net
        self.a.wait_recv()
        self.c = self.piece(net.at(net.h, net.x + 3), 0, net.right)
        self.b.wait_recv()
        self.d = self.piece(net.at(net.h, net.x + 1), 1, net.left)

    def relay_two(self):
        net = self.net
        self.z.wait_recv()
        part = self.whole.at[net.at(1 - net.h, net.x), :, pl.ds(128, D - 128)]
        self.rest = [net.copy(part, part, net.right), net.copy(part, part, net.left)]
        for made, k in zip(self.more, (3, 1)):
            made.wait_recv()
            part = self.whole.at[net.at(net.h, net.x + k), :, pl.ds(0, 128)]
            self.rest.append(net.copy(part, part, net.across))
        block = net.at(net.h, net.x + 2)
        self.c.wait_recv()
        self.rest.append(self.piece(block, 0, net.across))
        self.d.wait_recv()
        self.rest.append(self.piece(block, 1, net.across))

    def finish(self):
        for made in self.rest:
            made.wait_recv()


class Scatter:
    def __init__(self, net, part, hop, side, near, far, passed, kept, came):
        self.net, self.part, self.hop_in, self.side_in = net, part, hop, side
        self.near_in, self.far_in, self.passed, self.kept, self.came = near, far, passed, kept, came
        self.one, self.two = pl.ds(0, HALF), pl.ds(HALF, HALF)
        h, x = net.h, net.x
        self.own, self.facing = net.s, net.at(h, x + 2)
        self.right, self.left = net.at(h, x + 1), net.at(h, x + 3)
        self.other = [net.at(1 - h, x + k) for k in range(4)]

    def hop(self):
        self.hopped = self.net.copy(self.part.at[self.other[2]], self.hop_in, self.net.across)

    def side(self):
        net, part = self.net, self.part
        self.sides = [
            net.copy(part.at[self.other[1]], self.side_in.at[0], net.right),
            net.copy(part.at[self.other[3]], self.side_in.at[1], net.left),
        ]

    def near(self):
        net, part = self.net, self.part
        self.nears = [
            net.copy(part.at[self.right, :, self.two], self.near_in.at[0], net.right),
            net.copy(part.at[self.left, :, self.one], self.near_in.at[1], net.left),
        ]

    def far(self):
        net, hop = self.net, self.hop_in
        self.hopped.wait_recv()
        hop[...] = add(hop[...], self.part[self.facing]).astype(BF16)
        self.fars = [
            net.copy(hop.at[:, self.one], self.far_in.at[0], net.right),
            net.copy(hop.at[:, self.two], self.far_in.at[1], net.left),
        ]

    def over(self):
        for made in self.sides:
            made.wait_recv()
        self.kept[...] = add(
            self.part[self.other[0]], self.side_in[0], self.side_in[1]
        ).astype(BF16)
        self.crossed = self.net.copy(self.kept, self.came, self.net.across)

    def relay(self):
        net, part, far = self.net, self.part, self.far_in
        self.fars[0].wait_recv()
        far[0] = add(far[0], part[self.right, :, self.one]).astype(BF16)
        passes = [net.copy(far.at[0], self.passed.at[0], net.right)]
        self.fars[1].wait_recv()
        far[1] = add(far[1], part[self.left, :, self.two]).astype(BF16)
        passes.append(net.copy(far.at[1], self.passed.at[1], net.left))
        self.last = [*self.nears, *passes, self.crossed]

    def finish(self):
        for made in self.last:
            made.wait_recv()
        part, near, passed, came = self.part, self.near_in, self.passed, self.came
        one, two = self.one, self.two
        return jnp.concatenate(
            [
                add(part[self.own, :, one], passed[0], near[1], came[:, one]),
                add(part[self.own, :, two], passed[1], near[0], came[:, two]),
            ],
            axis=1,
        )


class Reduce:
    def __init__(self, net, grad, pair, ring, out, turned=None):
        self.net, self.grad, self.out, self.turned = net, grad, out, turned
        self.sent, self.work = pair
        *self.three, self.kept, self.came = ring
        self.mine = pl.ds(net.core * 4, 4)
        self.q = net.core * 4 + net.y
        self.at_up, self.at_facing, self.at_down = (lax.rem(net.y + k, 4) for k in (1, 2, 3))

    def core(self):
        net = self.net
        self.moved = net.copy(self.grad.at[pl.ds((1 - net.core) * 4, 4)], self.sent, net.twin)

    def ring(self):
        net, work = self.net, self.work
        self.moved.wait_recv()
        work[...] = add(self.grad[self.mine], self.sent[...]).astype(BF16)
        steps = ((self.at_up, net.up), (self.at_down, net.down), (self.at_facing, net.facing))
        self.nears = [
            net.copy(work.at[block], there, to) for there, (block, to) in zip(self.three, steps)
        ]

    def beside(self):
        net = self.net
        for made in self.nears:
            made.wait_recv()
        three = [part[...] for part in self.three]
        self.kept[...] = add(self.work[net.y], *three).astype(BF16)
        self.over = net.copy(self.kept, self.came, net.beside)

    def place(self, q, eighths=1):
        rows = self.out.shape[0] // 8
        return pl.ds(pl.multiple_of(q * rows, 16), rows * eighths)

    def cross(self):
        net = self.net
        self.over.wait_recv()
        total = add(self.kept[...], self.came[...]).astype(BF16)
        if self.turned is None:
            self.out[self.place(self.q)] = total
            return
        away, back = self.turned
        away[...] = total.reshape(away.shape)
        self.crossed = [
            net.copy(away.at[to["shard"]], back.at[net.s], to) for to in net.peers
        ]
        back[net.s] = away[net.s]

    def back(self):
        net, out = self.net, self.out
        own = self.place(self.q)
        if self.turned is not None:
            for made in self.crossed:
                made.wait_recv()
            incoming = self.turned[1]
            blocks = [incoming[t] for t in range(8)]
            width = blocks[0].shape[-1]
            for i in range(width // 128 if width == 384 else 1):
                size = 128 if width == 384 else width
                for t in range(8):
                    at = i * D + t * size
                    out[own, at : at + size] = blocks[t][:, i * 128 : i * 128 + size]
        part = out.at[own]
        self.shared = [net.copy(part, part, to) for to in (net.up, net.down, net.facing)]

    def swap(self):
        for made in self.shared:
            made.wait_recv()
        part = self.out.at[self.place(self.net.core * 4, 4)]
        self.ended = self.net.copy(part, part, self.net.twin)

    def end(self):
        self.ended.wait_recv()


def layer_kernel(*refs):
    layer_steps(*refs[:2], refs[2:8], *refs[8:])


def layer_steps(
    tokens,
    cotangent,
    singles,
    query_bias,
    value_bias,
    up_bias,
    qkv_weight,
    up_weight,
    out_source,
    down_source,
    block_out,
    input_grad,
    down_sum,
    out_sum,
    up_sum,
    qkv_sum,
    small_sum,
    down_grad,
    out_grad,
    up_grad,
    qkv_grad,
    wide_vectors,
    vectors,
    all_vectors,
    columns,
    first,
    cot,
    second,
    branch,
    mixed,
    qkv_low,
    heads,
    lse,
    attended,
    active,
    grad_upper,
    grad_qkv,
    resid_ref,
    grad_resid_ref,
    unit_ref,
    small,
    fours,
    fours_in,
    parts,
    hop,
    side,
    near,
    far,
    passed,
    kept,
    came,
    small_low,
    small_ring,
    down_pair,
    down_ring,
    out_pair,
    out_ring,
    up_pair,
    up_ring,
    up_turned,
    qkv_pair,
    qkv_ring,
    qkv_turned,
    out_weight,
    down_weight,
    load,
    send,
    recv,
):
    net = Net(send, recv)
    s, core = net.s, net.core
    net.barrier([*net.peers, *net.replicas])

    def reduce(grad, pair, ring, out, turned=None):
        split = lambda ref, n: [ref.at[i] for i in range(n)]
        turned = None if turned is None else split(turned, 2)
        return Reduce(net, grad, split(pair, 2), split(ring, 5), out, turned)

    down_all = reduce(down_grad, down_pair, down_ring, down_sum)
    out_all = reduce(out_grad, out_pair, out_ring, out_sum)
    up_all = reduce(up_grad, up_pair, up_ring, up_sum, up_turned)
    qkv_all = reduce(qkv_grad, qkv_pair, qkv_ring, qkv_sum, qkv_turned)
    mine = pl.ds(pl.multiple_of(core * 64, 64), 64)
    sixteen = pl.ds(pl.multiple_of(core * 64 + net.y * 16, 16), 16)

    def scatter(i):
        buffers = (hop, side, near, far, passed, kept, came)
        return Scatter(net, parts.at[i % 3], *(buffer.at[i] for buffer in buffers))

    def each(work, least, end, carry=0):
        def step(i, carry):
            row, j = i // 4, lax.rem(i, 4)
            same = j + j // 2 - 2 * (j // 3)
            cross = lax.rem(2 * j, 3) + 3 * (j // 3)
            h = net.h + row - 2 * net.h * row
            return work(net.at(h, net.x + (1 - row) * same + row * cross), carry)

        return lax.fori_loop(least, end, step, carry)

    def each_sent(rs, work, carry, beside=None):
        carry = each(work, 5, 6, carry)
        rs.hop()
        carry = each(work, 6, 8, carry)
        rs.side()
        carry = each(work, 1, 3, carry)
        rs.near()
        carry = each(work, 3, 5, carry)
        if beside is None:
            rs.far()
            return each(work, 0, 1, carry)
        carry = each(work, 0, 1, carry)
        beside()
        rs.far()
        return carry

    wide_vectors[...] = jnp.zeros_like(wide_vectors)
    for k, single in enumerate(singles):
        wide_vectors[k : k + 1, :] = single[...].astype(F32)
    vectors[...] = wide_vectors[...].astype(BF16)
    vec = [net.copy(vectors, all_vectors.at[s], to) for to in net.peers]
    all_vectors[s] = vectors[...]
    cot[s] = cotangent[...]
    qkv_in, up_in = [], []
    thirds = [
        lambda t, i=i: qkv_weight.at[sixteen, pl.ds(pl.multiple_of(i * D + t * 128, 128), 128)]
        for i in range(3)
    ]
    quarter = lambda t: up_weight.at[sixteen, pl.ds(pl.multiple_of(t * 512, 512), 512)]
    for to in net.peers:
        for i in range(3):
            there = columns.at[s, sixteen, pl.ds(i * 128, 128)]
            qkv_in.append(net.copy(thirds[i](to["shard"]), there, to))
    for to in net.peers:
        there = columns.at[s, sixteen, pl.ds(384, 512)]
        up_in.append(net.copy(quarter(to["shard"]), there, to))
    loads = [
        (thirds[i](s), columns.at[s, sixteen, pl.ds(i * 128, 128)]) for i in range(3)
    ]
    loads += [
        (quarter(s), columns.at[s, sixteen, pl.ds(384, 512)]),
        (out_source, out_weight),
        (down_source, down_weight),
    ]
    loads = [pltpu.make_async_copy(*pair, load.at[i]) for i, pair in enumerate(loads)]
    for made in loads:
        made.start()

    def share(arrived, at):
        for made in arrived:
            made.wait_recv()
        part = columns.at[:, sixteen, at]
        return [net.copy(part, part, to) for to in (net.up, net.down, net.facing)]

    def share_twin(arrived, at):
        for made in arrived:
            made.wait_recv()
        part = columns.at[:, mine, at]
        return net.copy(part, part, net.twin)

    x = tokens[...].astype(F32)
    unit1, inverse1 = norm_unit(x)
    for made in vec:
        made.wait_recv()
    table = [all_vectors[j].astype(F32) for j in range(8)]
    gain1, shift1, gain2, shift2, bias_out, bias_down = (
        jnp.concatenate([t[i : i + 1] for t in table], axis=1) for i in range(6)
    )
    first[s] = (unit1 * gain1 + shift1).astype(BF16)
    ag = Gather(net, first)
    qkv_at, up_at = pl.ds(0, 384), pl.ds(384, 512)
    for made in loads[:4]:
        made.wait()
    qkv_in = share(qkv_in, qkv_at)
    ag.relay_one()
    up_in = share(up_in, up_at)
    ag.relay_two()
    qkv_pass = share_twin(qkv_in, qkv_at)
    qkv_bias = jnp.concatenate(
        [query_bias[...].astype(F32), jnp.zeros((1, 128), F32), value_bias[...].astype(F32)], axis=1
    )
    up_bias = up_bias[...].astype(F32)
    up_bias = jnp.concatenate([up_bias[k : k + 1] for k in range(4)], axis=1)
    qkv_pass.wait_recv()

    def project(b, carry):
        value = dot(first[b], columns[:, :, 0:384].reshape(D, 384)) + qkv_bias
        at = pl.multiple_of(b * 72, 8)
        mixed[0, pl.ds(at, 72), :] = value[0:72]
        mixed[1, pl.ds(at, 72), :] = value[72:144]
        return carry

    each(project, 0, 5)
    ag.finish()
    ag_cot = Gather(net, cot)
    each(project, 5, 8)
    qkv_low[...] = mixed[...].astype(BF16)
    ag_cot.relay_one()

    def attend(image, carry):
        q, k, v = (qkv_low[image, :, i * 128 : (i + 1) * 128] for i in range(3))
        zero = jnp.zeros_like(q)
        total = jnp.zeros(q.shape, F32)
        for h, mask in enumerate(head_masks(q.shape)):
            score = dot_last(jnp.where(mask, q, zero), k) * SCALE
            top = jnp.max(score, -1, keepdims=True)
            e = jnp.exp(score - top)
            row = jnp.sum(e, -1, keepdims=True)
            p = (e * (1.0 / row)).astype(BF16)
            total += dot(p, jnp.where(mask, v, zero))
            lse[image, :, h : h + 1] = top + jnp.log(row)
        heads[image] = total
        return carry

    lax.fori_loop(0, 2, attend, 0)
    up_pass = share_twin(up_in, up_at)

    def by_device(ref, b):
        at = pl.multiple_of(b * 72, 8)
        both = [ref[i, pl.ds(at, 72), :] for i in range(2)]
        return jnp.concatenate(both, axis=0).astype(BF16)

    def outward(b, carry):
        value = by_device(heads, b)
        attended[b] = value
        parts[0, b] = dot(value, out_weight[...]).astype(BF16)
        return carry

    for made in loads[4:]:
        made.wait()
    rs = rs_branch = scatter(0)
    each_sent(rs, outward, 0)
    rs.over()
    rs.relay()
    ag_cot.relay_two()
    resid = tokens[...].astype(F32) + (rs.finish() + bias_out)
    resid_ref[...] = resid
    unit2, inverse2 = norm_unit(resid)
    second[s] = (unit2 * gain2 + shift2).astype(BF16)
    ag = Gather(net, second)
    up_pass.wait_recv()

    def feed(b, total):
        up = columns[:, :, 384:896].reshape(D, 512)
        u = dot(second[b], up) + up_bias
        square = u * u
        t = jnp.tanh(GELU * (u + 0.044715 * u * square))
        act = (0.5 * u * (1.0 + t)).astype(BF16)
        slope = 0.5 * (1.0 + t) + (0.5 * GELU) * u * (1.0 - t * t) * (
            1.0 + 0.134145 * square
        )
        active[b] = act
        gu = (dot_last(cot[b], down_weight[...]) * slope).astype(BF16)
        grad_upper[b] = gu
        parts[1, b] = dot_last(gu, up).astype(BF16)
        parts[2, b] = dot(act, down_weight[...]).astype(BF16)
        return total + jnp.sum(gu.astype(F32), 0, keepdims=True)

    ag.relay_one()
    ag_cot.finish()
    up_bias_grad = each(feed, 0, 1, jnp.zeros((1, 512), F32))
    ag.relay_two()
    up_bias_grad = each(feed, 1, 5, up_bias_grad)
    ag.finish()
    rs = scatter(1)
    up_bias_grad = each(feed, 5, 6, up_bias_grad)
    rs.hop()
    up_bias_grad = each(feed, 6, 8, up_bias_grad)
    rs.side()
    rs.near()
    own = pl.ds(pl.multiple_of(s * 128, 128), 128)
    small[...] = jnp.zeros_like(small)
    for i in range(4):
        small[8 + i : 9 + i, :] = up_bias_grad[:, i * 128 : (i + 1) * 128]
    small[7:8, :] = jnp.sum(cot[:, :, own].astype(F32).reshape(1152, 128), 0, keepdims=True)

    def down_tile(i):
        at = pl.ds(i * 256, 256)
        value = dot_first(
            active[...].reshape(1152, 512), cot[:, :, at].reshape(1152, 256)
        ).astype(BF16)
        for q in range(8):
            down_grad[q, :, at] = value[q * 64 : (q + 1) * 64]

    down_tile(0)
    rs.far()
    down_tile(1)
    rs.over()
    rs.relay()
    down_tile(2)
    down_tile(3)
    down_all.core()
    unit2, inverse2 = norm_unit(resid_ref[...])
    unit_ref[...] = unit2
    grad_second = rs.finish()
    unit2 = unit_ref[...]
    grad_resid = cotangent[...].astype(F32) + norm_back(grad_second, unit2, inverse2, gain2)
    grad_resid_ref[...] = grad_resid
    branch[s] = grad_resid.astype(BF16)
    ag = Gather(net, branch)
    gain2_grad = jnp.sum(grad_second * unit2, 0, keepdims=True)
    shift2_grad = jnp.sum(grad_second, 0, keepdims=True)

    def up_tile(i):
        value = dot_first(
            second[:, :, i * 256 : (i + 1) * 256].reshape(1152, 256),
            grad_upper[...].reshape(1152, 512),
        ).astype(BF16)
        for j in range(2):
            for q in range(8):
                up_grad[q, (2 * i + j) * 16 : (2 * i + j + 1) * 16, :] = value[
                    j * 128 + q * 16 : j * 128 + (q + 1) * 16
                ]

    def back_heads(b, carry):
        value = dot_last(branch[b], out_weight[...])
        at = pl.multiple_of(b * 72, 8)
        heads[0, pl.ds(at, 72), :] = value[0:72]
        heads[1, pl.ds(at, 72), :] = value[72:144]
        return carry

    ag.relay_one()
    down_all.ring()
    up_tile(0)
    ag.relay_two()
    up_tile(1)
    up_tile(2)
    up_tile(3)
    up_all.core()
    each(back_heads, 0, 5)
    ag.finish()
    rs_out = scatter(2)
    rs_out.hop()
    rs_out.side()
    rs_out.near()
    down_all.beside()
    each(back_heads, 5, 8)
    def attend_back(image, carry):
        q, k, v = (qkv_low[image, :, i * 128 : (i + 1) * 128] for i in range(3))
        grad = heads[image].astype(BF16)
        zero = jnp.zeros_like(q)
        dq = jnp.zeros(q.shape, F32)
        dk, dv = dq, dq
        for h, mask in enumerate(head_masks(q.shape)):
            qh, kh, gh = (jnp.where(mask, a, zero) for a in (q, k, grad))
            p = jnp.exp(dot_last(qh, k) * SCALE - lse[image, :, h : h + 1])
            dp = dot_last(gh, v)
            inner = jnp.sum(p * dp, -1, keepdims=True)
            ds = (p * (dp - inner)).astype(BF16)
            dq += dot(ds, kh)
            dk += dot_first(ds, qh)
            dv += dot_first(p.astype(BF16), gh)
        mixed[image, :, 0:128] = dq * SCALE
        mixed[image, :, 128:256] = dk * SCALE
        mixed[image, :, 256:384] = dv
        return carry

    lax.fori_loop(0, 1, attend_back, 0)
    up_all.ring()
    lax.fori_loop(1, 2, attend_back, 0)
    rs_out.far()

    def back_first(b, total):
        value = by_device(mixed, b)
        grad_qkv[b] = value
        parts[0, b] = dot_last(value, columns[:, :, 0:384].reshape(D, 384)).astype(BF16)
        return total + jnp.sum(value.astype(F32), 0, keepdims=True)

    def qkv_tile(i):
        value = dot_first(
            first[:, :, i * 256 : (i + 1) * 256].reshape(1152, 256),
            grad_qkv[...].reshape(1152, 384),
        ).astype(BF16)
        for j in range(2):
            for q in range(8):
                qkv_grad[q, (2 * i + j) * 16 : (2 * i + j + 1) * 16, :] = value[
                    j * 128 + q * 16 : j * 128 + (q + 1) * 16
                ]

    def two_tiles():
        qkv_tile(0)
        down_all.cross()
        down_all.back()
        qkv_tile(1)

    net.settle([rs_branch.hopped, *rs_branch.sides, *rs_branch.nears])
    rs = scatter(3)
    qkv_bias_grad = each_sent(rs, back_first, jnp.zeros((1, 384), F32), two_tiles)
    small[4:5, :] = qkv_bias_grad[:, 0:128]
    small[5:6, :] = qkv_bias_grad[:, 256:384]
    small[6:7, :] = jnp.sum(branch[:, :, own].astype(F32).reshape(1152, 128), 0, keepdims=True)

    qkv_tile(2)
    qkv_tile(3)
    qkv_all.core()
    rs_out.over()
    up_all.beside()
    rs.over()
    qkv_all.ring()
    value = dot_first(attended[...].reshape(1152, 128), branch[...].reshape(1152, D)).astype(BF16)
    for q in range(8):
        out_grad[q] = value[q * 16 : (q + 1) * 16]
    out_all.core()
    rs_out.relay()
    rs.relay()
    up_all.cross()
    down_all.swap()
    qkv_all.beside()
    out_all.ring()
    up_all.back()
    unit1, inverse1 = norm_unit(tokens[...].astype(F32))
    unit_ref[...] = unit1
    grad_first = rs.finish()
    unit1 = unit_ref[...]
    gain1_grad = jnp.sum(grad_first * unit1, 0, keepdims=True)
    shift1_grad = jnp.sum(grad_first, 0, keepdims=True)
    four = jnp.concatenate(
        [gain1_grad, shift1_grad, gain2_grad, shift2_grad, jnp.zeros((12, D), F32)], axis=0
    ).astype(BF16)
    for t in range(8):
        fours[t] = four[:, t * 128 : (t + 1) * 128]
    moved = [net.copy(fours.at[to["shard"]], fours_in.at[s], to) for to in net.peers]
    fours_in[s] = fours[s]
    qkv_all.cross()
    out_all.beside()
    input_grad[...] = (
        grad_resid_ref[...] + norm_back(grad_first, unit1, inverse1, gain1)
    ).astype(BF16)
    for made in moved:
        made.wait_recv()
    total = jnp.sum(fours_in[...].astype(F32), 0)
    small[0:4, :] = total[0:4]
    small_low[...] = small[...].astype(BF16)
    moved = [net.copy(small_low, small_ring.at[net.r], to) for to in net.replicas]
    small_ring[net.r] = small_low[...]
    qkv_all.back()
    out_all.cross()
    out_all.back()
    up_all.swap()
    block_out[...] = (resid_ref[...] + (rs_out.finish() + bias_down)).astype(BF16)
    for made in moved:
        made.wait_recv()
    small_sum[...] = add(*(small_ring[k] for k in range(16)))
    qkv_all.swap()
    out_all.swap()
    for every in (down_all, out_all, up_all, qkv_all):
        every.end()
    net.drain()


def layer(*arguments):
    vmem = lambda *shape: pltpu.VMEM(shape, BF16)
    wide = lambda *shape: pltpu.VMEM(shape, F32)
    space = pl.BlockSpec(memory_space=pltpu.VMEM)
    shape = lambda *sizes: jax.ShapeDtypeStruct(sizes, BF16)
    return pl.pallas_call(
        layer_kernel,
        out_shape=[
            shape(ROWS, D),
            shape(ROWS, D),
            shape(512, D),
            shape(128, D),
            shape(128, 4096),
            shape(128, 3 * D),
            jax.ShapeDtypeStruct((16, 128), F32),
        ],
        in_specs=[space] * 11 + [pl.BlockSpec(memory_space=pl.ANY)] * 4,
        out_specs=[space] * 7,
        scratch_shapes=[
            vmem(8, 64, D),
            vmem(8, 16, D),
            vmem(8, 128, 512),
            vmem(8, 128, 384),
            wide(16, 128),
            vmem(16, 128),
            vmem(8, 16, 128),
            vmem(8, 128, 896),
            vmem(8, ROWS, D),
            vmem(8, ROWS, D),
            vmem(8, ROWS, D),
            vmem(8, ROWS, D),
            wide(2, 576, 384),
            vmem(2, 576, 384),
            wide(2, 576, 128),
            wide(2, 576, 128),
            vmem(8, ROWS, 128),
            vmem(8, ROWS, 512),
            vmem(8, ROWS, 512),
            vmem(8, ROWS, 384),
            wide(ROWS, D),
            wide(ROWS, D),
            wide(ROWS, D),
            wide(16, 128),
            vmem(8, 16, 128),
            vmem(8, 16, 128),
            vmem(3, 8, ROWS, D),
            vmem(4, ROWS, D),
            vmem(4, 2, ROWS, D),
            vmem(4, 2, ROWS, HALF),
            vmem(4, 2, ROWS, HALF),
            vmem(4, 2, ROWS, HALF),
            vmem(4, ROWS, D),
            vmem(4, ROWS, D),
            vmem(16, 128),
            vmem(16, 16, 128),
            vmem(2, 4, 64, D),
            vmem(5, 64, D),
            vmem(2, 4, 16, D),
            vmem(5, 16, D),
            vmem(2, 4, 128, 512),
            vmem(5, 128, 512),
            vmem(2, 8, 16, 512),
            vmem(2, 4, 128, 384),
            vmem(5, 128, 384),
            vmem(2, 8, 16, 384),
            vmem(128, D),
            vmem(512, D),
            pltpu.SemaphoreType.DMA((6,)),
            pltpu.SemaphoreType.DMA((240,)),
            pltpu.SemaphoreType.DMA((240,)),
        ],
        name="layer",
        cost_estimate=pl.CostEstimate(
            flops=11 * 10**9, bytes_accessed=12 * 10**6, transcendentals=0
        ),
        compiler_params=pltpu.CompilerParams(
            collective_id=1, has_side_effects=True, vmem_limit_bytes=62 << 20
        ),
    )(*arguments)


def cast_kernel(block, grad, down, out, up, qkv, small, *outs):
    for source, target in zip((block, grad), outs[:2]):
        target[...] = source[...].astype(F32).reshape(2, 72, D).astype(BF16)
    for source, target in zip((down, out, up, qkv), outs[2:6]):
        target[...] = source[...].astype(F32)
    for k, target in enumerate(outs[6:14]):
        target[...] = small[k]
    for k in range(4):
        outs[14][k * 128 : (k + 1) * 128] = small[8 + k]


def cast(*arrays):
    space = pl.BlockSpec(memory_space=pltpu.VMEM)
    shape = lambda *sizes: jax.ShapeDtypeStruct(sizes, F32)
    return pl.pallas_call(
        cast_kernel,
        out_shape=[
            *(jax.ShapeDtypeStruct((2, 72, D), BF16) for _ in range(2)),
            *(shape(*a.shape) for a in arrays[2:6]),
            *(shape(128) for _ in range(8)),
            shape(512),
        ],
        in_specs=[space] * 7,
        out_specs=[space] * 15,
        name="cast",
        compiler_params=pltpu.CompilerParams(vmem_limit_bytes=62 << 20),
    )(*arrays)


def body(
    tokens,
    cotangent,
    attn_gain,
    attn_shift,
    qkv_weight,
    query_bias,
    value_bias,
    out_weight,
    out_bias,
    mlp_gain,
    mlp_shift,
    up_weight,
    up_bias,
    down_weight,
    down_bias,
):
    vectors = (attn_gain, attn_shift, mlp_gain, mlp_shift, out_bias, down_bias)
    vectors = (*vectors, query_bias, value_bias, up_bias)
    sums = layer(
        tokens.reshape(ROWS, D),
        cotangent.reshape(ROWS, D),
        *(a.reshape(-1, 128) for a in vectors),
        qkv_weight,
        up_weight,
        out_weight,
        down_weight,
    )
    block_out, input_grad, down_grad, out_grad, up_grad, qkv_grad, *small = cast(*sums)
    up_bias_grad = small.pop()
    return (
        block_out,
        input_grad,
        small[0],
        small[1],
        qkv_grad,
        small[4],
        small[5],
        out_grad,
        small[6],
        small[2],
        small[3],
        up_grad,
        up_bias_grad,
        down_grad,
        small[7],
    )


def solution(mesh):
    row, cube, flat = P("shard"), P("replica", "shard", None), P("shard", None)
    return jax.shard_map(
        body,
        mesh=mesh,
        in_specs=(cube, cube, row, row, flat, row, row, flat, row, row, row, flat, row, flat, row),
        out_specs=(cube, cube, row, row, flat, row, row, flat, row, row, row, flat, row, flat, row),
        check_vma=False,
    )
```
